32 devices in a mesh: dp: 8 (over y, x, core), seq: 4 (over z).
Axes of the slice: x: 2, y: 2, z: 4, core: 2. Of those that a mesh axis runs over, the one named last changes fastest.
Arguments:
- hidden_in: bfloat16 [8, 8, 128, 768], P('dp', 'seq'), may hold values from -6 to 6
- stretch_order: int32 [8], replicated, may hold values from 0 to 7, each once
- doc_lengths: int32 [8, 4], P('dp'), may hold values from 1 to 896, 1024 in all within a row
- attn_gain: bfloat16 [768], P(('dp', 'seq')), may hold values from 0.5 to 1.5
- attn_shift: bfloat16 [768], P(('dp', 'seq')), may hold values from -1 to 1
- feed_gain: bfloat16 [768], P(('dp', 'seq')), may hold values from 0.5 to 1.5
- feed_shift: bfloat16 [768], P(('dp', 'seq')), may hold values from -1 to 1
- qkv_weight: bfloat16 [768, 2304], P(('dp', 'seq')), may hold values from -0.21875 to 0.21875
- qkv_bias: bfloat16 [2304], P(('dp', 'seq')), may hold values from -1 to 1
- out_weight: bfloat16 [768, 768], P(('dp', 'seq')), may hold values from -1.75 to 1.75
- out_bias: bfloat16 [768], P(('dp', 'seq')), may hold values from -1 to 1
- up_weight: bfloat16 [768, 3072], P(('dp', 'seq')), may hold values from -0.21875 to 0.21875
- up_bias: bfloat16 [3072], P(('dp', 'seq')), may hold values from -1 to 1
- down_weight: bfloat16 [3072, 768], P(('dp', 'seq')), may hold values from -0.109375 to 0.109375
- down_bias: bfloat16 [768], P(('dp', 'seq')), may hold values from -1 to 1
- grad_out: bfloat16 [8, 8, 128, 768], P('dp', 'seq'), may hold values from -6 to 6
Outputs:
- hidden_out: bfloat16 [8, 8, 128, 768], P('dp', 'seq')
- grad_in: bfloat16 [8, 8, 128, 768], P('dp', 'seq')
- grad_attn_gain: float32 [768], P(('dp', 'seq'))
- grad_attn_shift: float32 [768], P(('dp', 'seq'))
- grad_feed_gain: float32 [768], P(('dp', 'seq'))
- grad_feed_shift: float32 [768], P(('dp', 'seq'))
- grad_qkv_weight: float32 [768, 2304], P(('dp', 'seq'))
- grad_qkv_bias: float32 [2304], P(('dp', 'seq'))
- grad_out_weight: float32 [768, 768], P(('dp', 'seq'))
- grad_out_bias: float32 [768], P(('dp', 'seq'))
- grad_up_weight: float32 [768, 3072], P(('dp', 'seq'))
- grad_up_bias: float32 [3072], P(('dp', 'seq'))
- grad_down_weight: float32 [3072, 768], P(('dp', 'seq'))
- grad_down_bias: float32 [768], P(('dp', 'seq'))
The draws below stay inside these ranges and needn't reach their ends.
Inputs may be any that keep to these rules, and one draw needn't show every extreme that they name: `stretch_order`: each value 0 to 7 stands once. `doc_lengths`: each row sums to 1024, and its largest entry is exactly 896.
All inputs are finite; a program needn't handle non-finite values.
Results may differ from the reference program's by a relative error of at most 0.0095.
Values may be sent and summed in bfloat16 or wider, within the bound.
No kernel may reach another device: no remote copies, remote signals or barrier semaphores. Data moves between devices by JAX's collectives and lax.ppermute only.
A program may use at most 192 MiB of HBM per device.

```python
import math
import jax
import jax.numpy as jnp
import numpy as np
from jax import lax

D = 768
HEADS = 12
HD = 64
FF = 3072
ROT = 16
LENGTH = 1024
DOCS = 4
HALVES = 8
HALF = 128
SEQS = 8
TOKENS = 8192


def level_of(stream_key, dims, split, low, high):
    def one(axis_at, shards_of):
        draws = jax.random.uniform(jax.random.fold_in(jax.random.fold_in(stream_key, 6), axis_at), (shards_of,), jnp.float32, low / len(split), high / len(split))
        return jnp.repeat(jnp.exp(draws), dims[axis_at] // shards_of).reshape((-1,) + (1,) * (len(dims) - axis_at - 1))

    level = one(*split[0])
    for cut in split[1:]:
        level = level * one(*cut)
    return level


def profile(amount, total, bound, slope):
    portions = [(1 << 20) // math.isqrt(standing ** slope) + 1 for standing in range(2, amount + 1)]
    surplus, given = total - bound - (amount - 1), [1] * (amount - 1)
    while surplus > 0:
        free = [i for i in range(amount - 1) if given[i] < bound]
        mass, budget = sum([portions[i] for i in free]), surplus
        for i in free:
            extra = min(bound - given[i], max(1, budget * portions[i] // mass), surplus)
            given[i] = given[i] + extra
            surplus = surplus - extra
    return np.array([bound] + given)


def uneven_parts(rng, count, total, bound, skew):
    if count == 2:
        one = jax.random.randint(rng, (), max(1, total - bound), min(bound, total - 1) + 1)
        return jnp.stack([one, total - one])
    tallies = jnp.asarray(profile(count, total, bound, skew), jnp.int32)
    pairs = (count - 1) // 2
    donor, receiver = tallies[1:1 + 2 * pairs:2], tallies[2:2 + 2 * pairs:2]
    margin = jnp.minimum(donor - 1, bound - receiver)
    moved = jax.random.randint(jax.random.fold_in(rng, 1), (pairs,), 0, 1 << 20) % (margin + 1)
    tallies = tallies.at[1:1 + 2 * pairs:2].set(donor - moved).at[2:2 + 2 * pairs:2].set(receiver + moved)
    return tallies[jax.random.permutation(jax.random.fold_in(rng, 2), count)]


def noise(key, shape, scale, bound, shards=(), kind=jnp.bfloat16):
    entries = scale * jax.random.normal(key, shape, jnp.float32)
    if shards:
        entries = entries * level_of(key, shape, shards, -0.22, 0.18)
    return jnp.clip(entries, -bound, bound).astype(kind)


def setup_inputs(seed: int = 0) -> dict:
    key_list = jax.random.split(jax.random.key(seed), 17)
    hidden_in = noise(key_list[0], (SEQS, HALVES, HALF, D), 1.0, 6.0, ((0, 8), (1, 4)))
    stretch_order = jax.random.permutation(key_list[1], HALVES).astype(jnp.int32)
    doc_lengths = jax.vmap(lambda own: uneven_parts(own, DOCS, LENGTH, LENGTH - HALF, 1))(jax.random.split(key_list[2], SEQS)).reshape((SEQS, DOCS)).astype(jnp.int32)
    attn_gain = jnp.clip(1.0 + 0.1 * jax.random.normal(key_list[3], (D,), jnp.float32), 0.5, 1.5).astype(jnp.bfloat16)
    attn_shift = noise(key_list[4], (D,), 0.2, 1.0, ((0, 32),))
    feed_gain = jnp.clip(1.0 + 0.1 * jax.random.normal(key_list[5], (D,), jnp.float32), 0.5, 1.5).astype(jnp.bfloat16)
    feed_shift = noise(key_list[6], (D,), 0.2, 1.0, ((0, 32),))
    qkv_weight = noise(key_list[7], (D, 3 * D), D ** -0.5, 0.21875, ((0, 32),))
    qkv_bias = noise(key_list[8], (3 * D,), 0.2, 1.0, ((0, 32),))
    out_weight = noise(key_list[9], (D, D), (D // 64) ** -0.5, 1.75, ((0, 32),))
    out_bias = noise(key_list[10], (D,), 0.2, 1.0, ((0, 32),))
    up_weight = noise(key_list[11], (D, FF), D ** -0.5, 0.21875, ((0, 32),))
    up_bias = noise(key_list[12], (FF,), 0.2, 1.0, ((0, 32),))
    down_weight = noise(key_list[13], (FF, D), FF ** -0.5, 0.109375, ((0, 32),))
    down_bias = noise(key_list[14], (D,), 0.2, 1.0, ((0, 32),))
    grad_out = noise(key_list[15], (SEQS, HALVES, HALF, D), 1.0, 6.0, ((0, 8), (1, 4)))
    return {"hidden_in": hidden_in, "stretch_order": stretch_order, "doc_lengths": doc_lengths, "attn_gain": attn_gain, "attn_shift": attn_shift, "feed_gain": feed_gain, "feed_shift": feed_shift, "qkv_weight": qkv_weight, "qkv_bias": qkv_bias, "out_weight": out_weight, "out_bias": out_bias, "up_weight": up_weight, "up_bias": up_bias, "down_weight": down_weight, "down_bias": down_bias, "grad_out": grad_out}


eps = 1e-05
masked = -1e+30

@jax.custom_vjp
def low(v):
    return lax.optimization_barrier(v.astype(jnp.bfloat16)).astype(jnp.float32)

@jax.custom_vjp
def low_back(v):
    return v

def low_keep(v):
    return (low(v), None)

def low_pass(kept, grad):
    return (grad,)

def back_keep(v):
    return (v, None)

def back_low(kept, grad):
    return (low(grad),)
low.defvjp(low_keep, low_pass)
low_back.defvjp(back_keep, back_low)

def matmul(left, right):
    return jnp.dot(left, right, precision=lax.Precision.HIGHEST, preferred_element_type=jnp.float32)

def layer_norm(rows, gain, shift):
    mean = lax.optimization_barrier(jnp.mean(rows, axis=-1, keepdims=True))
    centred = rows - mean
    spread = lax.optimization_barrier(jnp.mean(centred * centred, axis=-1, keepdims=True))
    return centred * lax.rsqrt(spread + eps) * gain + shift

def frequencies():
    return jnp.power(10000.0, -2.0 * jnp.arange(ROT // 2, dtype=jnp.float32) / ROT)

def rotate(heads, cosine, sine):
    half_rot = ROT // 2
    first = heads[..., :half_rot]
    second = heads[..., half_rot:ROT]
    return jnp.concatenate([first * cosine - second * sine, second * cosine + first * sine, heads[..., ROT:]], axis=-1)

def forward(params, inputs, positions, documents):
    attn_gain, attn_shift, feed_gain, feed_shift, qkv_weight, qkv_bias, out_weight, out_bias, up_weight, up_bias, down_weight, down_bias = params
    group = inputs.shape[0]
    rows = inputs.reshape(group * LENGTH, D)
    first = low(layer_norm(rows, attn_gain, attn_shift))
    second = low(layer_norm(rows, feed_gain, feed_shift))
    mixed = low_back(matmul(first, qkv_weight)) + qkv_bias
    mixed = mixed.reshape(group, LENGTH, 3, HEADS, HD)
    angle = positions.astype(jnp.float32)[:, None] * frequencies()[None, :]
    cosine = jnp.cos(angle)[None, :, None, :]
    sine = jnp.sin(angle)[None, :, None, :]
    query = low(rotate(mixed[:, :, 0], cosine, sine))
    key = low(rotate(mixed[:, :, 1], cosine, sine))
    value = low(mixed[:, :, 2])
    scores = low_back(jnp.einsum('gqhd,gkhd->ghqk', query, key, precision=lax.Precision.HIGHEST))
    scores = scores * (1.0 / math.sqrt(HD))
    allowed = (positions[None, :] <= positions[:, None])[None] & (documents[:, :, None] == documents[:, None, :])
    scores = jnp.where(allowed[:, None], scores, masked)
    top = lax.optimization_barrier(jnp.max(scores, axis=-1, keepdims=True))
    weights = jnp.exp(scores - top)
    weights = weights / lax.optimization_barrier(jnp.sum(weights, axis=-1, keepdims=True))
    heads_out = jnp.einsum('ghqk,gkhd->gqhd', low(weights), value, precision=lax.Precision.HIGHEST)
    heads_out = low(low_back(heads_out.reshape(group * LENGTH, D)))
    attended = matmul(heads_out, out_weight) + out_bias
    inner = low_back(matmul(second, up_weight)) + up_bias
    active = low(jax.nn.gelu(inner, approximate=False))
    fed = matmul(active, down_weight) + down_bias
    return (rows + attended + fed).reshape(group, LENGTH, D)

def reference(hidden_in, stretch_order, doc_lengths, attn_gain, attn_shift, feed_gain, feed_shift, qkv_weight, qkv_bias, out_weight, out_bias, up_weight, up_bias, down_weight, down_bias, grad_out):
    params = tuple((p.astype(jnp.float32) for p in (attn_gain, attn_shift, feed_gain, feed_shift, qkv_weight, qkv_bias, out_weight, out_bias, up_weight, up_bias, down_weight, down_bias)))
    offsets = jnp.arange(HALF, dtype=jnp.int32)
    positions = (stretch_order.astype(jnp.int32)[:, None] * HALF + offsets[None, :]).reshape(LENGTH).astype(jnp.int32)
    ends = jnp.cumsum(doc_lengths.astype(jnp.int32), axis=1)[:, :-1]
    documents = lax.optimization_barrier(jnp.sum((positions[None, :, None] >= ends[:, None, :]).astype(jnp.int32), axis=-1)).astype(jnp.int32)
    group = math.gcd(SEQS, max(1, 4096 // LENGTH))
    count = SEQS // group
    inputs = hidden_in.astype(jnp.float32).reshape(count, group, LENGTH, D)
    cotangents = grad_out.astype(jnp.float32).reshape(count, group, LENGTH, D)
    doc_blocks = documents.reshape(count, group, LENGTH)

    def step(totals, item):
        block, cotangent, docs_block = item
        result, pull = jax.vjp(lambda p, v: forward(p, v, positions, docs_block), params, block)
        grads, grad_rows = pull(cotangent)
        totals = tuple((a + b for a, b in zip(totals, grads)))
        return (totals, (result.astype(jnp.bfloat16), grad_rows.astype(jnp.bfloat16)))
    zeros = tuple((jnp.zeros(p.shape, jnp.float32) for p in params))
    totals, (results, grad_rows) = lax.scan(step, zeros, (inputs, cotangents, doc_blocks))
    factor = 1.0 / math.sqrt(TOKENS)
    return (results.reshape(SEQS, HALVES, HALF, D), grad_rows.reshape(SEQS, HALVES, HALF, D), totals[0] * factor, totals[1] * factor, totals[2] * factor, totals[3] * factor, totals[4] * factor, totals[5] * factor, totals[6] * factor, totals[7] * factor, totals[8] * factor, totals[9] * factor, totals[10] * factor, totals[11] * factor)
```

```python
import math

import jax
import jax.numpy as jnp
from jax import lax
from jax.experimental import pallas as pl
from jax.experimental.pallas import tpu as pltpu
from jax.sharding import PartitionSpec as P

HD = 64
ROT = 16


eps = 1e-05
masked = -1e30


def layer_norm(rows, gain, shift):
    mean = jnp.mean(rows, axis=-1, keepdims=True)
    centred = rows - mean
    spread = jnp.mean(centred * centred, axis=-1, keepdims=True)
    return centred * lax.rsqrt(spread + eps) * gain + shift


def frequencies():
    return jnp.power(10000.0, -2.0 * jnp.arange(ROT // 2, dtype=jnp.float32) / ROT)


def rotate(heads, cosine, sine):
    half_rot = ROT // 2
    first = heads[..., :half_rot]
    second = heads[..., half_rot:ROT]
    return jnp.concatenate(
        [first * cosine - second * sine, second * cosine + first * sine, heads[..., ROT:]], axis=-1
    )


def doc_ids(positions, ends):
    return jnp.sum((positions[None, :, None] >= ends[:, None, :]).astype(jnp.int32), axis=-1)


def times_transposed(left, right):
    return lax.dot_general(
        left, right, (((1,), (1,)), ((), ())), preferred_element_type=jnp.float32
    )


def inner_rows(left, right):
    return lax.dot_general(
        left, right, (((0,), (0,)), ((), ())), preferred_element_type=jnp.float32
    )


def per_device_split(
    hidden_in,
    stretch_order,
    doc_lengths,
    attn_gain,
    attn_shift,
    feed_gain,
    feed_shift,
    qkv_weight,
    qkv_bias,
    out_weight,
    out_bias,
    up_weight,
    up_bias,
    down_weight,
    down_bias,
    grad_out,
):
    whole = (
        lax.all_gather(attn_gain, ("dp", "seq"), axis=0, tiled=True),
        lax.all_gather(attn_shift, ("dp", "seq"), axis=0, tiled=True),
        lax.all_gather(feed_gain, ("dp", "seq"), axis=0, tiled=True),
        lax.all_gather(feed_shift, ("dp", "seq"), axis=0, tiled=True),
        lax.all_gather(qkv_weight, ("dp", "seq"), axis=0, tiled=True),
        lax.all_gather(qkv_bias, ("dp", "seq"), axis=0, tiled=True),
        lax.all_gather(out_weight, ("dp", "seq"), axis=0, tiled=True),
        lax.all_gather(out_bias, ("dp", "seq"), axis=0, tiled=True),
        lax.all_gather(up_weight, ("dp", "seq"), axis=0, tiled=True),
        lax.all_gather(up_bias, ("dp", "seq"), axis=0, tiled=True),
        lax.all_gather(down_weight, ("dp", "seq"), axis=0, tiled=True),
        lax.all_gather(down_bias, ("dp", "seq"), axis=0, tiled=True),
    )
    seqs, blocks_own, half, width = hidden_in.shape
    heads = width // HD
    hidden_units = whole[8].shape[1]
    ratio = hidden_units // width
    queries = blocks_own * half
    count = seqs * queries
    scale_qk = 1.0 / math.sqrt(HD)
    lane = lax.axis_index("seq")
    offsets = jnp.arange(half, dtype=jnp.int32)
    own_blocks = lax.dynamic_slice_in_dim(stretch_order, lane * blocks_own, blocks_own)
    own_pos = (own_blocks[:, None] * half + offsets[None, :]).reshape(queries)
    ends = jnp.cumsum(doc_lengths, axis=1)[:, :-1]
    own_doc = doc_ids(own_pos, ends)
    angle = own_pos.astype(jnp.float32)[:, None] * frequencies()[None, :]
    cosine = jnp.cos(angle)[None, :, None, :]
    sine = jnp.sin(angle)[None, :, None, :]

    def allowed_of(key_pos, key_doc):
        causal = key_pos[None, None, None, :] <= own_pos[None, None, :, None]
        same = key_doc[:, None, None, :] == own_doc[:, None, :, None]
        return causal & same

    rows = hidden_in.astype(jnp.float32).reshape(count, width)
    normed_first, pull_first = jax.vjp(
        layer_norm, rows, whole[0].astype(jnp.float32), whole[1].astype(jnp.float32)
    )
    normed_second, pull_second = jax.vjp(
        layer_norm, rows, whole[2].astype(jnp.float32), whole[3].astype(jnp.float32)
    )
    first_low = normed_first.astype(jnp.bfloat16)
    second_low = normed_second.astype(jnp.bfloat16)
    mixed = jnp.dot(first_low, whole[4], preferred_element_type=jnp.float32) + whole[5].astype(
        jnp.float32
    )
    mixed = mixed.reshape(seqs, queries, 3, heads, HD)
    query = rotate(mixed[:, :, 0], cosine, sine).astype(jnp.bfloat16)
    key_own = (
        rotate(mixed[:, :, 1], cosine, sine)
        .astype(jnp.bfloat16)
        .reshape(seqs, blocks_own, half, width)
    )
    value_own = mixed[:, :, 2].astype(jnp.bfloat16).reshape(seqs, blocks_own, half, width)
    top = jnp.full((seqs, heads, queries), masked, jnp.float32)
    key_piece = lax.all_gather(key_own, "seq", axis=1, tiled=True)
    value_piece = lax.all_gather(value_own, "seq", axis=1, tiled=True)
    blocks = key_piece.shape[1]
    key_pos = (stretch_order[:, None] * half + offsets[None, :]).reshape(blocks * half)
    allowed = allowed_of(key_pos, doc_ids(key_pos, ends))
    keys = key_piece.reshape(seqs, blocks * half, heads, HD)
    values = value_piece.reshape(seqs, blocks * half, heads, HD)
    scores = (
        jnp.einsum("sqhd,skhd->shqk", query, keys, preferred_element_type=jnp.float32) * scale_qk
    )
    scores = jnp.where(allowed, scores, masked)
    new_top = jnp.maximum(top, jnp.max(scores, axis=-1))
    weights = jnp.where(allowed, jnp.exp(scores - new_top[..., None]), 0.0)
    total = jnp.sum(weights, axis=-1)
    accum = jnp.einsum(
        "shqk,skhd->shqd", weights.astype(jnp.bfloat16), values, preferred_element_type=jnp.float32
    )
    top, total, accum = (new_top, total, accum)
    logsum = top + jnp.log(total)
    heads_rows = jnp.transpose(accum / total[..., None], (0, 2, 1, 3))
    heads_low = heads_rows.reshape(count, width).astype(jnp.bfloat16)
    attended = jnp.dot(heads_low, whole[6], preferred_element_type=jnp.float32) + whole[7].astype(
        jnp.float32
    )
    inner = jnp.dot(second_low, whole[8], preferred_element_type=jnp.float32) + whole[9].astype(
        jnp.float32
    )
    active, pull_gelu = jax.vjp(lambda v: jax.nn.gelu(v, approximate=False), inner)
    active_low = active.astype(jnp.bfloat16)
    fed = jnp.dot(active_low, whole[10], preferred_element_type=jnp.float32) + whole[11].astype(
        jnp.float32
    )
    hidden_out = (rows + attended + fed).astype(jnp.bfloat16).reshape(hidden_in.shape)
    params_back = (
        lax.all_gather(attn_gain, ("dp", "seq"), axis=0, tiled=True),
        lax.all_gather(attn_shift, ("dp", "seq"), axis=0, tiled=True),
        lax.all_gather(feed_gain, ("dp", "seq"), axis=0, tiled=True),
        lax.all_gather(feed_shift, ("dp", "seq"), axis=0, tiled=True),
        lax.all_gather(qkv_weight, ("dp", "seq"), axis=0, tiled=True),
        lax.all_gather(qkv_bias, ("dp", "seq"), axis=0, tiled=True),
        lax.all_gather(out_weight, ("dp", "seq"), axis=0, tiled=True),
        lax.all_gather(out_bias, ("dp", "seq"), axis=0, tiled=True),
        lax.all_gather(up_weight, ("dp", "seq"), axis=0, tiled=True),
        lax.all_gather(up_bias, ("dp", "seq"), axis=0, tiled=True),
        lax.all_gather(down_weight, ("dp", "seq"), axis=0, tiled=True),
        lax.all_gather(down_bias, ("dp", "seq"), axis=0, tiled=True),
    )
    upstream_low = grad_out.reshape(count, width)
    upstream = upstream_low.astype(jnp.float32)
    grad_bias_out = jnp.sum(upstream, axis=0)
    grad_active = times_transposed(upstream_low, params_back[10])
    (grad_inner,) = pull_gelu(grad_active)
    inner_low = grad_inner.astype(jnp.bfloat16)
    grad_up_bias = jnp.sum(grad_inner, axis=0)
    grad_second = times_transposed(inner_low, params_back[8])
    grad_heads = times_transposed(upstream_low, params_back[6])
    heads_grad_low = grad_heads.astype(jnp.bfloat16).reshape(seqs, queries, heads, HD)
    delta = jnp.transpose(
        jnp.sum(heads_grad_low.astype(jnp.float32) * heads_rows, axis=-1), (0, 2, 1)
    )
    key_all, value_all = (
        lax.all_gather(key_own, "seq", axis=1, tiled=True),
        lax.all_gather(value_own, "seq", axis=1, tiled=True),
    )
    blocks_all = key_all.shape[1]

    def backstep(grad_query, block):
        keys = lax.dynamic_slice_in_dim(key_all, block, 1, axis=1).reshape(seqs, half, heads, HD)
        values = lax.dynamic_slice_in_dim(value_all, block, 1, axis=1).reshape(
            seqs, half, heads, HD
        )
        key_pos = lax.dynamic_slice_in_dim(stretch_order, block, 1) * half + offsets
        allowed = allowed_of(key_pos, doc_ids(key_pos, ends))
        scores = (
            jnp.einsum("sqhd,skhd->shqk", query, keys, preferred_element_type=jnp.float32)
            * scale_qk
        )
        probs = jnp.where(allowed, jnp.exp(scores - logsum[..., None]), 0.0)
        grad_probs = jnp.einsum(
            "sqhd,skhd->shqk", heads_grad_low, values, preferred_element_type=jnp.float32
        )
        grad_scores = (probs * (grad_probs - delta[..., None]) * scale_qk).astype(jnp.bfloat16)
        grad_query = grad_query + jnp.einsum(
            "shqk,skhd->sqhd", grad_scores, keys, preferred_element_type=jnp.float32
        )
        key_term = jnp.einsum(
            "shqk,sqhd->skhd", grad_scores, query, preferred_element_type=jnp.float32
        )
        value_term = jnp.einsum(
            "shqk,sqhd->skhd",
            probs.astype(jnp.bfloat16),
            heads_grad_low,
            preferred_element_type=jnp.float32,
        )
        return (
            grad_query,
            (key_term.reshape(seqs, half, width), value_term.reshape(seqs, half, width)),
        )

    grad_query, (grad_keys, grad_values) = lax.scan(
        backstep,
        jnp.zeros((seqs, queries, heads, HD), jnp.float32),
        jnp.arange(blocks_all, dtype=jnp.int32),
    )
    key_part, value_part = (
        lax.psum_scatter(
            grad_keys.astype(jnp.bfloat16), "seq", scatter_dimension=0, tiled=True
        ).astype(jnp.float32),
        lax.psum_scatter(
            grad_values.astype(jnp.bfloat16), "seq", scatter_dimension=0, tiled=True
        ).astype(jnp.float32),
    )
    key_sum = jnp.transpose(key_part, (1, 0, 2, 3))
    value_sum = jnp.transpose(value_part, (1, 0, 2, 3))
    query_back = rotate(grad_query, cosine, -sine).reshape(count, width)
    key_back = rotate(key_sum.reshape(seqs, queries, heads, HD), cosine, -sine).reshape(
        count, width
    )
    grad_mixed = jnp.concatenate([query_back, key_back, value_sum.reshape(count, width)], axis=1)
    mixed_low = grad_mixed.astype(jnp.bfloat16)
    grad_qkv_bias = jnp.sum(grad_mixed, axis=0)
    grad_first = times_transposed(mixed_low, params_back[4])
    rows_first, gain_first, shift_first = pull_first(grad_first)
    rows_second, gain_second, shift_second = pull_second(grad_second)
    grad_in = (upstream + rows_first + rows_second).astype(jnp.bfloat16).reshape(hidden_in.shape)
    factor = 1.0 / math.sqrt(count * lax.axis_size("dp") * lax.axis_size("seq"))
    small_columns = jnp.stack(
        [gain_first, shift_first, gain_second, shift_second, grad_bias_out], axis=1
    )
    qkv_bias_rows = grad_qkv_bias.reshape(width, 3)
    up_bias_rows = grad_up_bias.reshape(width, ratio)
    part_qkv = inner_rows(first_low, mixed_low)
    part_out = inner_rows(heads_low, upstream_low)
    part_up = inner_rows(second_low, inner_low)
    part_down = inner_rows(active_low, upstream_low).reshape(
        lax.axis_size(("dp", "seq")) * qkv_weight.shape[0], ratio * width
    )
    owned = lax.psum_scatter(
        jnp.concatenate(
            [part_qkv, part_out, part_up, part_down, small_columns, qkv_bias_rows, up_bias_rows],
            axis=1,
        )
        * factor,
        ("dp", "seq"),
        scatter_dimension=0,
        tiled=True,
    )
    own_rows = owned.shape[0]
    edge_out = 3 * width
    edge_up = edge_out + width
    edge_down = edge_up + hidden_units
    edge_small = edge_down + hidden_units
    edge_qkvb = edge_small + 5
    edge_upb = edge_qkvb + 3
    grad_qkv_own = owned[:, :edge_out]
    grad_out_own = owned[:, edge_out:edge_up]
    grad_up_own = owned[:, edge_up:edge_down]
    grad_down_own = owned[:, edge_down:edge_small].reshape(own_rows * ratio, width)
    grad_bias_own = owned[:, edge_small + 4]
    grad_qkvb_own = owned[:, edge_qkvb:edge_upb].reshape(own_rows * 3)
    grad_upb_own = owned[:, edge_upb : edge_upb + ratio].reshape(own_rows * ratio)
    return (
        hidden_out,
        grad_in,
        owned[:, edge_small],
        owned[:, edge_small + 1],
        owned[:, edge_small + 2],
        owned[:, edge_small + 3],
        grad_qkv_own,
        grad_qkvb_own,
        grad_out_own,
        grad_bias_own,
        grad_up_own,
        grad_upb_own,
        grad_down_own,
        grad_bias_own,
    )


f32 = jnp.float32
bf16 = jnp.bfloat16


def whole_block(shape):
    return pl.BlockSpec(shape, lambda *_: (0,) * len(shape))


def normalise(rows):
    centred = rows - jnp.mean(rows, axis=-1, keepdims=True)
    spread = jnp.mean(centred * centred, axis=-1, keepdims=True)
    return centred * lax.rsqrt(spread + eps)


def turn(upright, cosine, sine):
    half_rot = ROT // 2
    first = upright[:half_rot]
    second = upright[half_rot:ROT]
    return [first * cosine - second * sine, second * cosine + first * sine, upright[ROT:]]


def product(left, right, left_dim=1, right_dim=0):
    return lax.dot_general(
        left, right, (((left_dim,), (right_dim,)), ((), ())), preferred_element_type=f32
    )


def front_kernel(
    x_ref, vec_ref, bias_ref, cos_ref, sin_ref, up_ref, down_ref, attn_ref,
    n1_ref, n2_ref, act_ref, slope_ref, fed_ref, upright_ref, rows_ref,
):
    hat = normalise(x_ref[...].astype(f32))
    vec = vec_ref[...]
    n1 = (hat * vec[0:1] + vec[1:2]).astype(bf16)
    n2 = (hat * vec[2:3] + vec[3:4]).astype(bf16)
    n1_ref[...] = n1
    n2_ref[...] = n2
    width = upright_ref.shape[0]
    mixed = product(n1, attn_ref[:, :width]) + bias_ref[...]
    upright = mixed.T
    cosine, sine = cos_ref[...], sin_ref[...]
    part = width // 3
    pieces = []
    for start in range(0, part, HD):
        pieces += [v * HD**-0.5 for v in turn(upright[start : start + HD], cosine, sine)]
    for start in range(part, 2 * part, HD):
        pieces += turn(upright[start : start + HD], cosine, sine)
    upright = jnp.concatenate(pieces + [upright[2 * part :]], axis=0)
    upright_ref[...] = upright.astype(bf16)
    mixed = upright.T.astype(bf16)
    for j in range(width // HD):
        rows_ref[j] = mixed[:, j * HD : (j + 1) * HD]
    inner = product(n2, up_ref[...]) + vec[4:5]
    phi = 0.5 + 0.5 * lax.erf(inner * math.sqrt(0.5))
    active = (inner * phi).astype(bf16)
    act_ref[...] = active
    bell = jnp.exp(inner * inner * -0.5) * (1.0 / math.sqrt(2.0 * math.pi))
    slope_ref[...] = (phi + inner * bell).astype(bf16)
    fed_ref[...] = product(active, down_ref[...])


def attend_kernel(
    span_ref, place_ref, key_ref, query_ref, value_ref, fed_ref, out_ref,
    soft_ref, inv_ref, heads_ref, sum_ref, bias_ref,
):
    head = pl.program_id(1)

    @pl.when(head == 0)
    def _():
        place = place_ref[...]
        ok = (place <= span_ref[0:1]) & (place >= span_ref[1:2])
        bias_ref[...] = jnp.where(ok, 0.0, masked)

    scores = product(key_ref[head], query_ref[...]) + bias_ref[...]
    weights = jnp.exp(scores - jnp.max(scores, axis=0, keepdims=True))
    inverse = 1.0 / jnp.sum(weights, axis=0, keepdims=True)
    soft = weights.astype(bf16)
    soft_ref[0] = soft
    inv_ref[0] = jnp.broadcast_to(inverse, inv_ref.shape[1:])
    spot = pl.ds(pl.multiple_of(head * HD, HD), HD)
    heads_ref[spot, :] = (product(value_ref[...], soft) * inverse).astype(bf16)

    @pl.when(head == pl.num_programs(1) - 1)
    def _():
        sum_ref[...] = (fed_ref[...] + product(heads_ref[...], out_ref[...], 0, 0)).astype(bf16)


def feed_back_kernel(
    dy_ref, x_ref, act_ref, slope_ref, n2_ref, vec_ref, up_ref, down_ref,
    scaled_ref, gup_ref, gdown_ref, sums_ref, acc_up, acc_down,
):
    step = pl.program_id(0)

    @pl.when(step == 0)
    def _():
        acc_up[...] = jnp.zeros_like(acc_up)
        acc_down[...] = jnp.zeros_like(acc_down)
        sums_ref[...] = jnp.zeros_like(sums_ref)

    dy = dy_ref[...]
    grad_inner = product(dy, down_ref[...], 1, 1) * slope_ref[...].astype(f32)
    low = grad_inner.astype(bf16)
    grad = product(low, up_ref[...], 1, 1)
    hat = normalise(x_ref[...].astype(f32))
    scaled_ref[...] = grad * vec_ref[2:3]
    sums_ref[0:1] += jnp.sum(grad * hat, axis=0, keepdims=True)
    sums_ref[1:2] += jnp.sum(grad, axis=0, keepdims=True)
    sums_ref[2:3] += jnp.sum(grad_inner, axis=0, keepdims=True)
    acc_up[...] += product(n2_ref[...], low, 0, 0)
    acc_down[...] += product(act_ref[...], dy, 0, 0)

    @pl.when(step == pl.num_programs(0) - 1)
    def _():
        gup_ref[...] = acc_up[...].astype(bf16)
        gdown_ref[...] = acc_down[...].astype(bf16)


def attend_back_kernel(
    dy_ref, out_ref, heads_ref, inv_ref, soft_ref, value_ref, key_ref, query_ref, cos_ref, sin_ref,
    gquery_ref, gkey_ref, gvalue_ref, gout_ref, held_ref,
):
    step, head = pl.program_id(0), pl.program_id(1)

    @pl.when((step == 0) & (head == 0))
    def _():
        gkey_ref[...] = jnp.zeros_like(gkey_ref)
        gvalue_ref[...] = jnp.zeros_like(gvalue_ref)
        gout_ref[...] = jnp.zeros_like(gout_ref)

    @pl.when(head == 0)
    def _():
        dy = dy_ref[...]
        held_ref[...] = product(out_ref[...], dy, 1, 1).astype(bf16).astype(f32)
        gout_ref[...] += product(heads_ref[...], dy)

    spot = pl.ds(pl.multiple_of(head * HD, HD), HD)
    lifted = held_ref[spot, :] * inv_ref[0, 0:1]
    delta = jnp.sum(lifted * heads_ref[spot, :].astype(f32), axis=0, keepdims=True)
    lifted_rows = lifted.T.astype(bf16)
    soft = soft_ref[0]
    grad_soft = product(value_ref[head], lifted.astype(bf16))
    grad_scores = (soft.astype(f32) * (grad_soft - delta)).astype(bf16)
    gvalue_ref[head] += product(soft, lifted_rows)
    gkey_ref[head] += product(grad_scores, query_ref[0])
    back = product(key_ref[...], grad_scores) * HD**-0.5
    gquery_ref[spot, :] = jnp.concatenate(turn(back, cos_ref[...], -sin_ref[...]), axis=0)


def rear_kernel(
    gquery_ref, gkey_ref, gvalue_ref, cos_ref, sin_ref, n1_ref, x_ref, scaled_ref, vec_ref, attn_ref,
    total_ref, gattn_ref, sums_ref, gbias_ref, acc_ref,
):
    step = pl.program_id(0)

    @pl.when(step == 0)
    def _():
        acc_ref[...] = jnp.zeros_like(acc_ref)
        sums_ref[...] = jnp.zeros_like(sums_ref)
        gbias_ref[...] = jnp.zeros_like(gbias_ref)

    cosine, sine = cos_ref[...], sin_ref[...]
    pieces = [gquery_ref[...]]
    for j in range(gkey_ref.shape[0]):
        pieces += turn(gkey_ref[j].T, cosine, -sine)
    pieces += [gvalue_ref[j].T for j in range(gvalue_ref.shape[0])]
    mixed = jnp.concatenate(pieces, axis=0).T
    gbias_ref[0:1] += jnp.sum(mixed, axis=0, keepdims=True)
    low = mixed.astype(bf16)
    grad = product(low, attn_ref[:, : low.shape[1]], 1, 1)
    hat = normalise(x_ref[...].astype(f32))
    total_ref[...] = (grad * vec_ref[0:1] + scaled_ref[...]).astype(bf16)
    sums_ref[0:1] += jnp.sum(grad * hat, axis=0, keepdims=True)
    sums_ref[1:2] += jnp.sum(grad, axis=0, keepdims=True)
    acc_ref[...] += product(n1_ref[...], low, 0, 0)

    @pl.when(step == pl.num_programs(0) - 1)
    def _():
        gattn_ref[...] = acc_ref[...].astype(bf16)


VMEM = 56 * 1024 * 1024


def call(kernel, grid, ins, outs, scratch=()):
    arrays, in_specs = zip(*ins)
    shapes, out_specs = zip(*outs)
    return pl.pallas_call(
        kernel,
        grid=grid,
        in_specs=list(in_specs),
        out_specs=list(out_specs),
        out_shape=list(shapes),
        scratch_shapes=list(scratch),
        compiler_params=pltpu.CompilerParams(vmem_limit_bytes=VMEM),
    )(*arrays)


def shift(block, amount, ranks):
    return lax.ppermute(block, "seq", [(k, (k + amount) % ranks) for k in range(ranks)])


def swap(block, mask):
    return lax.ppermute(block, "dp", [(k, k ^ mask) for k in range(8)])


def gather_dp(piece):
    half = piece.shape[0] // 2
    place = lax.axis_index("dp")
    by_x, by_y = swap(piece, 2), swap(piece, 4)
    three = jnp.stack([piece, by_x, by_y])
    other = swap(three, 1)
    corner = jnp.concatenate([swap(by_x[:half], 4), swap(by_y[half:], 2)])
    far = swap(corner, 1)
    whole = jnp.zeros((8,) + piece.shape, piece.dtype)
    for mask, part in (
        (0, piece), (2, by_x), (4, by_y), (1, other[0]), (3, other[1]), (5, other[2]),
        (6, corner), (7, far),
    ):
        whole = lax.dynamic_update_slice(whole, part[None], (place ^ mask, 0, 0))
    return whole.reshape(8 * piece.shape[0], piece.shape[1])


def per_device_heads(
    hidden_in,
    stretch_order,
    doc_lengths,
    attn_gain,
    attn_shift,
    feed_gain,
    feed_shift,
    qkv_weight,
    qkv_bias,
    out_weight,
    out_bias,
    up_weight,
    up_bias,
    down_weight,
    down_bias,
    grad_out,
):
    ranks, groups = lax.axis_size("seq"), lax.axis_size("dp")
    rank = lax.axis_index("seq")
    blocks_own, half, width = hidden_in.shape[1:]
    own = blocks_own * half
    count = ranks * own
    share = qkv_weight.shape[0]
    piece = share * ranks
    cols = width // ranks
    heads = cols // HD
    hidden = up_weight.shape[1] // ranks
    ratio = up_weight.shape[1] // width
    mixed_cols = 3 * cols
    edge = hidden + width + mixed_cols

    small = jnp.concatenate(
        [attn_gain[:, None], attn_shift[:, None], feed_gain[:, None], feed_shift[:, None],
         out_bias[:, None], down_bias[:, None], qkv_bias.reshape(share, 3),
         up_bias.reshape(share, ratio)], axis=1,
    )
    small = jnp.pad(small, ((0, 0), (0, 128 - small.shape[1])))
    by_rank = jnp.concatenate(
        [
            up_weight.reshape(share, ranks, hidden),
            jnp.transpose(qkv_weight.reshape(share, 3, ranks, cols), (0, 2, 1, 3)).reshape(
                share, ranks, mixed_cols
            ),
            jnp.broadcast_to(small[:, None], (share, ranks, 128)),
        ],
        axis=2,
    )
    by_rank = jnp.transpose(by_rank, (1, 0, 2))
    spread = ranks * groups
    rows_piece = jnp.concatenate([down_weight, out_weight.reshape(piece, cols)], axis=1)
    rows_piece = lax.ppermute(
        rows_piece, ("dp", "seq"),
        [(k, (k % groups) * ranks + k // groups) for k in range(spread)],
    )
    landed = jnp.zeros((ranks,) + by_rank.shape[1:], bf16)
    for r in range(ranks):
        sent = lax.dynamic_index_in_dim(by_rank, (rank + r) % ranks, 0)
        got = shift(sent, r, ranks) if r else sent
        landed = lax.dynamic_update_slice(landed, got, ((rank - r) % ranks, 0, 0))
    landed = landed.reshape(piece, -1)
    weights = gather_dp(
        jnp.concatenate(
            [
                landed[:, :hidden],
                rows_piece[:, :width],
                landed[:, hidden : hidden + mixed_cols],
                rows_piece[:, width:],
                landed[:, hidden + mixed_cols :],
            ],
            axis=1,
        )
    )
    vectors = weights[:, edge + cols : edge + cols + 6 + 3 + ratio].astype(f32)
    up_bias_own = lax.dynamic_slice_in_dim(vectors[:, 9:].reshape(-1), rank * hidden, hidden)
    qkv_bias_own = lax.dynamic_index_in_dim(
        vectors[:, 6:9].reshape(3, ranks, cols), rank, 1, keepdims=False
    ).reshape(1, mixed_cols)
    vec = jnp.stack(
        [vectors[:, 0], vectors[:, 1], vectors[:, 2], vectors[:, 3], up_bias_own]
        + [jnp.zeros(width, f32)] * 3
    )
    out_own = weights[:, edge : edge + cols].reshape(cols, width)

    x_own = hidden_in.reshape(own, width)
    dy_own = grad_out.reshape(own, width)
    x_all = jnp.concatenate([x_own] + [shift(x_own, r, ranks) for r in range(1, ranks)])
    dy_all = jnp.concatenate([dy_own] + [shift(dy_own, r, ranks) for r in range(1, ranks)])

    owners = (rank - jnp.arange(ranks, dtype=jnp.int32)) % ranks
    blocks = stretch_order.reshape(ranks, blocks_own)[owners].reshape(-1)
    place = (blocks[:, None] * half + jnp.arange(half, dtype=jnp.int32)[None]).reshape(count)
    ends = jnp.cumsum(doc_lengths[0])[:-1]
    first = jnp.max(jnp.where(place[:, None] >= ends[None], ends[None], 0), axis=1)
    span = jnp.concatenate([place[None], first[None], jnp.zeros((6, count), jnp.int32)])
    angle = frequencies()[:, None] * place.astype(f32)[None]
    cosine, sine = jnp.cos(angle), jnp.sin(angle)

    tile = lambda w: pl.BlockSpec((own, w), lambda t, *_: (t, 0))
    upright_tile = lambda n: pl.BlockSpec((n, own), lambda t, *_: (0, t))
    column = lambda j: pl.BlockSpec((width, width), lambda *_: (0, j))
    shape = jax.ShapeDtypeStruct
    angles = [(cosine, upright_tile(ROT // 2)), (sine, upright_tile(ROT // 2))]

    n1, n2, active, slope, fed, upright, rows = call(
        front_kernel,
        (ranks,),
        [(x_all, tile(width)), (vec, whole_block((8, width))),
         (qkv_bias_own, whole_block((1, mixed_cols)))] + angles
        + [(weights, column(0)), (weights, column(1)), (weights, column(2))],
        [(shape((count, width), bf16), tile(width)), (shape((count, width), bf16), tile(width)),
         (shape((count, hidden), bf16), tile(hidden)), (shape((count, hidden), bf16), tile(hidden)),
         (shape((count, width), f32), tile(width)),
         (shape((mixed_cols, count), bf16), upright_tile(mixed_cols)),
         (shape((3 * heads, count, HD), bf16),
          pl.BlockSpec((3 * heads, own, HD), lambda t: (0, t, 0)))],
    )

    all_heads = lambda j: pl.BlockSpec((heads, count, HD), lambda *_: (j, 0, 0))
    soft_spec = pl.BlockSpec((1, count, own), lambda t, h: (h, 0, t))
    inv_spec = pl.BlockSpec((1, 8, own), lambda t, h: (h, 0, t))
    soft, inverse, heads_low, part_out = call(
        attend_kernel,
        (ranks, heads),
        [(span, upright_tile(8)), (place[:, None], whole_block((count, 1))),
         (rows, all_heads(1)), (upright, pl.BlockSpec((HD, own), lambda t, h: (h, t))),
         (upright, pl.BlockSpec((HD, count), lambda t, h: (2 * heads + h, 0))),
         (fed, tile(width)), (out_own, whole_block((cols, width)))],
        [(shape((heads, count, count), bf16), soft_spec),
         (shape((heads, 8, count), f32), inv_spec),
         (shape((cols, count), bf16), upright_tile(cols)),
         (shape((count, width), bf16), tile(width))],
        [pltpu.VMEM((count, own), f32)],
    )

    def give_back(parts):
        parts = parts.reshape(ranks, own, width)
        total = parts[0].astype(f32)
        for r in range(1, ranks):
            total = total + shift(parts[r], -r, ranks).astype(f32)
        return total

    hidden_out = (
        x_own.astype(f32) + (vectors[:, 4] + vectors[:, 5])[None] + give_back(part_out)
    ).astype(bf16)

    scaled, part_up, part_down, feed_sums = call(
        feed_back_kernel,
        (ranks,),
        [(dy_all, tile(width)), (x_all, tile(width)), (active, tile(hidden)),
         (slope, tile(hidden)), (n2, tile(width)), (vec, whole_block((8, width))),
         (weights, column(0)), (weights, column(1))],
        [(shape((count, width), f32), tile(width)),
         (shape((width, hidden), bf16), whole_block((width, hidden))),
         (shape((hidden, width), bf16), whole_block((hidden, width))),
         (shape((8, width), f32), whole_block((8, width)))],
        [pltpu.VMEM((width, hidden), f32), pltpu.VMEM((hidden, width), f32)],
    )
    feed_part = lax.psum_scatter(
        jnp.concatenate([part_up, part_down], axis=1), "dp", scatter_dimension=0, tiled=True
    )

    gquery, gkey, gvalue, part_proj = call(
        attend_back_kernel,
        (ranks, heads),
        [(dy_all, tile(width)), (out_own, whole_block((cols, width))),
         (heads_low, upright_tile(cols)), (inverse, inv_spec), (soft, soft_spec),
         (rows, all_heads(2)), (upright, pl.BlockSpec((HD, count), lambda t, h: (heads + h, 0))),
         (rows, pl.BlockSpec((1, own, HD), lambda t, h: (h, t, 0)))] + angles,
        [(shape((cols, count), f32), upright_tile(cols)),
         (shape((heads, count, HD), f32), whole_block((heads, count, HD))),
         (shape((heads, count, HD), f32), whole_block((heads, count, HD))),
         (shape((cols, width), f32), whole_block((cols, width)))],
        [pltpu.VMEM((cols, own), f32)],
    )

    head_tile = pl.BlockSpec((heads, own, HD), lambda t: (0, t, 0))
    total, part_attn, attn_sums, attn_bias = call(
        rear_kernel,
        (ranks,),
        [(gquery, upright_tile(cols)), (gkey, head_tile), (gvalue, head_tile)] + angles
        + [(n1, tile(width)), (x_all, tile(width)), (scaled, tile(width)),
           (vec, whole_block((8, width))), (weights, column(2))],
        [(shape((count, width), bf16), tile(width)),
         (shape((width, mixed_cols), bf16), whole_block((width, mixed_cols))),
         (shape((8, width), f32), whole_block((8, width))),
         (shape((8, mixed_cols), f32), whole_block((8, mixed_cols)))],
        [pltpu.VMEM((width, mixed_cols), f32)],
    )

    dy = dy_own.astype(f32)
    grad = give_back(total)
    rows_own = x_own.astype(f32)
    centred = rows_own - jnp.mean(rows_own, axis=-1, keepdims=True)
    rstd = lax.rsqrt(jnp.mean(centred * centred, axis=-1, keepdims=True) + eps)
    hat = centred * rstd
    grad_in = dy + rstd * (
        grad
        - jnp.mean(grad, axis=-1, keepdims=True)
        - hat * jnp.mean(grad * hat, axis=-1, keepdims=True)
    )

    qkv_bias_part = lax.dynamic_update_slice(
        jnp.zeros((3, ranks, cols), f32), attn_bias[0].reshape(3, 1, cols), (0, rank, 0)
    )
    up_bias_part = lax.dynamic_update_slice(
        jnp.zeros(ranks * hidden, f32), feed_sums[2], (rank * hidden,)
    )
    small_part = jnp.concatenate(
        [
            jnp.stack(
                [attn_sums[0], attn_sums[1], feed_sums[0], feed_sums[1], jnp.sum(dy, axis=0)],
                axis=1,
            ),
            qkv_bias_part.reshape(width, 3),
            up_bias_part.reshape(width, ratio),
        ],
        axis=1,
    ).astype(bf16)
    attn_part = lax.psum_scatter(
        jnp.concatenate(
            [
                part_attn,
                part_proj.astype(bf16).reshape(width, cols),
                jnp.pad(small_part, ((0, 0), (0, 128 - small_part.shape[1]))),
            ],
            axis=1,
        ),
        "dp",
        scatter_dimension=0,
        tiled=True,
    )
    factor = 1.0 / math.sqrt(count * groups)

    def exchange(parts):
        parts = parts.reshape(ranks, share, parts.shape[1])
        return lax.all_to_all(parts, "seq", 0, 0, tiled=True).astype(f32)

    def to_owner(parts):
        home = [((k % groups) * ranks + k // groups, k) for k in range(spread)]
        return lax.ppermute(parts, ("dp", "seq"), home).astype(f32) * factor

    up_own = jnp.transpose(exchange(feed_part[:, :hidden]), (1, 0, 2)) * factor
    down_own = to_owner(feed_part[:, hidden:])
    rest = exchange(
        jnp.concatenate([attn_part[:, :mixed_cols], attn_part[:, mixed_cols + cols :]], axis=1)
    )
    qkv_own = rest[:, :, :mixed_cols].reshape(ranks, share, 3, cols) * factor
    small_own = jnp.sum(rest[:, :, mixed_cols:], axis=0) * factor
    proj_own = to_owner(attn_part[:, mixed_cols : mixed_cols + cols]).reshape(share, width)
    return (
        hidden_out.reshape(hidden_in.shape),
        grad_in.astype(bf16).reshape(hidden_in.shape),
        small_own[:, 0],
        small_own[:, 1],
        small_own[:, 2],
        small_own[:, 3],
        jnp.transpose(qkv_own, (1, 2, 0, 3)).reshape(share, 3 * width),
        small_own[:, 5:8].reshape(share * 3),
        proj_own,
        small_own[:, 4],
        up_own.reshape(share, ranks * hidden),
        small_own[:, 8 : 8 + ratio].reshape(share * ratio),
        down_own,
        small_own[:, 4],
    )


def per_device(hidden_in, *rest):
    heads = hidden_in.shape[-1] // HD
    fits = heads % lax.axis_size("seq") == 0 and lax.axis_size("dp") == 8
    return (per_device_heads if fits else per_device_split)(hidden_in, *rest)


def solution(mesh):
    in_specs = (
        P("dp", "seq", None, None),
        P(),
        P("dp", None),
        P(("dp", "seq")),
        P(("dp", "seq")),
        P(("dp", "seq")),
        P(("dp", "seq")),
        P(("dp", "seq"), None),
        P(("dp", "seq")),
        P(("dp", "seq"), None),
        P(("dp", "seq")),
        P(("dp", "seq"), None),
        P(("dp", "seq")),
        P(("dp", "seq"), None),
        P(("dp", "seq")),
        P("dp", "seq", None, None),
    )
    out_specs = (
        P("dp", "seq", None, None),
        P("dp", "seq", None, None),
        P(("dp", "seq")),
        P(("dp", "seq")),
        P(("dp", "seq")),
        P(("dp", "seq")),
        P(("dp", "seq"), None),
        P(("dp", "seq")),
        P(("dp", "seq"), None),
        P(("dp", "seq")),
        P(("dp", "seq"), None),
        P(("dp", "seq")),
        P(("dp", "seq"), None),
        P(("dp", "seq")),
    )
    return jax.shard_map(
        per_device, mesh=mesh, in_specs=in_specs, out_specs=out_specs, check_vma=False
    )
```

```python
import functools
import math

import jax
import jax.numpy as jnp
from jax import lax
from jax.experimental import pallas as pl
from jax.experimental.pallas import tpu as pltpu
from jax.sharding import PartitionSpec as P

HD = 64
ROT = 16


eps = 1e-05
masked = -1e30


def layer_norm(rows, gain, shift):
    mean = jnp.mean(rows, axis=-1, keepdims=True)
    centred = rows - mean
    spread = jnp.mean(centred * centred, axis=-1, keepdims=True)
    return centred * lax.rsqrt(spread + eps) * gain + shift


def frequencies():
    return jnp.power(10000.0, -2.0 * jnp.arange(ROT // 2, dtype=jnp.float32) / ROT)


def rotate(heads, cosine, sine):
    half_rot = ROT // 2
    first = heads[..., :half_rot]
    second = heads[..., half_rot:ROT]
    return jnp.concatenate(
        [first * cosine - second * sine, second * cosine + first * sine, heads[..., ROT:]], axis=-1
    )


def doc_ids(positions, ends):
    return jnp.sum((positions[None, :, None] >= ends[:, None, :]).astype(jnp.int32), axis=-1)


def times_transposed(left, right):
    return lax.dot_general(
        left, right, (((1,), (1,)), ((), ())), preferred_element_type=jnp.float32
    )


def inner_rows(left, right):
    return lax.dot_general(
        left, right, (((0,), (0,)), ((), ())), preferred_element_type=jnp.float32
    )


def per_device_split(
    hidden_in,
    stretch_order,
    doc_lengths,
    attn_gain,
    attn_shift,
    feed_gain,
    feed_shift,
    qkv_weight,
    qkv_bias,
    out_weight,
    out_bias,
    up_weight,
    up_bias,
    down_weight,
    down_bias,
    grad_out,
):
    whole = (
        lax.all_gather(attn_gain, ("dp", "seq"), axis=0, tiled=True),
        lax.all_gather(attn_shift, ("dp", "seq"), axis=0, tiled=True),
        lax.all_gather(feed_gain, ("dp", "seq"), axis=0, tiled=True),
        lax.all_gather(feed_shift, ("dp", "seq"), axis=0, tiled=True),
        lax.all_gather(qkv_weight, ("dp", "seq"), axis=0, tiled=True),
        lax.all_gather(qkv_bias, ("dp", "seq"), axis=0, tiled=True),
        lax.all_gather(out_weight, ("dp", "seq"), axis=0, tiled=True),
        lax.all_gather(out_bias, ("dp", "seq"), axis=0, tiled=True),
        lax.all_gather(up_weight, ("dp", "seq"), axis=0, tiled=True),
        lax.all_gather(up_bias, ("dp", "seq"), axis=0, tiled=True),
        lax.all_gather(down_weight, ("dp", "seq"), axis=0, tiled=True),
        lax.all_gather(down_bias, ("dp", "seq"), axis=0, tiled=True),
    )
    seqs, blocks_own, half, width = hidden_in.shape
    heads = width // HD
    hidden_units = whole[8].shape[1]
    ratio = hidden_units // width
    queries = blocks_own * half
    count = seqs * queries
    scale_qk = 1.0 / math.sqrt(HD)
    lane = lax.axis_index("seq")
    offsets = jnp.arange(half, dtype=jnp.int32)
    own_blocks = lax.dynamic_slice_in_dim(stretch_order, lane * blocks_own, blocks_own)
    own_pos = (own_blocks[:, None] * half + offsets[None, :]).reshape(queries)
    ends = jnp.cumsum(doc_lengths, axis=1)[:, :-1]
    own_doc = doc_ids(own_pos, ends)
    angle = own_pos.astype(jnp.float32)[:, None] * frequencies()[None, :]
    cosine = jnp.cos(angle)[None, :, None, :]
    sine = jnp.sin(angle)[None, :, None, :]

    def allowed_of(key_pos, key_doc):
        causal = key_pos[None, None, None, :] <= own_pos[None, None, :, None]
        same = key_doc[:, None, None, :] == own_doc[:, None, :, None]
        return causal & same

    rows = hidden_in.astype(jnp.float32).reshape(count, width)
    normed_first, pull_first = jax.vjp(
        layer_norm, rows, whole[0].astype(jnp.float32), whole[1].astype(jnp.float32)
    )
    normed_second, pull_second = jax.vjp(
        layer_norm, rows, whole[2].astype(jnp.float32), whole[3].astype(jnp.float32)
    )
    first_low = normed_first.astype(jnp.bfloat16)
    second_low = normed_second.astype(jnp.bfloat16)
    mixed = jnp.dot(first_low, whole[4], preferred_element_type=jnp.float32) + whole[5].astype(
        jnp.float32
    )
    mixed = mixed.reshape(seqs, queries, 3, heads, HD)
    query = rotate(mixed[:, :, 0], cosine, sine).astype(jnp.bfloat16)
    key_own = (
        rotate(mixed[:, :, 1], cosine, sine)
        .astype(jnp.bfloat16)
        .reshape(seqs, blocks_own, half, width)
    )
    value_own = mixed[:, :, 2].astype(jnp.bfloat16).reshape(seqs, blocks_own, half, width)
    top = jnp.full((seqs, heads, queries), masked, jnp.float32)
    key_piece = lax.all_gather(key_own, "seq", axis=1, tiled=True)
    value_piece = lax.all_gather(value_own, "seq", axis=1, tiled=True)
    blocks = key_piece.shape[1]
    key_pos = (stretch_order[:, None] * half + offsets[None, :]).reshape(blocks * half)
    allowed = allowed_of(key_pos, doc_ids(key_pos, ends))
    keys = key_piece.reshape(seqs, blocks * half, heads, HD)
    values = value_piece.reshape(seqs, blocks * half, heads, HD)
    scores = (
        jnp.einsum("sqhd,skhd->shqk", query, keys, preferred_element_type=jnp.float32) * scale_qk
    )
    scores = jnp.where(allowed, scores, masked)
    new_top = jnp.maximum(top, jnp.max(scores, axis=-1))
    weights = jnp.where(allowed, jnp.exp(scores - new_top[..., None]), 0.0)
    total = jnp.sum(weights, axis=-1)
    accum = jnp.einsum(
        "shqk,skhd->shqd", weights.astype(jnp.bfloat16), values, preferred_element_type=jnp.float32
    )
    top, total, accum = (new_top, total, accum)
    logsum = top + jnp.log(total)
    heads_rows = jnp.transpose(accum / total[..., None], (0, 2, 1, 3))
    heads_low = heads_rows.reshape(count, width).astype(jnp.bfloat16)
    attended = jnp.dot(heads_low, whole[6], preferred_element_type=jnp.float32) + whole[7].astype(
        jnp.float32
    )
    inner = jnp.dot(second_low, whole[8], preferred_element_type=jnp.float32) + whole[9].astype(
        jnp.float32
    )
    active, pull_gelu = jax.vjp(lambda v: jax.nn.gelu(v, approximate=False), inner)
    active_low = active.astype(jnp.bfloat16)
    fed = jnp.dot(active_low, whole[10], preferred_element_type=jnp.float32) + whole[11].astype(
        jnp.float32
    )
    hidden_out = (rows + attended + fed).astype(jnp.bfloat16).reshape(hidden_in.shape)
    params_back = (
        lax.all_gather(attn_gain, ("dp", "seq"), axis=0, tiled=True),
        lax.all_gather(attn_shift, ("dp", "seq"), axis=0, tiled=True),
        lax.all_gather(feed_gain, ("dp", "seq"), axis=0, tiled=True),
        lax.all_gather(feed_shift, ("dp", "seq"), axis=0, tiled=True),
        lax.all_gather(qkv_weight, ("dp", "seq"), axis=0, tiled=True),
        lax.all_gather(qkv_bias, ("dp", "seq"), axis=0, tiled=True),
        lax.all_gather(out_weight, ("dp", "seq"), axis=0, tiled=True),
        lax.all_gather(out_bias, ("dp", "seq"), axis=0, tiled=True),
        lax.all_gather(up_weight, ("dp", "seq"), axis=0, tiled=True),
        lax.all_gather(up_bias, ("dp", "seq"), axis=0, tiled=True),
        lax.all_gather(down_weight, ("dp", "seq"), axis=0, tiled=True),
        lax.all_gather(down_bias, ("dp", "seq"), axis=0, tiled=True),
    )
    upstream_low = grad_out.reshape(count, width)
    upstream = upstream_low.astype(jnp.float32)
    grad_bias_out = jnp.sum(upstream, axis=0)
    grad_active = times_transposed(upstream_low, params_back[10])
    (grad_inner,) = pull_gelu(grad_active)
    inner_low = grad_inner.astype(jnp.bfloat16)
    grad_up_bias = jnp.sum(grad_inner, axis=0)
    grad_second = times_transposed(inner_low, params_back[8])
    grad_heads = times_transposed(upstream_low, params_back[6])
    heads_grad_low = grad_heads.astype(jnp.bfloat16).reshape(seqs, queries, heads, HD)
    delta = jnp.transpose(
        jnp.sum(heads_grad_low.astype(jnp.float32) * heads_rows, axis=-1), (0, 2, 1)
    )
    key_all, value_all = (
        lax.all_gather(key_own, "seq", axis=1, tiled=True),
        lax.all_gather(value_own, "seq", axis=1, tiled=True),
    )
    blocks_all = key_all.shape[1]

    def backstep(grad_query, block):
        keys = lax.dynamic_slice_in_dim(key_all, block, 1, axis=1).reshape(seqs, half, heads, HD)
        values = lax.dynamic_slice_in_dim(value_all, block, 1, axis=1).reshape(
            seqs, half, heads, HD
        )
        key_pos = lax.dynamic_slice_in_dim(stretch_order, block, 1) * half + offsets
        allowed = allowed_of(key_pos, doc_ids(key_pos, ends))
        scores = (
            jnp.einsum("sqhd,skhd->shqk", query, keys, preferred_element_type=jnp.float32)
            * scale_qk
        )
        probs = jnp.where(allowed, jnp.exp(scores - logsum[..., None]), 0.0)
        grad_probs = jnp.einsum(
            "sqhd,skhd->shqk", heads_grad_low, values, preferred_element_type=jnp.float32
        )
        grad_scores = (probs * (grad_probs - delta[..., None]) * scale_qk).astype(jnp.bfloat16)
        grad_query = grad_query + jnp.einsum(
            "shqk,skhd->sqhd", grad_scores, keys, preferred_element_type=jnp.float32
        )
        key_term = jnp.einsum(
            "shqk,sqhd->skhd", grad_scores, query, preferred_element_type=jnp.float32
        )
        value_term = jnp.einsum(
            "shqk,sqhd->skhd",
            probs.astype(jnp.bfloat16),
            heads_grad_low,
            preferred_element_type=jnp.float32,
        )
        return (
            grad_query,
            (key_term.reshape(seqs, half, width), value_term.reshape(seqs, half, width)),
        )

    grad_query, (grad_keys, grad_values) = lax.scan(
        backstep,
        jnp.zeros((seqs, queries, heads, HD), jnp.float32),
        jnp.arange(blocks_all, dtype=jnp.int32),
    )
    key_part, value_part = (
        lax.psum_scatter(
            grad_keys.astype(jnp.bfloat16), "seq", scatter_dimension=0, tiled=True
        ).astype(jnp.float32),
        lax.psum_scatter(
            grad_values.astype(jnp.bfloat16), "seq", scatter_dimension=0, tiled=True
        ).astype(jnp.float32),
    )
    key_sum = jnp.transpose(key_part, (1, 0, 2, 3))
    value_sum = jnp.transpose(value_part, (1, 0, 2, 3))
    query_back = rotate(grad_query, cosine, -sine).reshape(count, width)
    key_back = rotate(key_sum.reshape(seqs, queries, heads, HD), cosine, -sine).reshape(
        count, width
    )
    grad_mixed = jnp.concatenate([query_back, key_back, value_sum.reshape(count, width)], axis=1)
    mixed_low = grad_mixed.astype(jnp.bfloat16)
    grad_qkv_bias = jnp.sum(grad_mixed, axis=0)
    grad_first = times_transposed(mixed_low, params_back[4])
    rows_first, gain_first, shift_first = pull_first(grad_first)
    rows_second, gain_second, shift_second = pull_second(grad_second)
    grad_in = (upstream + rows_first + rows_second).astype(jnp.bfloat16).reshape(hidden_in.shape)
    factor = 1.0 / math.sqrt(count * lax.axis_size("dp") * lax.axis_size("seq"))
    small_columns = jnp.stack(
        [gain_first, shift_first, gain_second, shift_second, grad_bias_out], axis=1
    )
    qkv_bias_rows = grad_qkv_bias.reshape(width, 3)
    up_bias_rows = grad_up_bias.reshape(width, ratio)
    part_qkv = inner_rows(first_low, mixed_low)
    part_out = inner_rows(heads_low, upstream_low)
    part_up = inner_rows(second_low, inner_low)
    part_down = inner_rows(active_low, upstream_low).reshape(
        lax.axis_size(("dp", "seq")) * qkv_weight.shape[0], ratio * width
    )
    owned = lax.psum_scatter(
        jnp.concatenate(
            [part_qkv, part_out, part_up, part_down, small_columns, qkv_bias_rows, up_bias_rows],
            axis=1,
        )
        * factor,
        ("dp", "seq"),
        scatter_dimension=0,
        tiled=True,
    )
    own_rows = owned.shape[0]
    edge_out = 3 * width
    edge_up = edge_out + width
    edge_down = edge_up + hidden_units
    edge_small = edge_down + hidden_units
    edge_qkvb = edge_small + 5
    edge_upb = edge_qkvb + 3
    grad_qkv_own = owned[:, :edge_out]
    grad_out_own = owned[:, edge_out:edge_up]
    grad_up_own = owned[:, edge_up:edge_down]
    grad_down_own = owned[:, edge_down:edge_small].reshape(own_rows * ratio, width)
    grad_bias_own = owned[:, edge_small + 4]
    grad_qkvb_own = owned[:, edge_qkvb:edge_upb].reshape(own_rows * 3)
    grad_upb_own = owned[:, edge_upb : edge_upb + ratio].reshape(own_rows * ratio)
    return (
        hidden_out,
        grad_in,
        owned[:, edge_small],
        owned[:, edge_small + 1],
        owned[:, edge_small + 2],
        owned[:, edge_small + 3],
        grad_qkv_own,
        grad_qkvb_own,
        grad_out_own,
        grad_bias_own,
        grad_up_own,
        grad_upb_own,
        grad_down_own,
        grad_bias_own,
    )


f32 = jnp.float32
bf16 = jnp.bfloat16


def whole_block(shape):
    return pl.BlockSpec(shape, lambda *_: (0,) * len(shape))


def normalise(rows):
    centred = rows - jnp.mean(rows, axis=-1, keepdims=True)
    spread = jnp.mean(centred * centred, axis=-1, keepdims=True)
    return centred * lax.rsqrt(spread + eps)


def turn(upright, cosine, sine):
    half_rot = ROT // 2
    first = upright[:half_rot]
    second = upright[half_rot:ROT]
    return [first * cosine - second * sine, second * cosine + first * sine, upright[ROT:]]


def product(left, right, left_dim=1, right_dim=0):
    return lax.dot_general(
        left, right, (((left_dim,), (right_dim,)), ((), ())), preferred_element_type=f32
    )


def places(owners, per, base, index):
    lanes = lax.broadcasted_iota(jnp.int32, (LANES, index.shape[1]), 0)
    rows = lax.broadcasted_iota(jnp.int32, (owners, index.shape[1]), 0)
    return rows == index // per, (lanes == base + index % per).astype(bf16)


def vector_maps(rank, share, ranks, cols, hidden, ratio):
    line = lambda n: lax.broadcasted_iota(jnp.int32, (1, n), 1)
    width = ranks * cols
    part = line(3 * cols)
    maps = [(share, j * share, line(width)) for j in range(6)]
    maps.append((3 * share, 6 * share, part // cols * width + rank * cols + part % cols))
    held = ratio * share
    unit = line(hidden)
    maps.append((held, 9 * share, (unit // held * ranks + rank) * held + unit % held))
    return maps


def pack_kernel(rank_ref, up_ref, qkv_ref, out_ref, *refs, vectors, held):
    outs = refs[vectors:]
    ranks = len(outs) - 1
    rank = rank_ref[0]
    up, qkv = up_ref[...], qkv_ref[...]
    width = qkv.shape[1] // 3
    cols = width // ranks
    share = up.shape[0]
    line = jnp.concatenate([ref[...][None].astype(f32) for ref in refs[:vectors]], axis=1)
    line = jnp.pad(line, ((0, 0), (0, LANES - line.shape[1])))
    lines = [line[:, j : j + 128] for j in range(0, LANES, 128)]
    small = jnp.concatenate(lines + [jnp.zeros((share - len(lines), 128), f32)]).astype(bf16)
    for t in range(ranks):
        block = jnp.concatenate(
            [up[:, at : at + held] for at in range(t * held, up.shape[1], ranks * held)]
            + [qkv[:, j * width + t * cols : j * width + (t + 1) * cols] for j in range(3)]
            + [small],
            axis=1,
        )
        for r in range(ranks):

            @pl.when((rank + r) % ranks == t)
            def _():
                outs[r][...] = block

    out = out_ref[...].astype(f32)
    flat = jnp.concatenate([out[:, j * cols : (j + 1) * cols] for j in range(ranks)], axis=0)
    outs[-1][...] = flat.astype(bf16)


def land_kernel(rank_ref, *refs, hidden):
    ranks = len(refs) - 3
    rank = rank_ref[0]
    blocks = [ref[...].astype(f32) for ref in refs[:ranks]]
    ordered = []
    for t in range(ranks):
        picked = blocks[0]
        for r in range(1, ranks):
            picked = jnp.where((rank - r + ranks) % ranks == t, blocks[r], picked)
        ordered.append(picked)
    landed = jnp.concatenate(ordered, axis=0).astype(bf16)
    tail = landed.shape[1] - 128
    refs[-1][...] = jnp.concatenate(
        [landed[:, :hidden], refs[ranks][...], landed[:, hidden:tail], refs[ranks + 1][...],
         landed[:, tail:]], axis=1,
    )


def store_at(refs, step, block):
    for at, ref in enumerate(refs):

        @pl.when(step == at)
        def _():
            ref[...] = block


def front_kernel(
    rank_ref, x_ref, small_ref, cos_ref, sin_ref, up_ref, down_ref, attn_ref,
    n1_ref, n2_ref, act_ref, slope_ref, fed_ref, upright_ref, rows_ref, vec_ref, own_out_ref, bias_ref,
    *, ranks, ratio,
):
    width, part3 = n1_ref.shape[1], upright_ref.shape[0]
    cols, hidden = part3 // 3, act_ref.shape[1]
    owners = ranks * 8
    share = width // owners

    @pl.when(pl.program_id(0) == 0)
    def _():
        table = small_ref[...].astype(f32).reshape(owners, share, 128)
        table = jnp.concatenate([table[:, j, :] for j in range(LANES // 128)], axis=1).astype(bf16)
        vectors = []
        for per, base, index in vector_maps(rank_ref[0], share, ranks, cols, hidden, ratio):
            rows, lanes = places(owners, per, base, index)
            spread = jnp.where(rows, product(table, lanes), 0.0)
            vectors.append(jnp.sum(spread, axis=0, keepdims=True))
        bias_ref[...] = vectors[6]
        vec_ref[...] = jnp.concatenate(
            vectors[:4] + [vectors[7], vectors[4] + vectors[5], jnp.zeros((2, width), f32)], axis=0
        )
        flat = attn_ref[:, part3:].astype(f32)
        rebuilt = []
        for d in range(8):
            start = d * share * ranks
            rebuilt.append(
                jnp.concatenate(
                    [flat[start + j * share : start + (j + 1) * share] for j in range(ranks)], axis=1
                )
            )
        own_out_ref[...] = jnp.concatenate(rebuilt, axis=0).astype(bf16)

    hat = normalise(x_ref[...].astype(f32))
    vec = vec_ref[...]
    n1 = (hat * vec[0:1] + vec[1:2]).astype(bf16)
    n2 = (hat * vec[2:3] + vec[3:4]).astype(bf16)
    n1_ref[...] = n1
    n2_ref[...] = n2
    width = upright_ref.shape[0]
    mixed = product(n1, attn_ref[:, :width]) + bias_ref[...]
    upright = mixed.T
    cosine, sine = cos_ref[...], sin_ref[...]
    part = width // 3
    pieces = []
    for start in range(0, part, HD):
        pieces += [v * HD**-0.5 for v in turn(upright[start : start + HD], cosine, sine)]
    for start in range(part, 2 * part, HD):
        pieces += turn(upright[start : start + HD], cosine, sine)
    upright = jnp.concatenate(pieces + [upright[2 * part :]], axis=0)
    upright_ref[...] = upright.astype(bf16)
    mixed = upright.T.astype(bf16)
    for j in range(width // HD):
        rows_ref[j] = mixed[:, j * HD : (j + 1) * HD]
    inner = product(n2, up_ref[...]) + vec[4:5]
    phi = 0.5 + 0.5 * lax.erf(inner * math.sqrt(0.5))
    active = (inner * phi).astype(bf16)
    act_ref[...] = active
    bell = jnp.exp(inner * inner * -0.5) * (1.0 / math.sqrt(2.0 * math.pi))
    slope_ref[...] = (phi + inner * bell).astype(bf16)
    fed_ref[...] = product(active, down_ref[...])


def attend_kernel(
    span_ref, place_ref, key_ref, query_ref, value_ref, fed_ref, out_ref,
    soft_ref, inv_ref, heads_ref, *refs,
):
    *sum_refs, bias_ref = refs
    head = pl.program_id(1)

    @pl.when(head == 0)
    def _():
        place = place_ref[...]
        ok = (place <= span_ref[0:1]) & (place >= span_ref[1:2])
        bias_ref[...] = jnp.where(ok, 0.0, masked)

    scores = product(key_ref[head], query_ref[...]) + bias_ref[...]
    weights = jnp.exp(scores - jnp.max(scores, axis=0, keepdims=True))
    inverse = 1.0 / jnp.sum(weights, axis=0, keepdims=True)
    soft = weights.astype(bf16)
    soft_ref[0] = soft
    inv_ref[0] = jnp.broadcast_to(inverse, inv_ref.shape[1:])
    spot = pl.ds(pl.multiple_of(head * HD, HD), HD)
    heads_ref[spot, :] = (product(value_ref[...], soft) * inverse).astype(bf16)

    @pl.when(head == pl.num_programs(1) - 1)
    def _():
        part = (fed_ref[...] + product(heads_ref[...], out_ref[...], 0, 0)).astype(bf16)
        store_at(sum_refs, pl.program_id(0), part)


def feed_back_kernel(
    dy_ref, x_ref, act_ref, slope_ref, n2_ref, vec_ref, up_ref, down_ref, heads_ref,
    scaled_ref, grads_ref, sums_ref, acc_up, acc_down, acc_out,
    *, ranks,
):
    step = pl.program_id(0)

    @pl.when(step == 0)
    def _():
        acc_up[...] = jnp.zeros_like(acc_up)
        acc_down[...] = jnp.zeros_like(acc_down)
        acc_out[...] = jnp.zeros_like(acc_out)
        sums_ref[...] = jnp.zeros_like(sums_ref)
        sums_ref[3:4] = jnp.sum(dy_ref[...].astype(f32), axis=0, keepdims=True)

    dy = dy_ref[...]
    grad_inner = product(dy, down_ref[...], 1, 1) * slope_ref[...].astype(f32)
    low = grad_inner.astype(bf16)
    grad = product(low, up_ref[...], 1, 1)
    hat = normalise(x_ref[...].astype(f32))
    scaled_ref[...] = grad * vec_ref[2:3]
    sums_ref[0:1] += jnp.sum(grad * hat, axis=0, keepdims=True)
    sums_ref[1:2] += jnp.sum(grad, axis=0, keepdims=True)
    sums_ref[2:3] += jnp.sum(grad_inner, axis=0, keepdims=True)
    acc_up[...] += product(n2_ref[...], low, 0, 0)
    acc_down[...] += product(act_ref[...], dy, 0, 0)
    acc_out[...] += product(heads_ref[...], dy)

    @pl.when(step == pl.num_programs(0) - 1)
    def _():
        cols = acc_out.shape[0]
        share = cols // 8
        flat = []
        for d in range(8):
            rows = acc_out[d * share : (d + 1) * share]
            flat += [rows[:, j * cols : (j + 1) * cols] for j in range(ranks)]
        flat = jnp.concatenate(flat, axis=0)
        edge = acc_up.shape[1]
        grads_ref[:, :edge] = acc_up[...].astype(bf16)
        grads_ref[:, edge : edge + acc_down.shape[1]] = acc_down[...].astype(bf16)
        grads_ref[:, edge + acc_down.shape[1] :] = flat.astype(bf16)


def attend_back_kernel(
    dy_ref, out_ref, heads_ref, inv_ref, soft_ref, value_ref, key_ref, query_ref, cos_ref, sin_ref,
    gquery_ref, gkey_ref, gvalue_ref, held_ref,
):
    step, head = pl.program_id(0), pl.program_id(1)

    @pl.when((step == 0) & (head == 0))
    def _():
        gkey_ref[...] = jnp.zeros_like(gkey_ref)
        gvalue_ref[...] = jnp.zeros_like(gvalue_ref)

    @pl.when(head == 0)
    def _():
        held_ref[...] = product(out_ref[...], dy_ref[...], 1, 1).astype(bf16).astype(f32)

    spot = pl.ds(pl.multiple_of(head * HD, HD), HD)
    lifted = held_ref[spot, :] * inv_ref[0, 0:1]
    delta = jnp.sum(lifted * heads_ref[spot, :].astype(f32), axis=0, keepdims=True)
    lifted_rows = lifted.T.astype(bf16)
    soft = soft_ref[0]
    grad_soft = product(value_ref[head], lifted.astype(bf16))
    grad_scores = (soft.astype(f32) * (grad_soft - delta)).astype(bf16)
    gvalue_ref[head] += product(soft, lifted_rows)
    gkey_ref[head] += product(grad_scores, query_ref[0])
    back = product(key_ref[...], grad_scores) * HD**-0.5
    gquery_ref[spot, :] = jnp.concatenate(turn(back, cos_ref[...], -sin_ref[...]), axis=0)


def rear_kernel(
    spot_ref, gquery_ref, gkey_ref, gvalue_ref, cos_ref, sin_ref, n1_ref, x_ref, scaled_ref, vec_ref,
    attn_ref, feed_ref, *refs, ranks, ratio,
):
    total_refs, grads_ref = refs[:ranks], refs[ranks]
    acc_ref, sums_ref, gbias_ref, small_ref = refs[-4:]
    step = pl.program_id(0)

    @pl.when(step == 0)
    def _():
        acc_ref[...] = jnp.zeros_like(acc_ref)
        sums_ref[...] = jnp.zeros_like(sums_ref)
        gbias_ref[...] = jnp.zeros_like(gbias_ref)

    cosine, sine = cos_ref[...], sin_ref[...]
    pieces = [gquery_ref[...]]
    for j in range(gkey_ref.shape[0]):
        pieces += turn(gkey_ref[j].T, cosine, -sine)
    pieces += [gvalue_ref[j].T for j in range(gvalue_ref.shape[0])]
    mixed = jnp.concatenate(pieces, axis=0).T
    gbias_ref[0:1] += jnp.sum(mixed, axis=0, keepdims=True)
    low = mixed.astype(bf16)
    grad = product(low, attn_ref[:, : low.shape[1]], 1, 1)
    hat = normalise(x_ref[...].astype(f32))
    store_at(total_refs, step, (grad * vec_ref[0:1] + scaled_ref[...]).astype(bf16))
    sums_ref[0:1] += jnp.sum(grad * hat, axis=0, keepdims=True)
    sums_ref[1:2] += jnp.sum(grad, axis=0, keepdims=True)
    acc_ref[...] += product(n1_ref[...], low, 0, 0)

    @pl.when(step == pl.num_programs(0) - 1)
    def _():
        width, part3 = acc_ref.shape
        cols, owners = part3 // 3, small_ref.shape[0]
        share = width // owners
        feed = feed_ref[...]
        vectors = [sums_ref[0:1], sums_ref[1:2], feed[0:1], feed[1:2], feed[3:4], None]
        vectors += [gbias_ref[0:1], feed[2:3]]
        maps = vector_maps(spot_ref[0], share, ranks, cols, feed.shape[1], ratio)
        table = jnp.zeros((owners, LANES), f32)
        for vector, (per, base, index) in zip(vectors, maps):
            if vector is not None:
                rows, lanes = places(owners, per, base, index)
                table += product(jnp.where(rows, vector, 0.0).astype(bf16), lanes, 1, 1)
        small_ref[...] = jnp.zeros_like(small_ref)
        for j in range(LANES // 128):
            small_ref[:, j, :] = table[:, j * 128 : (j + 1) * 128]
        small = small_ref[...].reshape(width, 128)
        grads_ref[...] = jnp.concatenate([acc_ref[...], small], axis=1).astype(bf16)


def finish_kernel(
    rank_ref, *refs, factor, hidden,
):
    qkv_ref, up_ref, proj_ref, down_ref, *small_refs = refs[-11:]
    down_in, proj_in, refs = refs[-13], refs[-12], refs[:-13]
    ranks, rank = len(refs), rank_ref[0]
    blocks = [ref[...].astype(f32) * factor for ref in refs]
    share, width = proj_ref.shape
    cols = width // ranks
    small = jnp.zeros((share, 128), f32)
    for t in range(ranks):
        picked = blocks[0]
        for r in range(1, ranks):
            picked = jnp.where((rank - r + ranks) % ranks == t, blocks[r], picked)
        for at in range(0, hidden, down_ref.shape[0]):
            where = at * ranks + t * down_ref.shape[0]
            up_ref[:, where : where + down_ref.shape[0]] = picked[:, at : at + down_ref.shape[0]]
        for j in range(3):
            at = j * width + t * cols
            qkv_ref[:, at : at + cols] = picked[:, hidden + j * cols : hidden + (j + 1) * cols]
        small += picked[:, hidden + 3 * cols :]
    down_ref[...] = down_in[...].astype(f32) * factor
    rows = proj_in[...].astype(f32) * factor
    proj_ref[...] = jnp.concatenate(
        [rows[j * share : (j + 1) * share] for j in range(ranks)], axis=1
    )
    line = jnp.concatenate([small[j : j + 1] for j in range(LANES // 128)], axis=1)
    at = 0
    for j, ref in enumerate(small_refs):
        if j == 5:
            at += share
        ref[...] = line[0, at : at + ref.shape[0]]
        at += ref.shape[0]


LANES = 384
VMEM = 56 * 1024 * 1024


SMEM = pl.BlockSpec(memory_space=pltpu.SMEM)


def call(kernel, grid, ins, outs, scratch=(), cost=1, first=()):
    arrays, in_specs = zip(*ins)
    shapes, out_specs = zip(*outs)
    return pl.pallas_call(
        kernel,
        grid_spec=pltpu.PrefetchScalarGridSpec(
            num_scalar_prefetch=len(first),
            grid=grid,
            in_specs=list(in_specs),
            out_specs=list(out_specs),
            scratch_shapes=list(scratch),
        ),
        out_shape=list(shapes),
        compiler_params=pltpu.CompilerParams(vmem_limit_bytes=VMEM),
        cost_estimate=pl.CostEstimate(flops=cost * 10**9, bytes_accessed=0, transcendentals=0),
    )(*first, *arrays)


def after(value, *others):
    return lax.optimization_barrier((value,) + others)[0]


def shift(block, amount, ranks):
    return lax.ppermute(block, "seq", [(k, (k + amount) % ranks) for k in range(ranks)])


def around(blocks, sign, ranks):
    order = sorted(range(1, ranks), key=lambda r: abs(ranks - 2 * r))
    got = {r: shift(blocks[r - 1], sign * r, ranks) for r in order}
    return [got[r] for r in range(1, ranks)]


def swap(block, mask):
    return lax.ppermute(block, "dp", [(k, k ^ mask) for k in range(8)])


def gather_dp(piece, by_x, by_y):
    half = piece.shape[0] // 2
    place = lax.axis_index("dp")
    three = jnp.stack([piece, by_x, by_y])
    other = swap(three, 1)
    corner = jnp.concatenate([swap(by_x[:half], 4), swap(by_y[half:], 2)])
    far = swap(corner, 1)
    whole = jnp.zeros((8,) + piece.shape, piece.dtype)
    for mask, part in (
        (0, piece), (2, by_x), (4, by_y), (1, other[0]), (3, other[1]), (5, other[2]),
        (6, corner), (7, far),
    ):
        whole = lax.dynamic_update_slice(whole, part[None], (place ^ mask, 0, 0))
    return whole.reshape(8 * piece.shape[0], piece.shape[1])


def scatter_dp(parts):
    parts = lax.all_to_all(parts.reshape(8, -1, parts.shape[1]), "dp", 0, 0, tiled=True)
    return jnp.sum(parts.astype(f32), axis=0).astype(bf16)


def per_device_heads(
    hidden_in,
    stretch_order,
    doc_lengths,
    attn_gain,
    attn_shift,
    feed_gain,
    feed_shift,
    qkv_weight,
    qkv_bias,
    out_weight,
    out_bias,
    up_weight,
    up_bias,
    down_weight,
    down_bias,
    grad_out,
):
    ranks, groups = lax.axis_size("seq"), lax.axis_size("dp")
    rank = lax.axis_index("seq")
    blocks_own, half, width = hidden_in.shape[1:]
    own = blocks_own * half
    count = ranks * own
    share = qkv_weight.shape[0]
    piece = share * ranks
    cols = width // ranks
    heads = cols // HD
    hidden = up_weight.shape[1] // ranks
    ratio = up_weight.shape[1] // width
    mixed_cols = 3 * cols
    edge = hidden + width + mixed_cols

    small = [attn_gain, attn_shift, feed_gain, feed_shift, out_bias, down_bias, qkv_bias, up_bias]
    shape = jax.ShapeDtypeStruct
    spot = jnp.stack([rank, lax.axis_index("dp")])
    sent = (share, hidden + mixed_cols + 128)
    *packed, out_piece = call(
        functools.partial(pack_kernel, vectors=len(small), held=ratio * share),
        (1,),
        [(spot, SMEM)]
        + [(a, whole_block(a.shape)) for a in (up_weight, qkv_weight, out_weight, *small)],
        [(shape(sent, bf16), whole_block(sent))] * ranks
        + [(shape((piece, cols), bf16), whole_block((piece, cols)))],
    )
    spread = ranks * groups
    out_piece = lax.ppermute(
        out_piece, ("dp", "seq"),
        [(k, (k % groups) * ranks + k // groups) for k in range(spread)],
    )
    landed = packed[:1] + around(packed[1:], 1, ranks)
    total_cols = edge + cols + 128
    (weight_piece,) = call(
        functools.partial(land_kernel, hidden=hidden),
        (1,),
        [(spot, SMEM)] + [(a, whole_block(a.shape)) for a in (*landed, down_weight, out_piece)],
        [(shape((piece, total_cols), bf16), whole_block((piece, total_cols)))],
    )
    by_x, by_y = swap(weight_piece, 2), swap(weight_piece, 4)
    weights = gather_dp(weight_piece, by_x, by_y)

    x_own = hidden_in.reshape(own, width)
    dy_own = grad_out.reshape(own, width)
    x_go = after(x_own, *landed)
    x_near = after(x_own, by_x, by_y)
    x_sent = [x_go] * (ranks - 2) + [x_near]
    x_all = jnp.concatenate([x_own] + around(x_sent, 1, ranks))
    dy_go = after(dy_own, x_all, weights)
    dy_all = jnp.concatenate([dy_own] + around([dy_go] * (ranks - 1), 1, ranks))

    owners = (rank - jnp.arange(ranks, dtype=jnp.int32)) % ranks
    blocks = stretch_order.reshape(ranks, blocks_own)[owners].reshape(-1)
    place = (blocks[:, None] * half + jnp.arange(half, dtype=jnp.int32)[None]).reshape(count)
    ends = jnp.cumsum(doc_lengths[0])[:-1]
    first = jnp.max(jnp.where(place[:, None] >= ends[None], ends[None], 0), axis=1)
    span = jnp.concatenate([place[None], first[None], jnp.zeros((6, count), jnp.int32)])
    angle = frequencies()[:, None] * place.astype(f32)[None]
    cosine, sine = jnp.cos(angle), jnp.sin(angle)

    tile = lambda w: pl.BlockSpec((own, w), lambda t, *_: (t, 0))
    upright_tile = lambda n: pl.BlockSpec((n, own), lambda t, *_: (0, t))
    column = lambda j: pl.BlockSpec((width, width), lambda *_: (0, j))
    angles = [(cosine, upright_tile(ROT // 2)), (sine, upright_tile(ROT // 2))]

    n1, n2, active, slope, fed, upright, rows, vec, out_own = call(
        functools.partial(front_kernel, ranks=ranks, ratio=ratio),
        (ranks,),
        [(spot, SMEM), (x_all, tile(width)),
         (weights, pl.BlockSpec((width, 128), lambda t: (0, (edge + cols) // 128)))] + angles
        + [(weights, column(0)), (weights, column(1)), (weights, column(2))],
        [(shape((count, width), bf16), tile(width)), (shape((count, width), bf16), tile(width)),
         (shape((count, hidden), bf16), tile(hidden)), (shape((count, hidden), bf16), tile(hidden)),
         (shape((count, width), f32), tile(width)),
         (shape((mixed_cols, count), bf16), upright_tile(mixed_cols)),
         (shape((3 * heads, count, HD), bf16),
          pl.BlockSpec((3 * heads, own, HD), lambda t: (0, t, 0))),
         (shape((8, width), f32), whole_block((8, width))),
         (shape((cols, width), bf16), whole_block((cols, width)))],
        [pltpu.VMEM((1, mixed_cols), f32)],
        cost=10,
    )

    all_heads = lambda j: pl.BlockSpec((heads, count, HD), lambda *_: (j, 0, 0))
    soft_spec = pl.BlockSpec((1, count, own), lambda t, h, *_: (h, 0, t))
    inv_spec = pl.BlockSpec((1, 8, own), lambda t, h, *_: (h, 0, t))
    soft, inverse, heads_low, *part_out = call(
        attend_kernel,
        (ranks, heads),
        [(span, upright_tile(8)), (place[:, None], whole_block((count, 1))),
         (rows, all_heads(1)), (upright, pl.BlockSpec((HD, own), lambda t, h, *_: (h, t))),
         (upright, pl.BlockSpec((HD, count), lambda t, h, *_: (2 * heads + h, 0))),
         (fed, tile(width)), (out_own, whole_block((cols, width)))],
        [(shape((heads, count, count), bf16), soft_spec),
         (shape((heads, 8, count), f32), inv_spec),
         (shape((cols, count), bf16), upright_tile(cols))]
        + [(shape((own, width), bf16), whole_block((own, width)))] * ranks,
        [pltpu.VMEM((count, own), f32)],
        cost=16,
    )

    dy_all = after(dy_all, heads_low)
    scaled, grads_feed, feed_sums = call(
        functools.partial(feed_back_kernel, ranks=ranks),
        (ranks,),
        [(dy_all, tile(width)), (x_all, tile(width)), (active, tile(hidden)),
         (slope, tile(hidden)), (n2, tile(width)), (vec, whole_block((8, width))),
         (weights, column(0)), (weights, column(1)), (heads_low, upright_tile(cols))],
        [(shape((count, width), f32), tile(width)),
         (shape((width, edge - mixed_cols + cols), bf16),
          whole_block((width, edge - mixed_cols + cols))),
         (shape((8, width), f32), whole_block((8, width)))],
        [pltpu.VMEM((width, hidden), f32), pltpu.VMEM((hidden, width), f32),
         pltpu.VMEM((cols, width), f32)],
        cost=12,
    )
    feed_part = scatter_dp(grads_feed)

    far = [r for r in range(1, ranks) if 2 * r == ranks]
    near = [r for r in range(1, ranks) if r not in far]
    out_parts = part_out[:1] + [shift(part_out[r], -r, ranks) for r in near]
    heads_low = after(heads_low, scaled, *out_parts)
    far_parts = [shift(after(part_out[r], scaled), -r, ranks) for r in far]
    gquery, gkey, gvalue = call(
        attend_back_kernel,
        (ranks, heads),
        [(dy_all, tile(width)), (out_own, whole_block((cols, width))),
         (heads_low, upright_tile(cols)), (inverse, inv_spec), (soft, soft_spec),
         (rows, all_heads(2)), (upright, pl.BlockSpec((HD, count), lambda t, h: (heads + h, 0))),
         (rows, pl.BlockSpec((1, own, HD), lambda t, h: (h, t, 0)))] + angles,
        [(shape((cols, count), f32), upright_tile(cols)),
         (shape((heads, count, HD), f32), whole_block((heads, count, HD))),
         (shape((heads, count, HD), f32), whole_block((heads, count, HD)))],
        [pltpu.VMEM((cols, own), f32)],
        cost=16,
    )
    gquery = after(gquery, *far_parts)
    out_sum = sum(part.astype(f32) for part in out_parts + far_parts)
    hidden_out = (x_own.astype(f32) + vec[5:6] + out_sum).astype(bf16)

    head_tile = pl.BlockSpec((heads, own, HD), lambda t: (0, t, 0))
    *total, grads_attn = call(
        functools.partial(rear_kernel, ranks=ranks, ratio=ratio),
        (ranks,),
        [(spot, SMEM), (gquery, upright_tile(cols)), (gkey, head_tile), (gvalue, head_tile)]
        + angles
        + [(n1, tile(width)), (x_all, tile(width)), (scaled, tile(width)),
           (vec, whole_block((8, width))), (weights, column(2)),
           (feed_sums, whole_block((8, width)))],
        [(shape((own, width), bf16), whole_block((own, width)))] * ranks
        + [(shape((width, mixed_cols + 128), bf16), whole_block((width, mixed_cols + 128)))],
        [pltpu.VMEM((width, mixed_cols), f32), pltpu.VMEM((8, width), f32),
         pltpu.VMEM((8, mixed_cols), f32), pltpu.VMEM((spread, share, 128), f32)],
        cost=11,
    )

    dy = dy_own.astype(f32)
    grad_parts = total[:1] + around(total[1:], -1, ranks)
    attn_part = scatter_dp(after(grads_attn, feed_part))
    parts = jnp.concatenate([feed_part[:, :hidden], attn_part], axis=1)
    parts = parts.reshape(ranks, share, parts.shape[1])
    parts = [lax.dynamic_index_in_dim(parts, (rank + r) % ranks, 0, False) for r in range(ranks)]
    parts = parts[:1] + around([after(p, *grad_parts) for p in parts[1:]], 1, ranks)
    grad = sum(part.astype(f32) for part in grad_parts)
    rows_own = x_own.astype(f32)
    centred = rows_own - jnp.mean(rows_own, axis=-1, keepdims=True)
    rstd = lax.rsqrt(jnp.mean(centred * centred, axis=-1, keepdims=True) + eps)
    hat = centred * rstd
    grad_in = dy + rstd * (
        grad
        - jnp.mean(grad, axis=-1, keepdims=True)
        - hat * jnp.mean(grad * hat, axis=-1, keepdims=True)
    )

    factor = 1.0 / math.sqrt(count * groups)
    home = [((k % groups) * ranks + k // groups, k) for k in range(spread)]
    proj_part = lax.ppermute(feed_part[:, hidden + width :], ("dp", "seq"), home)
    down_part = feed_part[:, hidden : hidden + width]
    results = [(share, 3 * width), (share, ranks * hidden), (share, width), (piece, width)]
    results += [(share,)] * 5 + [(3 * share,), (ratio * share,)]
    qkv_own, up_own, proj_own, down_own, *small_own = call(
        functools.partial(finish_kernel, factor=factor, hidden=hidden),
        (1,),
        [(spot, SMEM)] + [(a, whole_block(a.shape)) for a in (*parts, down_part, proj_part)],
        [(shape(size, f32), whole_block(size)) for size in results],
    )
    return (
        hidden_out.reshape(hidden_in.shape),
        grad_in.astype(bf16).reshape(hidden_in.shape),
        *small_own[:4],
        qkv_own,
        small_own[5],
        proj_own,
        small_own[4],
        up_own,
        small_own[6],
        down_own,
        small_own[4],
    )


def per_device(hidden_in, *rest):
    heads = hidden_in.shape[-1] // HD
    fits = heads % lax.axis_size("seq") == 0 and lax.axis_size("dp") == 8
    return (per_device_heads if fits else per_device_split)(hidden_in, *rest)


def solution(mesh):
    in_specs = (
        P("dp", "seq", None, None),
        P(),
        P("dp", None),
        P(("dp", "seq")),
        P(("dp", "seq")),
        P(("dp", "seq")),
        P(("dp", "seq")),
        P(("dp", "seq"), None),
        P(("dp", "seq")),
        P(("dp", "seq"), None),
        P(("dp", "seq")),
        P(("dp", "seq"), None),
        P(("dp", "seq")),
        P(("dp", "seq"), None),
        P(("dp", "seq")),
        P("dp", "seq", None, None),
    )
    out_specs = (
        P("dp", "seq", None, None),
        P("dp", "seq", None, None),
        P(("dp", "seq")),
        P(("dp", "seq")),
        P(("dp", "seq")),
        P(("dp", "seq")),
        P(("dp", "seq"), None),
        P(("dp", "seq")),
        P(("dp", "seq"), None),
        P(("dp", "seq")),
        P(("dp", "seq"), None),
        P(("dp", "seq")),
        P(("dp", "seq"), None),
        P(("dp", "seq")),
    )
    return jax.shard_map(
        per_device, mesh=mesh, in_specs=in_specs, out_specs=out_specs, check_vma=False
    )
```

```python
import functools
import math

import jax
import jax.numpy as jnp
from jax import lax
from jax.experimental import pallas as pl
from jax.experimental.pallas import tpu as pltpu
from jax.sharding import PartitionSpec as P

HD = 64
ROT = 16


eps = 1e-05
masked = -1e30


def layer_norm(rows, gain, shift):
    mean = jnp.mean(rows, axis=-1, keepdims=True)
    centred = rows - mean
    spread = jnp.mean(centred * centred, axis=-1, keepdims=True)
    return centred * lax.rsqrt(spread + eps) * gain + shift


def frequencies():
    return jnp.power(10000.0, -2.0 * jnp.arange(ROT // 2, dtype=jnp.float32) / ROT)


def rotate(heads, cosine, sine):
    half_rot = ROT // 2
    first = heads[..., :half_rot]
    second = heads[..., half_rot:ROT]
    return jnp.concatenate(
        [first * cosine - second * sine, second * cosine + first * sine, heads[..., ROT:]], axis=-1
    )


def doc_ids(positions, ends):
    return jnp.sum((positions[None, :, None] >= ends[:, None, :]).astype(jnp.int32), axis=-1)


def times_transposed(left, right):
    return lax.dot_general(
        left, right, (((1,), (1,)), ((), ())), preferred_element_type=jnp.float32
    )


def inner_rows(left, right):
    return lax.dot_general(
        left, right, (((0,), (0,)), ((), ())), preferred_element_type=jnp.float32
    )


def per_device_split(
    hidden_in,
    stretch_order,
    doc_lengths,
    attn_gain,
    attn_shift,
    feed_gain,
    feed_shift,
    qkv_weight,
    qkv_bias,
    out_weight,
    out_bias,
    up_weight,
    up_bias,
    down_weight,
    down_bias,
    grad_out,
):
    whole = (
        lax.all_gather(attn_gain, ("dp", "seq"), axis=0, tiled=True),
        lax.all_gather(attn_shift, ("dp", "seq"), axis=0, tiled=True),
        lax.all_gather(feed_gain, ("dp", "seq"), axis=0, tiled=True),
        lax.all_gather(feed_shift, ("dp", "seq"), axis=0, tiled=True),
        lax.all_gather(qkv_weight, ("dp", "seq"), axis=0, tiled=True),
        lax.all_gather(qkv_bias, ("dp", "seq"), axis=0, tiled=True),
        lax.all_gather(out_weight, ("dp", "seq"), axis=0, tiled=True),
        lax.all_gather(out_bias, ("dp", "seq"), axis=0, tiled=True),
        lax.all_gather(up_weight, ("dp", "seq"), axis=0, tiled=True),
        lax.all_gather(up_bias, ("dp", "seq"), axis=0, tiled=True),
        lax.all_gather(down_weight, ("dp", "seq"), axis=0, tiled=True),
        lax.all_gather(down_bias, ("dp", "seq"), axis=0, tiled=True),
    )
    seqs, blocks_own, half, width = hidden_in.shape
    heads = width // HD
    hidden_units = whole[8].shape[1]
    ratio = hidden_units // width
    queries = blocks_own * half
    count = seqs * queries
    scale_qk = 1.0 / math.sqrt(HD)
    lane = lax.axis_index("seq")
    offsets = jnp.arange(half, dtype=jnp.int32)
    own_blocks = lax.dynamic_slice_in_dim(stretch_order, lane * blocks_own, blocks_own)
    own_pos = (own_blocks[:, None] * half + offsets[None, :]).reshape(queries)
    ends = jnp.cumsum(doc_lengths, axis=1)[:, :-1]
    own_doc = doc_ids(own_pos, ends)
    angle = own_pos.astype(jnp.float32)[:, None] * frequencies()[None, :]
    cosine = jnp.cos(angle)[None, :, None, :]
    sine = jnp.sin(angle)[None, :, None, :]

    def allowed_of(key_pos, key_doc):
        causal = key_pos[None, None, None, :] <= own_pos[None, None, :, None]
        same = key_doc[:, None, None, :] == own_doc[:, None, :, None]
        return causal & same

    rows = hidden_in.astype(jnp.float32).reshape(count, width)
    normed_first, pull_first = jax.vjp(
        layer_norm, rows, whole[0].astype(jnp.float32), whole[1].astype(jnp.float32)
    )
    normed_second, pull_second = jax.vjp(
        layer_norm, rows, whole[2].astype(jnp.float32), whole[3].astype(jnp.float32)
    )
    first_low = normed_first.astype(jnp.bfloat16)
    second_low = normed_second.astype(jnp.bfloat16)
    mixed = jnp.dot(first_low, whole[4], preferred_element_type=jnp.float32) + whole[5].astype(
        jnp.float32
    )
    mixed = mixed.reshape(seqs, queries, 3, heads, HD)
    query = rotate(mixed[:, :, 0], cosine, sine).astype(jnp.bfloat16)
    key_own = (
        rotate(mixed[:, :, 1], cosine, sine)
        .astype(jnp.bfloat16)
        .reshape(seqs, blocks_own, half, width)
    )
    value_own = mixed[:, :, 2].astype(jnp.bfloat16).reshape(seqs, blocks_own, half, width)
    top = jnp.full((seqs, heads, queries), masked, jnp.float32)
    key_piece = lax.all_gather(key_own, "seq", axis=1, tiled=True)
    value_piece = lax.all_gather(value_own, "seq", axis=1, tiled=True)
    blocks = key_piece.shape[1]
    key_pos = (stretch_order[:, None] * half + offsets[None, :]).reshape(blocks * half)
    allowed = allowed_of(key_pos, doc_ids(key_pos, ends))
    keys = key_piece.reshape(seqs, blocks * half, heads, HD)
    values = value_piece.reshape(seqs, blocks * half, heads, HD)
    scores = (
        jnp.einsum("sqhd,skhd->shqk", query, keys, preferred_element_type=jnp.float32) * scale_qk
    )
    scores = jnp.where(allowed, scores, masked)
    new_top = jnp.maximum(top, jnp.max(scores, axis=-1))
    weights = jnp.where(allowed, jnp.exp(scores - new_top[..., None]), 0.0)
    total = jnp.sum(weights, axis=-1)
    accum = jnp.einsum(
        "shqk,skhd->shqd", weights.astype(jnp.bfloat16), values, preferred_element_type=jnp.float32
    )
    top, total, accum = (new_top, total, accum)
    logsum = top + jnp.log(total)
    heads_rows = jnp.transpose(accum / total[..., None], (0, 2, 1, 3))
    heads_low = heads_rows.reshape(count, width).astype(jnp.bfloat16)
    attended = jnp.dot(heads_low, whole[6], preferred_element_type=jnp.float32) + whole[7].astype(
        jnp.float32
    )
    inner = jnp.dot(second_low, whole[8], preferred_element_type=jnp.float32) + whole[9].astype(
        jnp.float32
    )
    active, pull_gelu = jax.vjp(lambda v: jax.nn.gelu(v, approximate=False), inner)
    active_low = active.astype(jnp.bfloat16)
    fed = jnp.dot(active_low, whole[10], preferred_element_type=jnp.float32) + whole[11].astype(
        jnp.float32
    )
    hidden_out = (rows + attended + fed).astype(jnp.bfloat16).reshape(hidden_in.shape)
    params_back = (
        lax.all_gather(attn_gain, ("dp", "seq"), axis=0, tiled=True),
        lax.all_gather(attn_shift, ("dp", "seq"), axis=0, tiled=True),
        lax.all_gather(feed_gain, ("dp", "seq"), axis=0, tiled=True),
        lax.all_gather(feed_shift, ("dp", "seq"), axis=0, tiled=True),
        lax.all_gather(qkv_weight, ("dp", "seq"), axis=0, tiled=True),
        lax.all_gather(qkv_bias, ("dp", "seq"), axis=0, tiled=True),
        lax.all_gather(out_weight, ("dp", "seq"), axis=0, tiled=True),
        lax.all_gather(out_bias, ("dp", "seq"), axis=0, tiled=True),
        lax.all_gather(up_weight, ("dp", "seq"), axis=0, tiled=True),
        lax.all_gather(up_bias, ("dp", "seq"), axis=0, tiled=True),
        lax.all_gather(down_weight, ("dp", "seq"), axis=0, tiled=True),
        lax.all_gather(down_bias, ("dp", "seq"), axis=0, tiled=True),
    )
    upstream_low = grad_out.reshape(count, width)
    upstream = upstream_low.astype(jnp.float32)
    grad_bias_out = jnp.sum(upstream, axis=0)
    grad_active = times_transposed(upstream_low, params_back[10])
    (grad_inner,) = pull_gelu(grad_active)
    inner_low = grad_inner.astype(jnp.bfloat16)
    grad_up_bias = jnp.sum(grad_inner, axis=0)
    grad_second = times_transposed(inner_low, params_back[8])
    grad_heads = times_transposed(upstream_low, params_back[6])
    heads_grad_low = grad_heads.astype(jnp.bfloat16).reshape(seqs, queries, heads, HD)
    delta = jnp.transpose(
        jnp.sum(heads_grad_low.astype(jnp.float32) * heads_rows, axis=-1), (0, 2, 1)
    )
    key_all, value_all = (
        lax.all_gather(key_own, "seq", axis=1, tiled=True),
        lax.all_gather(value_own, "seq", axis=1, tiled=True),
    )
    blocks_all = key_all.shape[1]

    def backstep(grad_query, block):
        keys = lax.dynamic_slice_in_dim(key_all, block, 1, axis=1).reshape(seqs, half, heads, HD)
        values = lax.dynamic_slice_in_dim(value_all, block, 1, axis=1).reshape(
            seqs, half, heads, HD
        )
        key_pos = lax.dynamic_slice_in_dim(stretch_order, block, 1) * half + offsets
        allowed = allowed_of(key_pos, doc_ids(key_pos, ends))
        scores = (
            jnp.einsum("sqhd,skhd->shqk", query, keys, preferred_element_type=jnp.float32)
            * scale_qk
        )
        probs = jnp.where(allowed, jnp.exp(scores - logsum[..., None]), 0.0)
        grad_probs = jnp.einsum(
            "sqhd,skhd->shqk", heads_grad_low, values, preferred_element_type=jnp.float32
        )
        grad_scores = (probs * (grad_probs - delta[..., None]) * scale_qk).astype(jnp.bfloat16)
        grad_query = grad_query + jnp.einsum(
            "shqk,skhd->sqhd", grad_scores, keys, preferred_element_type=jnp.float32
        )
        key_term = jnp.einsum(
            "shqk,sqhd->skhd", grad_scores, query, preferred_element_type=jnp.float32
        )
        value_term = jnp.einsum(
            "shqk,sqhd->skhd",
            probs.astype(jnp.bfloat16),
            heads_grad_low,
            preferred_element_type=jnp.float32,
        )
        return (
            grad_query,
            (key_term.reshape(seqs, half, width), value_term.reshape(seqs, half, width)),
        )

    grad_query, (grad_keys, grad_values) = lax.scan(
        backstep,
        jnp.zeros((seqs, queries, heads, HD), jnp.float32),
        jnp.arange(blocks_all, dtype=jnp.int32),
    )
    key_part, value_part = (
        lax.psum_scatter(
            grad_keys.astype(jnp.bfloat16), "seq", scatter_dimension=0, tiled=True
        ).astype(jnp.float32),
        lax.psum_scatter(
            grad_values.astype(jnp.bfloat16), "seq", scatter_dimension=0, tiled=True
        ).astype(jnp.float32),
    )
    key_sum = jnp.transpose(key_part, (1, 0, 2, 3))
    value_sum = jnp.transpose(value_part, (1, 0, 2, 3))
    query_back = rotate(grad_query, cosine, -sine).reshape(count, width)
    key_back = rotate(key_sum.reshape(seqs, queries, heads, HD), cosine, -sine).reshape(
        count, width
    )
    grad_mixed = jnp.concatenate([query_back, key_back, value_sum.reshape(count, width)], axis=1)
    mixed_low = grad_mixed.astype(jnp.bfloat16)
    grad_qkv_bias = jnp.sum(grad_mixed, axis=0)
    grad_first = times_transposed(mixed_low, params_back[4])
    rows_first, gain_first, shift_first = pull_first(grad_first)
    rows_second, gain_second, shift_second = pull_second(grad_second)
    grad_in = (upstream + rows_first + rows_second).astype(jnp.bfloat16).reshape(hidden_in.shape)
    factor = 1.0 / math.sqrt(count * lax.axis_size("dp") * lax.axis_size("seq"))
    small_columns = jnp.stack(
        [gain_first, shift_first, gain_second, shift_second, grad_bias_out], axis=1
    )
    qkv_bias_rows = grad_qkv_bias.reshape(width, 3)
    up_bias_rows = grad_up_bias.reshape(width, ratio)
    part_qkv = inner_rows(first_low, mixed_low)
    part_out = inner_rows(heads_low, upstream_low)
    part_up = inner_rows(second_low, inner_low)
    part_down = inner_rows(active_low, upstream_low).reshape(
        lax.axis_size(("dp", "seq")) * qkv_weight.shape[0], ratio * width
    )
    owned = lax.psum_scatter(
        jnp.concatenate(
            [part_qkv, part_out, part_up, part_down, small_columns, qkv_bias_rows, up_bias_rows],
            axis=1,
        )
        * factor,
        ("dp", "seq"),
        scatter_dimension=0,
        tiled=True,
    )
    own_rows = owned.shape[0]
    edge_out = 3 * width
    edge_up = edge_out + width
    edge_down = edge_up + hidden_units
    edge_small = edge_down + hidden_units
    edge_qkvb = edge_small + 5
    edge_upb = edge_qkvb + 3
    grad_qkv_own = owned[:, :edge_out]
    grad_out_own = owned[:, edge_out:edge_up]
    grad_up_own = owned[:, edge_up:edge_down]
    grad_down_own = owned[:, edge_down:edge_small].reshape(own_rows * ratio, width)
    grad_bias_own = owned[:, edge_small + 4]
    grad_qkvb_own = owned[:, edge_qkvb:edge_upb].reshape(own_rows * 3)
    grad_upb_own = owned[:, edge_upb : edge_upb + ratio].reshape(own_rows * ratio)
    return (
        hidden_out,
        grad_in,
        owned[:, edge_small],
        owned[:, edge_small + 1],
        owned[:, edge_small + 2],
        owned[:, edge_small + 3],
        grad_qkv_own,
        grad_qkvb_own,
        grad_out_own,
        grad_bias_own,
        grad_up_own,
        grad_upb_own,
        grad_down_own,
        grad_bias_own,
    )


f32 = jnp.float32
bf16 = jnp.bfloat16


def whole_block(shape):
    return pl.BlockSpec(shape, lambda *_: (0,) * len(shape))


def normalise(rows):
    centred = rows - jnp.mean(rows, axis=-1, keepdims=True)
    spread = jnp.mean(centred * centred, axis=-1, keepdims=True)
    return centred * lax.rsqrt(spread + eps)


def turn(upright, cosine, sine):
    half_rot = ROT // 2
    first = upright[:half_rot]
    second = upright[half_rot:ROT]
    return [first * cosine - second * sine, second * cosine + first * sine, upright[ROT:]]


def product(left, right, left_dim=1, right_dim=0):
    return lax.dot_general(
        left, right, (((left_dim,), (right_dim,)), ((), ())), preferred_element_type=f32
    )


def places(owners, per, base, index):
    lanes = lax.broadcasted_iota(jnp.int32, (LANES, index.shape[1]), 0)
    rows = lax.broadcasted_iota(jnp.int32, (owners, index.shape[1]), 0)
    return rows == index // per, (lanes == base + index % per).astype(bf16)


def vector_maps(rank, share, ranks, cols, hidden, ratio):
    line = lambda n: lax.broadcasted_iota(jnp.int32, (1, n), 1)
    width = ranks * cols
    part = line(3 * cols)
    maps = [(share, j * share, line(width)) for j in range(6)]
    maps.append((3 * share, 6 * share, part // cols * width + rank * cols + part % cols))
    held = ratio * share
    unit = line(hidden)
    maps.append((held, 9 * share, (unit // held * ranks + rank) * held + unit % held))
    return maps


def pack_kernel(rank_ref, up_ref, qkv_ref, out_ref, *refs, vectors, held):
    outs = refs[vectors:]
    ranks = len(outs) - 1
    rank = rank_ref[0]
    up, qkv = up_ref[...], qkv_ref[...]
    width = qkv.shape[1] // 3
    cols = width // ranks
    share = up.shape[0]
    line = jnp.concatenate([ref[...][None].astype(f32) for ref in refs[:vectors]], axis=1)
    line = jnp.pad(line, ((0, 0), (0, LANES - line.shape[1])))
    lines = [line[:, j : j + 128] for j in range(0, LANES, 128)]
    small = jnp.concatenate(lines + [jnp.zeros((share - len(lines), 128), f32)]).astype(bf16)
    for t in range(ranks):
        block = jnp.concatenate(
            [up[:, at : at + held] for at in range(t * held, up.shape[1], ranks * held)]
            + [qkv[:, j * width + t * cols : j * width + (t + 1) * cols] for j in range(3)]
            + [small],
            axis=1,
        )
        for r in range(ranks):

            @pl.when((rank + r) % ranks == t)
            def _():
                outs[r][...] = block

    out = out_ref[...].astype(f32)
    flat = jnp.concatenate([out[:, j * cols : (j + 1) * cols] for j in range(ranks)], axis=0)
    outs[-1][...] = flat.astype(bf16)


def land_kernel(rank_ref, *refs, hidden):
    ranks = len(refs) - 3
    rank = rank_ref[0]
    blocks = [ref[...].astype(f32) for ref in refs[:ranks]]
    ordered = []
    for t in range(ranks):
        picked = blocks[0]
        for r in range(1, ranks):
            picked = jnp.where((rank - r + ranks) % ranks == t, blocks[r], picked)
        ordered.append(picked)
    landed = jnp.concatenate(ordered, axis=0).astype(bf16)
    tail = landed.shape[1] - 128
    refs[-1][...] = jnp.concatenate(
        [landed[:, :hidden], refs[ranks][...], landed[:, hidden:tail], refs[ranks + 1][...],
         landed[:, tail:]], axis=1,
    )


def join(refs):
    return jnp.concatenate([ref[...] for ref in refs], axis=0)


def store_blocks(refs, spot_ref, step, tile, parts):
    half = tile.shape[0] // parts
    for k in range(parts):
        block = tile[k * half : (k + 1) * half]
        where = spot_ref[2 + step * parts + k]
        for r, ref in enumerate(refs):
            for slot in range(parts):

                @pl.when(where == r * parts + slot)
                def _():
                    ref[slot * half : (slot + 1) * half, :] = block


def front_kernel(rank_ref, *refs, ranks, ratio, parts):
    x_refs, (small_ref, cos_ref, sin_ref, up_ref, down_ref, attn_ref) = refs[:parts], refs[parts:-10]
    n1_ref, n2_ref, act_ref, slope_ref, fed_ref, upright_ref, rows_ref = refs[-10:-3]
    vec_ref, own_out_ref, bias_ref = refs[-3:]
    width, part3 = n1_ref.shape[1], upright_ref.shape[0]
    cols, hidden = part3 // 3, act_ref.shape[1]
    owners = ranks * 8
    share = width // owners

    @pl.when(pl.program_id(0) == 0)
    def _():
        table = small_ref[...].astype(f32).reshape(owners, share, 128)
        table = jnp.concatenate([table[:, j, :] for j in range(LANES // 128)], axis=1).astype(bf16)
        vectors = []
        for per, base, index in vector_maps(rank_ref[0], share, ranks, cols, hidden, ratio):
            rows, lanes = places(owners, per, base, index)
            spread = jnp.where(rows, product(table, lanes), 0.0)
            vectors.append(jnp.sum(spread, axis=0, keepdims=True))
        bias_ref[...] = vectors[6]
        vec_ref[...] = jnp.concatenate(
            vectors[:4] + [vectors[7], vectors[4] + vectors[5], jnp.zeros((2, width), f32)], axis=0
        )
        flat = attn_ref[:, part3:].astype(f32)
        rebuilt = []
        for d in range(8):
            start = d * share * ranks
            rebuilt.append(
                jnp.concatenate(
                    [flat[start + j * share : start + (j + 1) * share] for j in range(ranks)], axis=1
                )
            )
        own_out_ref[...] = jnp.concatenate(rebuilt, axis=0).astype(bf16)

    hat = normalise(join(x_refs).astype(f32))
    vec = vec_ref[...]
    n1 = (hat * vec[0:1] + vec[1:2]).astype(bf16)
    n2 = (hat * vec[2:3] + vec[3:4]).astype(bf16)
    n1_ref[...] = n1
    n2_ref[...] = n2
    width = upright_ref.shape[0]
    mixed = product(n1, attn_ref[:, :width]) + bias_ref[...]
    upright = mixed.T
    cosine, sine = cos_ref[...], sin_ref[...]
    part = width // 3
    pieces = []
    for start in range(0, part, HD):
        pieces += [v * HD**-0.5 for v in turn(upright[start : start + HD], cosine, sine)]
    for start in range(part, 2 * part, HD):
        pieces += turn(upright[start : start + HD], cosine, sine)
    upright = jnp.concatenate(pieces + [upright[2 * part :]], axis=0)
    upright_ref[...] = upright.astype(bf16)
    mixed = upright.T.astype(bf16)
    for j in range(width // HD):
        rows_ref[j] = mixed[:, j * HD : (j + 1) * HD]
    inner = product(n2, up_ref[...]) + vec[4:5]
    phi = 0.5 + 0.5 * lax.erf(inner * math.sqrt(0.5))
    active = (inner * phi).astype(bf16)
    act_ref[...] = active
    bell = jnp.exp(inner * inner * -0.5) * (1.0 / math.sqrt(2.0 * math.pi))
    slope_ref[...] = (phi + inner * bell).astype(bf16)
    fed_ref[...] = product(active, down_ref[...])


def attend_kernel(spot_ref, *refs, ranks, parts):
    start_ref, key_ref, query_ref, value_ref, fed_ref, out_ref, soft_ref, inv_ref, heads_ref = refs[:9]
    step, own = pl.program_id(0), query_ref.shape[1]

    def tile(at):
        held = own * (at + 1)
        place = lax.broadcasted_iota(jnp.int32, (held, own), 0)
        asks = lax.broadcasted_iota(jnp.int32, (held, own), 1) + at * own
        bias = jnp.where((place <= asks) & (place >= start_ref[0:1]), 0.0, masked)
        for head in range(key_ref.shape[0]):
            spot = slice(head * HD, (head + 1) * HD)
            scores = product(key_ref[head, :held], query_ref[spot, :]) + bias
            weights = jnp.exp(scores - jnp.max(scores, axis=0, keepdims=True))
            inverse = 1.0 / jnp.sum(weights, axis=0, keepdims=True)
            soft = weights.astype(bf16)
            soft_ref[head, :held] = soft
            inv_ref[head : head + 1] = inverse
            heads_ref[spot, :] = (product(value_ref[spot, :held], soft) * inverse).astype(bf16)

    for at in range(ranks):
        pl.when(step == at)(functools.partial(tile, at))
    part = (fed_ref[...] + product(heads_ref[...], out_ref[...], 0, 0)).astype(bf16)
    store_blocks(refs[9:], spot_ref, step, part, parts)


def feed_back_kernel(spot_ref, *refs, ranks, parts):
    dy_refs, x_refs, refs = refs[:parts], refs[parts : 2 * parts], refs[2 * parts :]
    own_ref, act_ref, slope_ref, n2_ref, vec_ref, up_ref, down_ref, heads_ref = refs[:8]
    scaled_ref, grads_ref, sums_ref, acc_up, acc_down, acc_out = refs[8:]
    step = pl.program_id(0)

    @pl.when(step == 0)
    def _():
        acc_up[...] = jnp.zeros_like(acc_up)
        acc_down[...] = jnp.zeros_like(acc_down)
        acc_out[...] = jnp.zeros_like(acc_out)
        sums_ref[...] = jnp.zeros_like(sums_ref)
        sums_ref[3:4] = jnp.sum(own_ref[...].astype(f32), axis=0, keepdims=True)

    dy = join(dy_refs)
    grad_inner = product(dy, down_ref[...], 1, 1) * slope_ref[...].astype(f32)
    low = grad_inner.astype(bf16)
    grad = product(low, up_ref[...], 1, 1)
    hat = normalise(join(x_refs).astype(f32))
    scaled_ref[...] = grad * vec_ref[2:3]
    sums_ref[0:1] += jnp.sum(grad * hat, axis=0, keepdims=True)
    sums_ref[1:2] += jnp.sum(grad, axis=0, keepdims=True)
    sums_ref[2:3] += jnp.sum(grad_inner, axis=0, keepdims=True)
    acc_up[...] += product(n2_ref[...], low, 0, 0)
    acc_down[...] += product(act_ref[...], dy, 0, 0)
    acc_out[...] += product(heads_ref[...], dy)

    @pl.when(step == pl.num_programs(0) - 1)
    def _():
        cols = acc_out.shape[0]
        share = cols // 8
        flat = []
        for d in range(8):
            rows = acc_out[d * share : (d + 1) * share]
            flat += [rows[:, j * cols : (j + 1) * cols] for j in range(ranks)]
        flat = jnp.concatenate(flat, axis=0)
        edge = acc_up.shape[1]
        grads_ref[:, :edge] = acc_up[...].astype(bf16)
        grads_ref[:, edge : edge + acc_down.shape[1]] = acc_down[...].astype(bf16)
        grads_ref[:, edge + acc_down.shape[1] :] = flat.astype(bf16)


def attend_back_kernel(spot_ref, *refs, ranks, parts):
    dy_refs, refs = refs[:parts], refs[parts:]
    out_ref, heads_ref, inv_ref, soft_ref, value_ref, key_ref, query_ref, cos_ref, sin_ref = refs[:9]
    gquery_ref, gkey_ref, gvalue_ref = refs[9:]
    step, own = pl.program_id(0), cos_ref.shape[1]

    @pl.when(step == 0)
    def _():
        gkey_ref[...] = jnp.zeros_like(gkey_ref)
        gvalue_ref[...] = jnp.zeros_like(gvalue_ref)

    lifted_all = product(out_ref[...], join(dy_refs), 1, 1).astype(bf16).astype(f32)

    def tile(at):
        held = own * (at + 1)
        for head in range(gkey_ref.shape[0]):
            spot = slice(head * HD, (head + 1) * HD)
            lifted = lifted_all[spot] * inv_ref[head : head + 1]
            delta = jnp.sum(lifted * heads_ref[spot, :].astype(f32), axis=0, keepdims=True)
            lifted_rows = lifted.T.astype(bf16)
            soft = soft_ref[head, :held]
            grad_soft = product(value_ref[head, :held], lifted.astype(bf16))
            grad_scores = (soft.astype(f32) * (grad_soft - delta)).astype(bf16)
            gvalue_ref[head, :held] += product(soft, lifted_rows)
            gkey_ref[head, :held] += product(grad_scores, query_ref[head])
            back = product(key_ref[spot, :held], grad_scores) * HD**-0.5
            gquery_ref[spot, :] = jnp.concatenate(turn(back, cos_ref[...], -sin_ref[...]), axis=0)

    for at in range(ranks):
        pl.when(step == at)(functools.partial(tile, at))


def rear_kernel(spot_ref, *refs, ranks, parts):
    x_refs, refs = refs[:parts], refs[parts:]
    gquery_ref, gkey_ref, gvalue_ref, cos_ref, sin_ref, scaled_ref, vec_ref, attn_ref = refs[:8]
    mixed_ref, sums_ref, gbias_ref = refs[8:11]
    step = pl.program_id(0)

    @pl.when(step == 0)
    def _():
        sums_ref[...] = jnp.zeros_like(sums_ref)
        gbias_ref[...] = jnp.zeros_like(gbias_ref)

    cosine, sine = cos_ref[...], sin_ref[...]
    pieces = [gquery_ref[...]]
    for j in range(gkey_ref.shape[0]):
        pieces += turn(gkey_ref[j].T, cosine, -sine)
    pieces += [gvalue_ref[j].T for j in range(gvalue_ref.shape[0])]
    mixed = jnp.concatenate(pieces, axis=0).T
    gbias_ref[0:1] += jnp.sum(mixed, axis=0, keepdims=True)
    low = mixed.astype(bf16)
    mixed_ref[...] = low
    grad = product(low, attn_ref[:, : low.shape[1]], 1, 1)
    hat = normalise(join(x_refs).astype(f32))
    total = (grad * vec_ref[0:1] + scaled_ref[...]).astype(bf16)
    store_blocks(refs[11:], spot_ref, step, total, parts)
    sums_ref[0:1] += jnp.sum(grad * hat, axis=0, keepdims=True)
    sums_ref[1:2] += jnp.sum(grad, axis=0, keepdims=True)


def weigh_kernel(
    spot_ref, n1_ref, mixed_ref, sums_ref, gbias_ref, feed_ref, grads_ref, small_ref, *, ranks, ratio
):
    acc = product(n1_ref[...], mixed_ref[...], 0, 0)
    width, part3 = acc.shape
    cols, owners = part3 // 3, small_ref.shape[0]
    share = width // owners
    feed = feed_ref[...]
    vectors = [sums_ref[0:1], sums_ref[1:2], feed[0:1], feed[1:2], feed[3:4], None]
    vectors += [gbias_ref[0:1], feed[2:3]]
    maps = vector_maps(spot_ref[0], share, ranks, cols, feed.shape[1], ratio)
    table = jnp.zeros((owners, LANES), f32)
    for vector, (per, base, index) in zip(vectors, maps):
        if vector is not None:
            rows, lanes = places(owners, per, base, index)
            table += product(jnp.where(rows, vector, 0.0).astype(bf16), lanes, 1, 1)
    small_ref[...] = jnp.zeros_like(small_ref)
    for j in range(LANES // 128):
        small_ref[:, j, :] = table[:, j * 128 : (j + 1) * 128]
    small = small_ref[...].reshape(width, 128)
    grads_ref[...] = jnp.concatenate([acc, small], axis=1).astype(bf16)


def finish_kernel(
    rank_ref, *refs, factor, hidden,
):
    qkv_ref, up_ref, proj_ref, down_ref, *small_refs = refs[-11:]
    down_in, proj_in, refs = refs[-13], refs[-12], refs[:-13]
    ranks, rank = len(refs), rank_ref[0]
    blocks = [ref[...].astype(f32) * factor for ref in refs]
    share, width = proj_ref.shape
    cols = width // ranks
    small = jnp.zeros((share, 128), f32)
    for t in range(ranks):
        picked = blocks[0]
        for r in range(1, ranks):
            picked = jnp.where((rank - r + ranks) % ranks == t, blocks[r], picked)
        for at in range(0, hidden, down_ref.shape[0]):
            where = at * ranks + t * down_ref.shape[0]
            up_ref[:, where : where + down_ref.shape[0]] = picked[:, at : at + down_ref.shape[0]]
        for j in range(3):
            at = j * width + t * cols
            qkv_ref[:, at : at + cols] = picked[:, hidden + j * cols : hidden + (j + 1) * cols]
        small += picked[:, hidden + 3 * cols :]
    down_ref[...] = down_in[...].astype(f32) * factor
    rows = proj_in[...].astype(f32) * factor
    proj_ref[...] = jnp.concatenate(
        [rows[j * share : (j + 1) * share] for j in range(ranks)], axis=1
    )
    line = jnp.concatenate([small[j : j + 1] for j in range(LANES // 128)], axis=1)
    at = 0
    for j, ref in enumerate(small_refs):
        if j == 5:
            at += share
        ref[...] = line[0, at : at + ref.shape[0]]
        at += ref.shape[0]


LANES = 384
VMEM = 56 * 1024 * 1024


SMEM = pl.BlockSpec(memory_space=pltpu.SMEM)


def call(kernel, grid, ins, outs, scratch=(), cost=1, first=()):
    arrays, in_specs = zip(*ins)
    shapes, out_specs = zip(*outs)
    return pl.pallas_call(
        kernel,
        grid_spec=pltpu.PrefetchScalarGridSpec(
            num_scalar_prefetch=len(first),
            grid=grid,
            in_specs=list(in_specs),
            out_specs=list(out_specs),
            scratch_shapes=list(scratch),
        ),
        out_shape=list(shapes),
        compiler_params=pltpu.CompilerParams(vmem_limit_bytes=VMEM),
        cost_estimate=pl.CostEstimate(flops=cost * 10**9, bytes_accessed=0, transcendentals=0),
    )(*first, *arrays)


def after(value, *others):
    return lax.optimization_barrier((value,) + others)[0]


def shift(block, amount, ranks):
    return lax.ppermute(block, "seq", [(k, (k + amount) % ranks) for k in range(ranks)])


def around(blocks, sign, ranks):
    order = sorted(range(1, ranks), key=lambda r: abs(ranks - 2 * r))
    got = {r: shift(blocks[r - 1], sign * r, ranks) for r in order if blocks[r - 1] is not None}
    return [got.get(r) for r in range(1, ranks)]


def swap(block, mask):
    return lax.ppermute(block, "dp", [(k, k ^ mask) for k in range(8)])


def gather_dp(piece):
    place = lax.axis_index("dp")
    by_x, by_y, by_both = swap(piece, 2), swap(piece, 4), swap(piece, 6)
    near, beside, across = swap(piece, 1), swap(jnp.stack([by_x, by_y]), 1), swap(by_both, 1)
    whole = jnp.zeros((8,) + piece.shape, piece.dtype)
    for mask, part in (
        (0, piece), (1, near), (2, by_x), (4, by_y), (6, by_both),
        (3, beside[0]), (5, beside[1]), (7, across),
    ):
        whole = lax.dynamic_update_slice(whole, part[None], (place ^ mask, 0, 0))
    return whole.reshape(8 * piece.shape[0], piece.shape[1])


def scatter_dp(parts):
    parts = lax.all_to_all(parts.reshape(8, -1, parts.shape[1]), "dp", 0, 0, tiled=True)
    return jnp.sum(parts.astype(f32), axis=0).astype(bf16)


def per_device_heads(
    hidden_in,
    stretch_order,
    doc_lengths,
    attn_gain,
    attn_shift,
    feed_gain,
    feed_shift,
    qkv_weight,
    qkv_bias,
    out_weight,
    out_bias,
    up_weight,
    up_bias,
    down_weight,
    down_bias,
    grad_out,
):
    ranks, groups = lax.axis_size("seq"), lax.axis_size("dp")
    rank = lax.axis_index("seq")
    blocks_own, half, width = hidden_in.shape[1:]
    own = blocks_own * half
    count = ranks * own
    share = qkv_weight.shape[0]
    piece = share * ranks
    cols = width // ranks
    heads = cols // HD
    hidden = up_weight.shape[1] // ranks
    ratio = up_weight.shape[1] // width
    mixed_cols = 3 * cols
    edge = hidden + width + mixed_cols

    x_own = hidden_in.reshape(own, width)
    dy_own = grad_out.reshape(own, width)

    small = [attn_gain, attn_shift, feed_gain, feed_shift, out_bias, down_bias, qkv_bias, up_bias]
    shape = jax.ShapeDtypeStruct
    blocks = stretch_order.shape[0]
    slots = jnp.arange(blocks, dtype=jnp.int32)
    lies = jnp.sum(jnp.where(stretch_order[None] == slots[:, None], slots[None], 0), axis=1)
    lies = (rank - lies // blocks_own) % ranks * blocks_own + lies % blocks_own
    spot = jnp.concatenate([jnp.stack([rank, lax.axis_index("dp")]), lies])
    sent = (share, hidden + mixed_cols + 128)
    *packed, out_piece = call(
        functools.partial(pack_kernel, vectors=len(small), held=ratio * share),
        (1,),
        [(spot, SMEM)]
        + [(a, whole_block(a.shape)) for a in (up_weight, qkv_weight, out_weight, *small)],
        [(shape(sent, bf16), whole_block(sent))] * ranks
        + [(shape((piece, cols), bf16), whole_block((piece, cols)))],
    )
    spread = ranks * groups
    out_piece = lax.ppermute(
        out_piece, ("dp", "seq"),
        [(k, (k % groups) * ranks + k // groups) for k in range(spread)],
    )
    landed = packed[:1] + around(packed[1:], 1, ranks)
    x_next = shift(x_own, 1, ranks)
    landed[0] = after(landed[0], x_next)
    total_cols = edge + cols + 128
    (weight_piece,) = call(
        functools.partial(land_kernel, hidden=hidden),
        (1,),
        [(spot, SMEM)] + [(a, whole_block(a.shape)) for a in (*landed, down_weight, out_piece)],
        [(shape((piece, total_cols), bf16), whole_block((piece, total_cols)))],
    )
    weights = gather_dp(weight_piece)

    x_go = after(x_own, *landed)
    x_rest = around([None] + [x_go] * (ranks - 2), 1, ranks)[1:]
    x_all = jnp.concatenate([x_own, x_next] + x_rest)
    dy_go = after(dy_own, x_all)
    dy_got = around([dy_go] * (ranks - 1), 1, ranks)

    ends = jnp.cumsum(doc_lengths[0])[:-1]
    place = jnp.arange(count, dtype=jnp.int32)
    first_of = jnp.max(jnp.where(place[:, None] >= ends[None], ends[None], 0), axis=1)
    start = jnp.broadcast_to(first_of[None], (8, count))
    angle = frequencies()[:, None] * place.astype(f32)[None]
    cosine, sine = jnp.cos(angle), jnp.sin(angle)

    tile = lambda w: pl.BlockSpec((own, w), lambda t, *_: (t, 0))
    upright_tile = lambda n: pl.BlockSpec((n, own), lambda t, *_: (0, t))
    upright_all = lambda j: pl.BlockSpec((cols, count), lambda *_: (j, 0))
    column = lambda j: pl.BlockSpec((width, width), lambda *_: (0, j))
    angles = [(cosine, upright_tile(ROT // 2)), (sine, upright_tile(ROT // 2))]
    by_place = [
        pl.BlockSpec((half, width), lambda t, spot, k=k: (spot[2 + t * blocks_own + k], 0))
        for k in range(blocks_own)
    ]
    in_order = lambda array: [(array, spec) for spec in by_place]
    each = [(shape((own, width), bf16), whole_block((own, width)))] * ranks

    n1, n2, active, slope, fed, upright, rows, vec, out_own = call(
        functools.partial(front_kernel, ranks=ranks, ratio=ratio, parts=blocks_own),
        (ranks,),
        in_order(x_all)
        + [(weights, pl.BlockSpec((width, 128), lambda *_: (0, (edge + cols) // 128)))] + angles
        + [(weights, column(0)), (weights, column(1)), (weights, column(2))],
        [(shape((count, width), bf16), tile(width)), (shape((count, width), bf16), tile(width)),
         (shape((count, hidden), bf16), tile(hidden)), (shape((count, hidden), bf16), tile(hidden)),
         (shape((count, width), f32), tile(width)),
         (shape((mixed_cols, count), bf16), upright_tile(mixed_cols)),
         (shape((3 * heads, count, HD), bf16),
          pl.BlockSpec((3 * heads, own, HD), lambda t, *_: (0, t, 0))),
         (shape((8, width), f32), whole_block((8, width))),
         (shape((cols, width), bf16), whole_block((cols, width)))],
        [pltpu.VMEM((1, mixed_cols), f32)],
        cost=10,
        first=(spot,),
    )

    all_heads = lambda j: pl.BlockSpec((heads, count, HD), lambda *_: (j, 0, 0))
    soft_spec = pl.BlockSpec((heads, count, own), lambda t, *_: (0, 0, t))
    soft, inverse, heads_low, *part_out = call(
        functools.partial(attend_kernel, ranks=ranks, parts=blocks_own),
        (ranks,),
        [(start, upright_tile(8)), (rows, all_heads(1)), (upright, upright_tile(cols)),
         (upright, upright_all(2)), (fed, tile(width)), (out_own, whole_block((cols, width)))],
        [(shape((heads, count, count), bf16), soft_spec), (shape((8, count), f32), upright_tile(8)),
         (shape((cols, count), bf16), upright_tile(cols))] + each,
        cost=10,
        first=(spot,),
    )

    dy_all = jnp.concatenate([dy_own] + [after(block, heads_low) for block in dy_got])
    scaled, grads_feed, feed_sums = call(
        functools.partial(feed_back_kernel, ranks=ranks, parts=blocks_own),
        (ranks,),
        in_order(dy_all) + in_order(x_all)
        + [(dy_own, whole_block((own, width))), (active, tile(hidden)),
         (slope, tile(hidden)), (n2, tile(width)), (vec, whole_block((8, width))),
         (weights, column(0)), (weights, column(1)), (heads_low, upright_tile(cols))],
        [(shape((count, width), f32), tile(width)),
         (shape((width, edge - mixed_cols + cols), bf16),
          whole_block((width, edge - mixed_cols + cols))),
         (shape((8, width), f32), whole_block((8, width)))],
        [pltpu.VMEM((width, hidden), f32), pltpu.VMEM((hidden, width), f32),
         pltpu.VMEM((cols, width), f32)],
        cost=12,
        first=(spot,),
    )
    feed_part = scatter_dp(grads_feed)

    far = [r for r in range(1, ranks) if 2 * r == ranks]
    near = [r for r in range(1, ranks) if r not in far]
    out_parts = part_out[:1] + [shift(after(part_out[r], dy_all), -r, ranks) for r in near]
    heads_low = after(heads_low, scaled, *out_parts)
    far_parts = [shift(after(part_out[r], scaled), -r, ranks) for r in far]
    head_tile = pl.BlockSpec((heads, own, HD), lambda t, *_: (0, t, 0))
    gquery, gkey, gvalue = call(
        functools.partial(attend_back_kernel, ranks=ranks, parts=blocks_own),
        (ranks,),
        in_order(dy_all)
        + [(out_own, whole_block((cols, width))), (heads_low, upright_tile(cols)),
           (inverse, upright_tile(8)), (soft, soft_spec), (rows, all_heads(2)),
           (upright, upright_all(1)), (rows, head_tile)] + angles,
        [(shape((cols, count), f32), upright_tile(cols)),
         (shape((heads, count, HD), f32), whole_block((heads, count, HD))),
         (shape((heads, count, HD), f32), whole_block((heads, count, HD)))],
        cost=10,
        first=(spot,),
    )
    gquery = after(gquery, *far_parts)
    out_sum = sum(part.astype(f32) for part in out_parts + far_parts)
    hidden_out = (x_own.astype(f32) + vec[5:6] + out_sum).astype(bf16)

    mixed, attn_sums, attn_bias, *total = call(
        functools.partial(rear_kernel, ranks=ranks, parts=blocks_own),
        (ranks,),
        in_order(x_all) + [(gquery, upright_tile(cols)), (gkey, head_tile), (gvalue, head_tile)]
        + angles
        + [(scaled, tile(width)), (vec, whole_block((8, width))), (weights, column(2))],
        [(shape((count, mixed_cols), bf16), tile(mixed_cols)),
         (shape((8, width), f32), whole_block((8, width))),
         (shape((8, mixed_cols), f32), whole_block((8, mixed_cols)))] + each,
        cost=8,
        first=(spot,),
    )
    (grads_attn,) = call(
        functools.partial(weigh_kernel, ranks=ranks, ratio=ratio),
        (1,),
        [(a, whole_block(a.shape)) for a in (n1, mixed, attn_sums, attn_bias, feed_sums)],
        [(shape((width, mixed_cols + 128), bf16), whole_block((width, mixed_cols + 128)))],
        [pltpu.VMEM((spread, share, 128), f32)],
        cost=5,
        first=(spot,),
    )

    grad_parts = total[:1] + around(total[1:], -1, ranks)
    attn_part = scatter_dp(after(grads_attn, feed_part))
    home = [((k % groups) * ranks + k // groups, k) for k in range(spread)]
    proj_part = lax.ppermute(feed_part[:, hidden + width :], ("dp", "seq"), home)
    parts = jnp.concatenate([feed_part[:, :hidden], attn_part], axis=1)
    parts = parts.reshape(ranks, share, parts.shape[1])
    parts = [lax.dynamic_index_in_dim(parts, (rank + r) % ranks, 0, False) for r in range(ranks)]
    parts = parts[:1] + around([after(p, proj_part, *grad_parts) for p in parts[1:]], 1, ranks)
    dy = dy_own.astype(f32)
    grad = sum(part.astype(f32) for part in grad_parts)
    rows_own = x_own.astype(f32)
    centred = rows_own - jnp.mean(rows_own, axis=-1, keepdims=True)
    rstd = lax.rsqrt(jnp.mean(centred * centred, axis=-1, keepdims=True) + eps)
    hat = centred * rstd
    grad_in = dy + rstd * (
        grad
        - jnp.mean(grad, axis=-1, keepdims=True)
        - hat * jnp.mean(grad * hat, axis=-1, keepdims=True)
    )

    factor = 1.0 / math.sqrt(count * groups)
    down_part = feed_part[:, hidden : hidden + width]
    results = [(share, 3 * width), (share, ranks * hidden), (share, width), (piece, width)]
    results += [(share,)] * 5 + [(3 * share,), (ratio * share,)]
    qkv_own, up_own, proj_own, down_own, *small_own = call(
        functools.partial(finish_kernel, factor=factor, hidden=hidden),
        (1,),
        [(spot, SMEM)] + [(a, whole_block(a.shape)) for a in (*parts, down_part, proj_part)],
        [(shape(size, f32), whole_block(size)) for size in results],
    )
    return (
        hidden_out.reshape(hidden_in.shape),
        grad_in.astype(bf16).reshape(hidden_in.shape),
        *small_own[:4],
        qkv_own,
        small_own[5],
        proj_own,
        small_own[4],
        up_own,
        small_own[6],
        down_own,
        small_own[4],
    )


def per_device(hidden_in, *rest):
    heads = hidden_in.shape[-1] // HD
    fits = heads % lax.axis_size("seq") == 0 and lax.axis_size("dp") == 8
    return (per_device_heads if fits else per_device_split)(hidden_in, *rest)


def solution(mesh):
    in_specs = (
        P("dp", "seq", None, None),
        P(),
        P("dp", None),
        P(("dp", "seq")),
        P(("dp", "seq")),
        P(("dp", "seq")),
        P(("dp", "seq")),
        P(("dp", "seq"), None),
        P(("dp", "seq")),
        P(("dp", "seq"), None),
        P(("dp", "seq")),
        P(("dp", "seq"), None),
        P(("dp", "seq")),
        P(("dp", "seq"), None),
        P(("dp", "seq")),
        P("dp", "seq", None, None),
    )
    out_specs = (
        P("dp", "seq", None, None),
        P("dp", "seq", None, None),
        P(("dp", "seq")),
        P(("dp", "seq")),
        P(("dp", "seq")),
        P(("dp", "seq")),
        P(("dp", "seq"), None),
        P(("dp", "seq")),
        P(("dp", "seq"), None),
        P(("dp", "seq")),
        P(("dp", "seq"), None),
        P(("dp", "seq")),
        P(("dp", "seq"), None),
        P(("dp", "seq")),
    )
    return jax.shard_map(
        per_device, mesh=mesh, in_specs=in_specs, out_specs=out_specs, check_vma=False
    )
```

```python
import functools
import math

import jax
import jax.numpy as jnp
from jax import lax
from jax.experimental import pallas as pl
from jax.experimental.pallas import tpu as pltpu
from jax.sharding import PartitionSpec as P

HD = 64
ROT = 16


eps = 1e-05
masked = -1e30


def layer_norm(rows, gain, shift):
    mean = jnp.mean(rows, axis=-1, keepdims=True)
    centred = rows - mean
    spread = jnp.mean(centred * centred, axis=-1, keepdims=True)
    return centred * lax.rsqrt(spread + eps) * gain + shift


def frequencies():
    return jnp.power(10000.0, -2.0 * jnp.arange(ROT // 2, dtype=jnp.float32) / ROT)


def rotate(heads, cosine, sine):
    half_rot = ROT // 2
    first = heads[..., :half_rot]
    second = heads[..., half_rot:ROT]
    return jnp.concatenate(
        [first * cosine - second * sine, second * cosine + first * sine, heads[..., ROT:]], axis=-1
    )


def doc_ids(positions, ends):
    return jnp.sum((positions[None, :, None] >= ends[:, None, :]).astype(jnp.int32), axis=-1)


def times_transposed(left, right):
    return lax.dot_general(
        left, right, (((1,), (1,)), ((), ())), preferred_element_type=jnp.float32
    )


def inner_rows(left, right):
    return lax.dot_general(
        left, right, (((0,), (0,)), ((), ())), preferred_element_type=jnp.float32
    )


def per_device_split(
    hidden_in,
    stretch_order,
    doc_lengths,
    attn_gain,
    attn_shift,
    feed_gain,
    feed_shift,
    qkv_weight,
    qkv_bias,
    out_weight,
    out_bias,
    up_weight,
    up_bias,
    down_weight,
    down_bias,
    grad_out,
):
    whole = (
        lax.all_gather(attn_gain, ("dp", "seq"), axis=0, tiled=True),
        lax.all_gather(attn_shift, ("dp", "seq"), axis=0, tiled=True),
        lax.all_gather(feed_gain, ("dp", "seq"), axis=0, tiled=True),
        lax.all_gather(feed_shift, ("dp", "seq"), axis=0, tiled=True),
        lax.all_gather(qkv_weight, ("dp", "seq"), axis=0, tiled=True),
        lax.all_gather(qkv_bias, ("dp", "seq"), axis=0, tiled=True),
        lax.all_gather(out_weight, ("dp", "seq"), axis=0, tiled=True),
        lax.all_gather(out_bias, ("dp", "seq"), axis=0, tiled=True),
        lax.all_gather(up_weight, ("dp", "seq"), axis=0, tiled=True),
        lax.all_gather(up_bias, ("dp", "seq"), axis=0, tiled=True),
        lax.all_gather(down_weight, ("dp", "seq"), axis=0, tiled=True),
        lax.all_gather(down_bias, ("dp", "seq"), axis=0, tiled=True),
    )
    seqs, blocks_own, half, width = hidden_in.shape
    heads = width // HD
    hidden_units = whole[8].shape[1]
    ratio = hidden_units // width
    queries = blocks_own * half
    count = seqs * queries
    scale_qk = 1.0 / math.sqrt(HD)
    lane = lax.axis_index("seq")
    offsets = jnp.arange(half, dtype=jnp.int32)
    own_blocks = lax.dynamic_slice_in_dim(stretch_order, lane * blocks_own, blocks_own)
    own_pos = (own_blocks[:, None] * half + offsets[None, :]).reshape(queries)
    ends = jnp.cumsum(doc_lengths, axis=1)[:, :-1]
    own_doc = doc_ids(own_pos, ends)
    angle = own_pos.astype(jnp.float32)[:, None] * frequencies()[None, :]
    cosine = jnp.cos(angle)[None, :, None, :]
    sine = jnp.sin(angle)[None, :, None, :]

    def allowed_of(key_pos, key_doc):
        causal = key_pos[None, None, None, :] <= own_pos[None, None, :, None]
        same = key_doc[:, None, None, :] == own_doc[:, None, :, None]
        return causal & same

    rows = hidden_in.astype(jnp.float32).reshape(count, width)
    normed_first, pull_first = jax.vjp(
        layer_norm, rows, whole[0].astype(jnp.float32), whole[1].astype(jnp.float32)
    )
    normed_second, pull_second = jax.vjp(
        layer_norm, rows, whole[2].astype(jnp.float32), whole[3].astype(jnp.float32)
    )
    first_low = normed_first.astype(jnp.bfloat16)
    second_low = normed_second.astype(jnp.bfloat16)
    mixed = jnp.dot(first_low, whole[4], preferred_element_type=jnp.float32) + whole[5].astype(
        jnp.float32
    )
    mixed = mixed.reshape(seqs, queries, 3, heads, HD)
    query = rotate(mixed[:, :, 0], cosine, sine).astype(jnp.bfloat16)
    key_own = (
        rotate(mixed[:, :, 1], cosine, sine)
        .astype(jnp.bfloat16)
        .reshape(seqs, blocks_own, half, width)
    )
    value_own = mixed[:, :, 2].astype(jnp.bfloat16).reshape(seqs, blocks_own, half, width)
    top = jnp.full((seqs, heads, queries), masked, jnp.float32)
    key_piece = lax.all_gather(key_own, "seq", axis=1, tiled=True)
    value_piece = lax.all_gather(value_own, "seq", axis=1, tiled=True)
    blocks = key_piece.shape[1]
    key_pos = (stretch_order[:, None] * half + offsets[None, :]).reshape(blocks * half)
    allowed = allowed_of(key_pos, doc_ids(key_pos, ends))
    keys = key_piece.reshape(seqs, blocks * half, heads, HD)
    values = value_piece.reshape(seqs, blocks * half, heads, HD)
    scores = (
        jnp.einsum("sqhd,skhd->shqk", query, keys, preferred_element_type=jnp.float32) * scale_qk
    )
    scores = jnp.where(allowed, scores, masked)
    new_top = jnp.maximum(top, jnp.max(scores, axis=-1))
    weights = jnp.where(allowed, jnp.exp(scores - new_top[..., None]), 0.0)
    total = jnp.sum(weights, axis=-1)
    accum = jnp.einsum(
        "shqk,skhd->shqd", weights.astype(jnp.bfloat16), values, preferred_element_type=jnp.float32
    )
    top, total, accum = (new_top, total, accum)
    logsum = top + jnp.log(total)
    heads_rows = jnp.transpose(accum / total[..., None], (0, 2, 1, 3))
    heads_low = heads_rows.reshape(count, width).astype(jnp.bfloat16)
    attended = jnp.dot(heads_low, whole[6], preferred_element_type=jnp.float32) + whole[7].astype(
        jnp.float32
    )
    inner = jnp.dot(second_low, whole[8], preferred_element_type=jnp.float32) + whole[9].astype(
        jnp.float32
    )
    active, pull_gelu = jax.vjp(lambda v: jax.nn.gelu(v, approximate=False), inner)
    active_low = active.astype(jnp.bfloat16)
    fed = jnp.dot(active_low, whole[10], preferred_element_type=jnp.float32) + whole[11].astype(
        jnp.float32
    )
    hidden_out = (rows + attended + fed).astype(jnp.bfloat16).reshape(hidden_in.shape)
    params_back = (
        lax.all_gather(attn_gain, ("dp", "seq"), axis=0, tiled=True),
        lax.all_gather(attn_shift, ("dp", "seq"), axis=0, tiled=True),
        lax.all_gather(feed_gain, ("dp", "seq"), axis=0, tiled=True),
        lax.all_gather(feed_shift, ("dp", "seq"), axis=0, tiled=True),
        lax.all_gather(qkv_weight, ("dp", "seq"), axis=0, tiled=True),
        lax.all_gather(qkv_bias, ("dp", "seq"), axis=0, tiled=True),
        lax.all_gather(out_weight, ("dp", "seq"), axis=0, tiled=True),
        lax.all_gather(out_bias, ("dp", "seq"), axis=0, tiled=True),
        lax.all_gather(up_weight, ("dp", "seq"), axis=0, tiled=True),
        lax.all_gather(up_bias, ("dp", "seq"), axis=0, tiled=True),
        lax.all_gather(down_weight, ("dp", "seq"), axis=0, tiled=True),
        lax.all_gather(down_bias, ("dp", "seq"), axis=0, tiled=True),
    )
    upstream_low = grad_out.reshape(count, width)
    upstream = upstream_low.astype(jnp.float32)
    grad_bias_out = jnp.sum(upstream, axis=0)
    grad_active = times_transposed(upstream_low, params_back[10])
    (grad_inner,) = pull_gelu(grad_active)
    inner_low = grad_inner.astype(jnp.bfloat16)
    grad_up_bias = jnp.sum(grad_inner, axis=0)
    grad_second = times_transposed(inner_low, params_back[8])
    grad_heads = times_transposed(upstream_low, params_back[6])
    heads_grad_low = grad_heads.astype(jnp.bfloat16).reshape(seqs, queries, heads, HD)
    delta = jnp.transpose(
        jnp.sum(heads_grad_low.astype(jnp.float32) * heads_rows, axis=-1), (0, 2, 1)
    )
    key_all, value_all = (
        lax.all_gather(key_own, "seq", axis=1, tiled=True),
        lax.all_gather(value_own, "seq", axis=1, tiled=True),
    )
    blocks_all = key_all.shape[1]

    def backstep(grad_query, block):
        keys = lax.dynamic_slice_in_dim(key_all, block, 1, axis=1).reshape(seqs, half, heads, HD)
        values = lax.dynamic_slice_in_dim(value_all, block, 1, axis=1).reshape(
            seqs, half, heads, HD
        )
        key_pos = lax.dynamic_slice_in_dim(stretch_order, block, 1) * half + offsets
        allowed = allowed_of(key_pos, doc_ids(key_pos, ends))
        scores = (
            jnp.einsum("sqhd,skhd->shqk", query, keys, preferred_element_type=jnp.float32)
            * scale_qk
        )
        probs = jnp.where(allowed, jnp.exp(scores - logsum[..., None]), 0.0)
        grad_probs = jnp.einsum(
            "sqhd,skhd->shqk", heads_grad_low, values, preferred_element_type=jnp.float32
        )
        grad_scores = (probs * (grad_probs - delta[..., None]) * scale_qk).astype(jnp.bfloat16)
        grad_query = grad_query + jnp.einsum(
            "shqk,skhd->sqhd", grad_scores, keys, preferred_element_type=jnp.float32
        )
        key_term = jnp.einsum(
            "shqk,sqhd->skhd", grad_scores, query, preferred_element_type=jnp.float32
        )
        value_term = jnp.einsum(
            "shqk,sqhd->skhd",
            probs.astype(jnp.bfloat16),
            heads_grad_low,
            preferred_element_type=jnp.float32,
        )
        return (
            grad_query,
            (key_term.reshape(seqs, half, width), value_term.reshape(seqs, half, width)),
        )

    grad_query, (grad_keys, grad_values) = lax.scan(
        backstep,
        jnp.zeros((seqs, queries, heads, HD), jnp.float32),
        jnp.arange(blocks_all, dtype=jnp.int32),
    )
    key_part, value_part = (
        lax.psum_scatter(
            grad_keys.astype(jnp.bfloat16), "seq", scatter_dimension=0, tiled=True
        ).astype(jnp.float32),
        lax.psum_scatter(
            grad_values.astype(jnp.bfloat16), "seq", scatter_dimension=0, tiled=True
        ).astype(jnp.float32),
    )
    key_sum = jnp.transpose(key_part, (1, 0, 2, 3))
    value_sum = jnp.transpose(value_part, (1, 0, 2, 3))
    query_back = rotate(grad_query, cosine, -sine).reshape(count, width)
    key_back = rotate(key_sum.reshape(seqs, queries, heads, HD), cosine, -sine).reshape(
        count, width
    )
    grad_mixed = jnp.concatenate([query_back, key_back, value_sum.reshape(count, width)], axis=1)
    mixed_low = grad_mixed.astype(jnp.bfloat16)
    grad_qkv_bias = jnp.sum(grad_mixed, axis=0)
    grad_first = times_transposed(mixed_low, params_back[4])
    rows_first, gain_first, shift_first = pull_first(grad_first)
    rows_second, gain_second, shift_second = pull_second(grad_second)
    grad_in = (upstream + rows_first + rows_second).astype(jnp.bfloat16).reshape(hidden_in.shape)
    factor = 1.0 / math.sqrt(count * lax.axis_size("dp") * lax.axis_size("seq"))
    small_columns = jnp.stack(
        [gain_first, shift_first, gain_second, shift_second, grad_bias_out], axis=1
    )
    qkv_bias_rows = grad_qkv_bias.reshape(width, 3)
    up_bias_rows = grad_up_bias.reshape(width, ratio)
    part_qkv = inner_rows(first_low, mixed_low)
    part_out = inner_rows(heads_low, upstream_low)
    part_up = inner_rows(second_low, inner_low)
    part_down = inner_rows(active_low, upstream_low).reshape(
        lax.axis_size(("dp", "seq")) * qkv_weight.shape[0], ratio * width
    )
    owned = lax.psum_scatter(
        jnp.concatenate(
            [part_qkv, part_out, part_up, part_down, small_columns, qkv_bias_rows, up_bias_rows],
            axis=1,
        )
        * factor,
        ("dp", "seq"),
        scatter_dimension=0,
        tiled=True,
    )
    own_rows = owned.shape[0]
    edge_out = 3 * width
    edge_up = edge_out + width
    edge_down = edge_up + hidden_units
    edge_small = edge_down + hidden_units
    edge_qkvb = edge_small + 5
    edge_upb = edge_qkvb + 3
    grad_qkv_own = owned[:, :edge_out]
    grad_out_own = owned[:, edge_out:edge_up]
    grad_up_own = owned[:, edge_up:edge_down]
    grad_down_own = owned[:, edge_down:edge_small].reshape(own_rows * ratio, width)
    grad_bias_own = owned[:, edge_small + 4]
    grad_qkvb_own = owned[:, edge_qkvb:edge_upb].reshape(own_rows * 3)
    grad_upb_own = owned[:, edge_upb : edge_upb + ratio].reshape(own_rows * ratio)
    return (
        hidden_out,
        grad_in,
        owned[:, edge_small],
        owned[:, edge_small + 1],
        owned[:, edge_small + 2],
        owned[:, edge_small + 3],
        grad_qkv_own,
        grad_qkvb_own,
        grad_out_own,
        grad_bias_own,
        grad_up_own,
        grad_upb_own,
        grad_down_own,
        grad_bias_own,
    )


f32 = jnp.float32
bf16 = jnp.bfloat16


def whole_block(shape):
    return pl.BlockSpec(shape, lambda *_: (0,) * len(shape))


def normalise(rows):
    centred = rows - jnp.mean(rows, axis=-1, keepdims=True)
    spread = jnp.mean(centred * centred, axis=-1, keepdims=True)
    return centred * lax.rsqrt(spread + eps)


def turn(upright, cosine, sine):
    half_rot = ROT // 2
    first = upright[:half_rot]
    second = upright[half_rot:ROT]
    return [first * cosine - second * sine, second * cosine + first * sine, upright[ROT:]]


def product(left, right, left_dim=1, right_dim=0):
    return lax.dot_general(
        left, right, (((left_dim,), (right_dim,)), ((), ())), preferred_element_type=f32
    )


def places(owners, per, base, index):
    lanes = lax.broadcasted_iota(jnp.int32, (LANES, index.shape[1]), 0)
    rows = lax.broadcasted_iota(jnp.int32, (owners, index.shape[1]), 0)
    return rows == index // per, (lanes == base + index % per).astype(bf16)


def vector_maps(rank, share, ranks, cols, hidden, ratio):
    line = lambda n: lax.broadcasted_iota(jnp.int32, (1, n), 1)
    width = ranks * cols
    part = line(3 * cols)
    maps = [(share, j * share, line(width)) for j in range(6)]
    maps.append((3 * share, 6 * share, part // cols * width + rank * cols + part % cols))
    held = ratio * share
    unit = line(hidden)
    maps.append((held, 9 * share, (unit // held * ranks + rank) * held + unit % held))
    return maps


def pack_kernel(rank_ref, up_ref, qkv_ref, out_ref, *refs, vectors, held):
    outs = refs[vectors:]
    ranks = len(outs) - 1
    rank = rank_ref[0]
    up, qkv = up_ref[...], qkv_ref[...]
    width = qkv.shape[1] // 3
    cols = width // ranks
    share = up.shape[0]
    line = jnp.concatenate([ref[...][None].astype(f32) for ref in refs[:vectors]], axis=1)
    line = jnp.pad(line, ((0, 0), (0, LANES - line.shape[1])))
    lines = [line[:, j : j + 128] for j in range(0, LANES, 128)]
    small = jnp.concatenate(lines + [jnp.zeros((share - len(lines), 128), f32)]).astype(bf16)
    for t in range(ranks):
        block = jnp.concatenate(
            [up[:, at : at + held] for at in range(t * held, up.shape[1], ranks * held)]
            + [qkv[:, j * width + t * cols : j * width + (t + 1) * cols] for j in range(3)]
            + [small],
            axis=1,
        )
        for r in range(ranks):

            @pl.when((rank + r) % ranks == t)
            def _():
                outs[r][...] = block

    out = out_ref[...].astype(f32)
    flat = jnp.concatenate([out[:, j * cols : (j + 1) * cols] for j in range(ranks)], axis=0)
    outs[-1][...] = flat.astype(bf16)


def land_kernel(rank_ref, *refs, hidden):
    ranks = len(refs) - 3
    rank = rank_ref[0]
    blocks = [ref[...].astype(f32) for ref in refs[:ranks]]
    ordered = []
    for t in range(ranks):
        picked = blocks[0]
        for r in range(1, ranks):
            picked = jnp.where((rank - r + ranks) % ranks == t, blocks[r], picked)
        ordered.append(picked)
    landed = jnp.concatenate(ordered, axis=0).astype(bf16)
    tail = landed.shape[1] - 128
    refs[-1][...] = jnp.concatenate(
        [landed[:, :hidden], refs[ranks][...], landed[:, hidden:tail], refs[ranks + 1][...],
         landed[:, tail:]], axis=1,
    )


def join(refs):
    return jnp.concatenate([ref[...] for ref in refs], axis=0)


def store_blocks(refs, spot_ref, step, tile, parts):
    half = tile.shape[0] // parts
    for k in range(parts):
        block = tile[k * half : (k + 1) * half]
        where = spot_ref[2 + step * parts + k]
        for r, ref in enumerate(refs):
            for slot in range(parts):

                @pl.when(where == r * parts + slot)
                def _():
                    ref[slot * half : (slot + 1) * half, :] = block


def front_kernel(rank_ref, *refs, ranks, ratio, parts):
    x_refs, (small_ref, cos_ref, sin_ref, up_ref, down_ref, attn_ref) = refs[:parts], refs[parts:-10]
    n1_ref, n2_ref, act_ref, slope_ref, fed_ref, upright_ref, rows_ref = refs[-10:-3]
    vec_ref, own_out_ref, bias_ref = refs[-3:]
    width, part3 = n1_ref.shape[1], upright_ref.shape[0]
    cols, hidden = part3 // 3, act_ref.shape[1]
    owners = ranks * 8
    share = width // owners

    @pl.when(pl.program_id(0) == 0)
    def _():
        table = small_ref[...].astype(f32).reshape(owners, share, 128)
        table = jnp.concatenate([table[:, j, :] for j in range(LANES // 128)], axis=1).astype(bf16)
        vectors = []
        for per, base, index in vector_maps(rank_ref[0], share, ranks, cols, hidden, ratio):
            rows, lanes = places(owners, per, base, index)
            spread = jnp.where(rows, product(table, lanes), 0.0)
            vectors.append(jnp.sum(spread, axis=0, keepdims=True))
        bias_ref[...] = vectors[6]
        vec_ref[...] = jnp.concatenate(
            vectors[:4] + [vectors[7], vectors[4] + vectors[5], jnp.zeros((2, width), f32)], axis=0
        )
        flat = attn_ref[:, part3:].astype(f32)
        rebuilt = []
        for d in range(8):
            start = d * share * ranks
            rebuilt.append(
                jnp.concatenate(
                    [flat[start + j * share : start + (j + 1) * share] for j in range(ranks)], axis=1
                )
            )
        own_out_ref[...] = jnp.concatenate(rebuilt, axis=0).astype(bf16)

    hat = normalise(join(x_refs).astype(f32))
    vec = vec_ref[...]
    n1 = (hat * vec[0:1] + vec[1:2]).astype(bf16)
    n2 = (hat * vec[2:3] + vec[3:4]).astype(bf16)
    n1_ref[...] = n1
    n2_ref[...] = n2
    width = upright_ref.shape[0]
    mixed = product(n1, attn_ref[:, :width]) + bias_ref[...]
    upright = mixed.T
    cosine, sine = cos_ref[...], sin_ref[...]
    part = width // 3
    pieces = []
    for start in range(0, part, HD):
        pieces += [v * HD**-0.5 for v in turn(upright[start : start + HD], cosine, sine)]
    for start in range(part, 2 * part, HD):
        pieces += turn(upright[start : start + HD], cosine, sine)
    upright = jnp.concatenate(pieces + [upright[2 * part :]], axis=0)
    upright_ref[...] = upright.astype(bf16)
    mixed = upright.T.astype(bf16)
    for j in range(width // HD):
        rows_ref[j] = mixed[:, j * HD : (j + 1) * HD]
    inner = product(n2, up_ref[...]) + vec[4:5]
    phi = 0.5 + 0.5 * lax.erf(inner * math.sqrt(0.5))
    active = (inner * phi).astype(bf16)
    act_ref[...] = active
    bell = jnp.exp(inner * inner * -0.5) * (1.0 / math.sqrt(2.0 * math.pi))
    slope_ref[...] = (phi + inner * bell).astype(bf16)
    fed_ref[...] = product(active, down_ref[...])


def attend_kernel(spot_ref, *refs, ranks, parts):
    start_ref, key_ref, query_ref, value_ref, fed_ref, out_ref, soft_ref, inv_ref, heads_ref = refs[:9]
    step, own = pl.program_id(0), query_ref.shape[1]

    def tile(at):
        held = own * (at + 1)
        place = lax.broadcasted_iota(jnp.int32, (held, own), 0)
        asks = lax.broadcasted_iota(jnp.int32, (held, own), 1) + at * own
        bias = jnp.where((place <= asks) & (place >= start_ref[0:1]), 0.0, masked)
        for head in range(key_ref.shape[0]):
            spot = slice(head * HD, (head + 1) * HD)
            scores = product(key_ref[head, :held], query_ref[spot, :]) + bias
            weights = jnp.exp(scores - jnp.max(scores, axis=0, keepdims=True))
            inverse = 1.0 / jnp.sum(weights, axis=0, keepdims=True)
            soft = weights.astype(bf16)
            soft_ref[head, :held] = soft
            inv_ref[head : head + 1] = inverse
            heads_ref[spot, :] = (product(value_ref[spot, :held], soft) * inverse).astype(bf16)

    for at in range(ranks):
        pl.when(step == at)(functools.partial(tile, at))
    part = (fed_ref[...] + product(heads_ref[...], out_ref[...], 0, 0)).astype(bf16)
    store_blocks(refs[9:], spot_ref, step, part, parts)


def feed_back_kernel(spot_ref, *refs, ranks, parts):
    dy_refs, x_refs, refs = refs[:parts], refs[parts : 2 * parts], refs[2 * parts :]
    own_ref, act_ref, slope_ref, n2_ref, vec_ref, up_ref, down_ref, heads_ref = refs[:8]
    scaled_ref, grads_ref, sums_ref, acc_up, acc_down, acc_out = refs[8:]
    step = pl.program_id(0)

    @pl.when(step == 0)
    def _():
        acc_up[...] = jnp.zeros_like(acc_up)
        acc_down[...] = jnp.zeros_like(acc_down)
        acc_out[...] = jnp.zeros_like(acc_out)
        sums_ref[...] = jnp.zeros_like(sums_ref)
        sums_ref[3:4] = jnp.sum(own_ref[...].astype(f32), axis=0, keepdims=True)

    dy = join(dy_refs)
    grad_inner = product(dy, down_ref[...], 1, 1) * slope_ref[...].astype(f32)
    low = grad_inner.astype(bf16)
    grad = product(low, up_ref[...], 1, 1)
    hat = normalise(join(x_refs).astype(f32))
    scaled_ref[...] = (grad * vec_ref[2:3]).astype(bf16)
    sums_ref[0:1] += jnp.sum(grad * hat, axis=0, keepdims=True)
    sums_ref[1:2] += jnp.sum(grad, axis=0, keepdims=True)
    sums_ref[2:3] += jnp.sum(grad_inner, axis=0, keepdims=True)
    acc_up[...] += product(n2_ref[...], low, 0, 0)
    acc_down[...] += product(act_ref[...], dy, 0, 0)
    acc_out[...] += product(heads_ref[...], dy)

    @pl.when(step == pl.num_programs(0) - 1)
    def _():
        cols = acc_out.shape[0]
        share = cols // 8
        flat = []
        for d in range(8):
            rows = acc_out[d * share : (d + 1) * share]
            flat += [rows[:, j * cols : (j + 1) * cols] for j in range(ranks)]
        flat = jnp.concatenate(flat, axis=0)
        edge = acc_up.shape[1]
        grads_ref[:, :edge] = acc_up[...].astype(bf16)
        grads_ref[:, edge : edge + acc_down.shape[1]] = acc_down[...].astype(bf16)
        grads_ref[:, edge + acc_down.shape[1] :] = flat.astype(bf16)


def attend_back_kernel(spot_ref, *refs, ranks, parts):
    dy_refs, refs = refs[:parts], refs[parts:]
    out_ref, heads_ref, inv_ref, soft_ref, value_ref, key_ref, query_ref, cos_ref, sin_ref = refs[:9]
    gquery_ref, gkey_ref, gvalue_ref = refs[9:]
    step, own = pl.program_id(0), cos_ref.shape[1]

    @pl.when(step == 0)
    def _():
        gkey_ref[...] = jnp.zeros_like(gkey_ref)
        gvalue_ref[...] = jnp.zeros_like(gvalue_ref)

    lifted_all = product(out_ref[...], join(dy_refs), 1, 1).astype(bf16).astype(f32)

    def tile(at):
        held = own * (at + 1)
        for head in range(gkey_ref.shape[0]):
            spot = slice(head * HD, (head + 1) * HD)
            lifted = lifted_all[spot] * inv_ref[head : head + 1]
            delta = jnp.sum(lifted * heads_ref[spot, :].astype(f32), axis=0, keepdims=True)
            lifted_rows = lifted.T.astype(bf16)
            soft = soft_ref[head, :held]
            grad_soft = product(value_ref[head, :held], lifted.astype(bf16))
            grad_scores = (soft.astype(f32) * (grad_soft - delta)).astype(bf16)
            gvalue_ref[head, :held] += product(soft, lifted_rows)
            gkey_ref[head, :held] += product(grad_scores, query_ref[head])
            back = product(key_ref[spot, :held], grad_scores) * HD**-0.5
            gquery_ref[spot, :] = jnp.concatenate(turn(back, cos_ref[...], -sin_ref[...]), axis=0)

    for at in range(ranks):
        pl.when(step == at)(functools.partial(tile, at))


def rear_kernel(spot_ref, *refs, ranks, parts):
    x_refs, refs = refs[:parts], refs[parts:]
    gquery_ref, gkey_ref, gvalue_ref, cos_ref, sin_ref, scaled_ref, vec_ref, attn_ref = refs[:8]
    mixed_ref, sums_ref, gbias_ref = refs[8:11]
    step = pl.program_id(0)

    @pl.when(step == 0)
    def _():
        sums_ref[...] = jnp.zeros_like(sums_ref)
        gbias_ref[...] = jnp.zeros_like(gbias_ref)

    cosine, sine = cos_ref[...], sin_ref[...]
    pieces = [gquery_ref[...]]
    for j in range(gkey_ref.shape[0]):
        pieces += turn(gkey_ref[j].T, cosine, -sine)
    pieces += [gvalue_ref[j].T for j in range(gvalue_ref.shape[0])]
    mixed = jnp.concatenate(pieces, axis=0).T
    gbias_ref[0:1] += jnp.sum(mixed, axis=0, keepdims=True)
    low = mixed.astype(bf16)
    mixed_ref[...] = low
    grad = product(low, attn_ref[:, : low.shape[1]], 1, 1)
    hat = normalise(join(x_refs).astype(f32))
    total = (grad * vec_ref[0:1] + scaled_ref[...].astype(f32)).astype(bf16)
    store_blocks(refs[11:], spot_ref, step, total, parts)
    sums_ref[0:1] += jnp.sum(grad * hat, axis=0, keepdims=True)
    sums_ref[1:2] += jnp.sum(grad, axis=0, keepdims=True)


def weigh_kernel(
    spot_ref, n1_ref, mixed_ref, sums_ref, gbias_ref, feed_ref, grads_ref, small_ref, *, ranks, ratio
):
    acc = product(n1_ref[...], mixed_ref[...], 0, 0)
    width, part3 = acc.shape
    cols, owners = part3 // 3, small_ref.shape[0]
    share = width // owners
    feed = feed_ref[...]
    vectors = [sums_ref[0:1], sums_ref[1:2], feed[0:1], feed[1:2], feed[3:4], None]
    vectors += [gbias_ref[0:1], feed[2:3]]
    maps = vector_maps(spot_ref[0], share, ranks, cols, feed.shape[1], ratio)
    table = jnp.zeros((owners, LANES), f32)
    for vector, (per, base, index) in zip(vectors, maps):
        if vector is not None:
            rows, lanes = places(owners, per, base, index)
            table += product(jnp.where(rows, vector, 0.0).astype(bf16), lanes, 1, 1)
    small_ref[...] = jnp.zeros_like(small_ref)
    for j in range(LANES // 128):
        small_ref[:, j, :] = table[:, j * 128 : (j + 1) * 128]
    small = small_ref[...].reshape(width, 128)
    grads_ref[...] = jnp.concatenate([acc, small], axis=1).astype(bf16)


def finish_kernel(
    rank_ref, *refs, factor, hidden,
):
    qkv_ref, up_ref, proj_ref, down_ref, *small_refs = refs[-12:]
    down_in, proj_in, refs = refs[-14], refs[-13], refs[:-14]
    ranks, rank = len(refs), rank_ref[0]
    blocks = [ref[...].astype(f32) * factor for ref in refs]
    share, width = proj_ref.shape
    cols = width // ranks
    small = jnp.zeros((share, 128), f32)
    for t in range(ranks):
        picked = blocks[0]
        for r in range(1, ranks):
            picked = jnp.where((rank - r + ranks) % ranks == t, blocks[r], picked)
        for at in range(0, hidden, down_ref.shape[0]):
            where = at * ranks + t * down_ref.shape[0]
            up_ref[:, where : where + down_ref.shape[0]] = picked[:, at : at + down_ref.shape[0]]
        for j in range(3):
            at = j * width + t * cols
            qkv_ref[:, at : at + cols] = picked[:, hidden + j * cols : hidden + (j + 1) * cols]
        small += picked[:, hidden + 3 * cols :]
    down_ref[...] = down_in[...].astype(f32) * factor
    rows = proj_in[...].astype(f32) * factor
    proj_ref[...] = jnp.concatenate(
        [rows[j * share : (j + 1) * share] for j in range(ranks)], axis=1
    )
    line = jnp.concatenate([small[j : j + 1] for j in range(LANES // 128)], axis=1)
    at = 0
    for j, ref in enumerate(small_refs):
        at -= share if j == 5 else 0
        at += share if j == 6 else 0
        ref[...] = line[0, at : at + ref.shape[0]]
        at += ref.shape[0]


LANES = 384
VMEM = 56 * 1024 * 1024


SMEM = pl.BlockSpec(memory_space=pltpu.SMEM)


def call(kernel, grid, ins, outs, scratch=(), cost=1, first=()):
    arrays, in_specs = zip(*ins)
    shapes, out_specs = zip(*outs)
    return pl.pallas_call(
        kernel,
        grid_spec=pltpu.PrefetchScalarGridSpec(
            num_scalar_prefetch=len(first),
            grid=grid,
            in_specs=list(in_specs),
            out_specs=list(out_specs),
            scratch_shapes=list(scratch),
        ),
        out_shape=list(shapes),
        compiler_params=pltpu.CompilerParams(vmem_limit_bytes=VMEM),
        cost_estimate=pl.CostEstimate(flops=cost * 10**9, bytes_accessed=0, transcendentals=0),
    )(*first, *arrays)


def after(value, *others):
    return lax.optimization_barrier((value,) + others)[0]


def shift(block, amount, ranks):
    return lax.ppermute(block, "seq", [(k, (k + amount) % ranks) for k in range(ranks)])


def around(blocks, sign, ranks):
    order = sorted(range(1, ranks), key=lambda r: abs(ranks - 2 * r))
    got = {r: shift(blocks[r - 1], sign * r, ranks) for r in order if blocks[r - 1] is not None}
    return [got.get(r) for r in range(1, ranks)]


def swap(block, mask):
    return lax.ppermute(block, "dp", [(k, k ^ mask) for k in range(8)])


def gather_dp(piece):
    place = lax.axis_index("dp")
    by_x, by_y, by_both = swap(piece, 2), swap(piece, 4), swap(piece, 6)
    near, beside, across = swap(piece, 1), swap(jnp.stack([by_x, by_y]), 1), swap(by_both, 1)
    whole = jnp.zeros((8,) + piece.shape, piece.dtype)
    for mask, part in (
        (0, piece), (1, near), (2, by_x), (4, by_y), (6, by_both),
        (3, beside[0]), (5, beside[1]), (7, across),
    ):
        whole = lax.dynamic_update_slice(whole, part[None], (place ^ mask, 0, 0))
    return whole.reshape(8 * piece.shape[0], piece.shape[1])


def scatter_dp(parts):
    parts = lax.all_to_all(parts.reshape(8, -1, parts.shape[1]), "dp", 0, 0, tiled=True)
    return jnp.sum(parts.astype(f32), axis=0).astype(bf16)


def per_device_heads(
    hidden_in,
    stretch_order,
    doc_lengths,
    attn_gain,
    attn_shift,
    feed_gain,
    feed_shift,
    qkv_weight,
    qkv_bias,
    out_weight,
    out_bias,
    up_weight,
    up_bias,
    down_weight,
    down_bias,
    grad_out,
):
    ranks, groups = lax.axis_size("seq"), lax.axis_size("dp")
    rank = lax.axis_index("seq")
    blocks_own, half, width = hidden_in.shape[1:]
    own = blocks_own * half
    count = ranks * own
    share = qkv_weight.shape[0]
    piece = share * ranks
    cols = width // ranks
    heads = cols // HD
    hidden = up_weight.shape[1] // ranks
    ratio = up_weight.shape[1] // width
    mixed_cols = 3 * cols
    edge = hidden + width + mixed_cols

    x_own = hidden_in.reshape(own, width)
    dy_own = grad_out.reshape(own, width)

    small = [attn_gain, attn_shift, feed_gain, feed_shift, out_bias, down_bias, qkv_bias, up_bias]
    shape = jax.ShapeDtypeStruct
    blocks = stretch_order.shape[0]
    slots = jnp.arange(blocks, dtype=jnp.int32)
    lies = jnp.sum(jnp.where(stretch_order[None] == slots[:, None], slots[None], 0), axis=1)
    lies = (rank - lies // blocks_own) % ranks * blocks_own + lies % blocks_own
    spot = jnp.concatenate([jnp.stack([rank, lax.axis_index("dp")]), lies])
    sent = (share, hidden + mixed_cols + 128)
    *packed, out_piece = call(
        functools.partial(pack_kernel, vectors=len(small), held=ratio * share),
        (1,),
        [(spot, SMEM)]
        + [(a, whole_block(a.shape)) for a in (up_weight, qkv_weight, out_weight, *small)],
        [(shape(sent, bf16), whole_block(sent))] * ranks
        + [(shape((piece, cols), bf16), whole_block((piece, cols)))],
    )
    spread = ranks * groups
    out_piece = lax.ppermute(
        out_piece, ("dp", "seq"),
        [(k, (k % groups) * ranks + k // groups) for k in range(spread)],
    )
    landed = packed[:1] + around(packed[1:], 1, ranks)
    x_next = shift(x_own, 1, ranks)
    landed[0] = after(landed[0], x_next)
    total_cols = edge + cols + 128
    (weight_piece,) = call(
        functools.partial(land_kernel, hidden=hidden),
        (1,),
        [(spot, SMEM)] + [(a, whole_block(a.shape)) for a in (*landed, down_weight, out_piece)],
        [(shape((piece, total_cols), bf16), whole_block((piece, total_cols)))],
    )
    weights = gather_dp(weight_piece)

    x_go = after(x_own, *landed)
    x_rest = around([None] + [x_go] * (ranks - 2), 1, ranks)[1:]
    x_all = jnp.concatenate([x_own] + [after(block, weights) for block in (x_next, *x_rest)])
    dy_go = after(dy_own, x_all)
    dy_got = around([dy_go] * (ranks - 1), 1, ranks)

    ends = jnp.cumsum(doc_lengths[0])[:-1]
    place = jnp.arange(count, dtype=jnp.int32)
    first_of = jnp.max(jnp.where(place[:, None] >= ends[None], ends[None], 0), axis=1)
    start = jnp.broadcast_to(first_of[None], (8, count))
    angle = frequencies()[:, None] * place.astype(f32)[None]
    cosine, sine = jnp.cos(angle), jnp.sin(angle)

    tile = lambda w: pl.BlockSpec((own, w), lambda t, *_: (t, 0))
    upright_tile = lambda n: pl.BlockSpec((n, own), lambda t, *_: (0, t))
    upright_all = lambda j: pl.BlockSpec((cols, count), lambda *_: (j, 0))
    column = lambda j: pl.BlockSpec((width, width), lambda *_: (0, j))
    angles = [(cosine, upright_tile(ROT // 2)), (sine, upright_tile(ROT // 2))]
    by_place = [
        pl.BlockSpec((half, width), lambda t, spot, k=k: (spot[2 + t * blocks_own + k], 0))
        for k in range(blocks_own)
    ]
    in_order = lambda array: [(array, spec) for spec in by_place]
    each = [(shape((own, width), bf16), whole_block((own, width)))] * ranks

    n1, n2, active, slope, fed, upright, rows, vec, out_own = call(
        functools.partial(front_kernel, ranks=ranks, ratio=ratio, parts=blocks_own),
        (ranks,),
        in_order(x_all)
        + [(weights, pl.BlockSpec((width, 128), lambda *_: (0, (edge + cols) // 128)))] + angles
        + [(weights, column(0)), (weights, column(1)), (weights, column(2))],
        [(shape((count, width), bf16), tile(width)), (shape((count, width), bf16), tile(width)),
         (shape((count, hidden), bf16), tile(hidden)), (shape((count, hidden), bf16), tile(hidden)),
         (shape((count, width), f32), tile(width)),
         (shape((mixed_cols, count), bf16), upright_tile(mixed_cols)),
         (shape((3 * heads, count, HD), bf16),
          pl.BlockSpec((3 * heads, own, HD), lambda t, *_: (0, t, 0))),
         (shape((8, width), f32), whole_block((8, width))),
         (shape((cols, width), bf16), whole_block((cols, width)))],
        [pltpu.VMEM((1, mixed_cols), f32)],
        cost=10,
        first=(spot,),
    )

    all_heads = lambda j: pl.BlockSpec((heads, count, HD), lambda *_: (j, 0, 0))
    soft_spec = pl.BlockSpec((heads, count, own), lambda t, *_: (0, 0, t))
    soft, inverse, heads_low, *part_out = call(
        functools.partial(attend_kernel, ranks=ranks, parts=blocks_own),
        (ranks,),
        [(start, upright_tile(8)), (rows, all_heads(1)), (upright, upright_tile(cols)),
         (upright, upright_all(2)), (fed, tile(width)), (out_own, whole_block((cols, width)))],
        [(shape((heads, count, count), bf16), soft_spec), (shape((8, count), f32), upright_tile(8)),
         (shape((cols, count), bf16), upright_tile(cols))] + each,
        cost=10,
        first=(spot,),
    )

    dy_all = jnp.concatenate([dy_own] + [after(block, heads_low) for block in dy_got])
    scaled, grads_feed, feed_sums = call(
        functools.partial(feed_back_kernel, ranks=ranks, parts=blocks_own),
        (ranks,),
        in_order(dy_all) + in_order(x_all)
        + [(dy_own, whole_block((own, width))), (active, tile(hidden)),
         (slope, tile(hidden)), (n2, tile(width)), (vec, whole_block((8, width))),
         (weights, column(0)), (weights, column(1)), (heads_low, upright_tile(cols))],
        [(shape((count, width), bf16), tile(width)),
         (shape((width, edge - mixed_cols + cols), bf16),
          whole_block((width, edge - mixed_cols + cols))),
         (shape((8, width), f32), whole_block((8, width)))],
        [pltpu.VMEM((width, hidden), f32), pltpu.VMEM((hidden, width), f32),
         pltpu.VMEM((cols, width), f32)],
        cost=12,
        first=(spot,),
    )
    feed_part = scatter_dp(grads_feed)

    far = [r for r in range(1, ranks) if 2 * r == ranks]
    near = [r for r in range(1, ranks) if r not in far]
    out_parts = part_out[:1] + [shift(part_out[r], -r, ranks) for r in near]
    heads_low = after(heads_low, scaled, *out_parts)
    far_parts = [shift(after(part_out[r], scaled), -r, ranks) for r in far]
    head_tile = pl.BlockSpec((heads, own, HD), lambda t, *_: (0, t, 0))
    gquery, gkey, gvalue = call(
        functools.partial(attend_back_kernel, ranks=ranks, parts=blocks_own),
        (ranks,),
        in_order(dy_all)
        + [(out_own, whole_block((cols, width))), (heads_low, upright_tile(cols)),
           (inverse, upright_tile(8)), (soft, soft_spec), (rows, all_heads(2)),
           (upright, upright_all(1)), (rows, head_tile)] + angles,
        [(shape((cols, count), f32), upright_tile(cols)),
         (shape((heads, count, HD), f32), whole_block((heads, count, HD))),
         (shape((heads, count, HD), f32), whole_block((heads, count, HD)))],
        cost=10,
        first=(spot,),
    )
    gquery = after(gquery, *far_parts)
    out_sum = sum(part.astype(f32) for part in out_parts + far_parts)
    hidden_out = (x_own.astype(f32) + vec[5:6] + out_sum).astype(bf16)

    mixed, attn_sums, attn_bias, *total = call(
        functools.partial(rear_kernel, ranks=ranks, parts=blocks_own),
        (ranks,),
        in_order(x_all) + [(gquery, upright_tile(cols)), (gkey, head_tile), (gvalue, head_tile)]
        + angles
        + [(scaled, tile(width)), (vec, whole_block((8, width))), (weights, column(2))],
        [(shape((count, mixed_cols), bf16), tile(mixed_cols)),
         (shape((8, width), f32), whole_block((8, width))),
         (shape((8, mixed_cols), f32), whole_block((8, mixed_cols)))] + each,
        cost=8,
        first=(spot,),
    )
    (grads_attn,) = call(
        functools.partial(weigh_kernel, ranks=ranks, ratio=ratio),
        (1,),
        [(a, whole_block(a.shape)) for a in (n1, mixed, attn_sums, attn_bias, feed_sums)],
        [(shape((width, mixed_cols + 128), bf16), whole_block((width, mixed_cols + 128)))],
        [pltpu.VMEM((spread, share, 128), f32)],
        cost=5,
        first=(spot,),
    )

    grad_parts = total[:1] + around(total[1:], -1, ranks)
    attn_part = scatter_dp(after(grads_attn, feed_part))
    home = [((k % groups) * ranks + k // groups, k) for k in range(spread)]
    proj_part = lax.ppermute(feed_part[:, hidden + width :], ("dp", "seq"), home)
    parts = jnp.concatenate([feed_part[:, :hidden], attn_part], axis=1)
    parts = parts.reshape(ranks, share, parts.shape[1])
    parts = [lax.dynamic_index_in_dim(parts, (rank + r) % ranks, 0, False) for r in range(ranks)]
    parts = parts[:1] + around([after(p, proj_part, *grad_parts) for p in parts[1:]], 1, ranks)
    dy = dy_own.astype(f32)
    grad = sum(part.astype(f32) for part in grad_parts)
    rows_own = x_own.astype(f32)
    centred = rows_own - jnp.mean(rows_own, axis=-1, keepdims=True)
    rstd = lax.rsqrt(jnp.mean(centred * centred, axis=-1, keepdims=True) + eps)
    hat = centred * rstd
    grad_in = dy + rstd * (
        grad
        - jnp.mean(grad, axis=-1, keepdims=True)
        - hat * jnp.mean(grad * hat, axis=-1, keepdims=True)
    )

    factor = 1.0 / math.sqrt(count * groups)
    down_part = feed_part[:, hidden : hidden + width]
    results = [(share, 3 * width), (share, ranks * hidden), (share, width), (piece, width)]
    results += [(share,)] * 6 + [(3 * share,), (ratio * share,)]
    qkv_own, up_own, proj_own, down_own, *small_own = call(
        functools.partial(finish_kernel, factor=factor, hidden=hidden),
        (1,),
        [(spot, SMEM)] + [(a, whole_block(a.shape)) for a in (*parts, down_part, proj_part)],
        [(shape(size, f32), whole_block(size)) for size in results],
    )
    return (
        hidden_out.reshape(hidden_in.shape),
        grad_in.astype(bf16).reshape(hidden_in.shape),
        *small_own[:4],
        qkv_own,
        small_own[6],
        proj_own,
        small_own[4],
        up_own,
        small_own[7],
        down_own,
        small_own[5],
    )


def per_device(hidden_in, *rest):
    heads = hidden_in.shape[-1] // HD
    fits = heads % lax.axis_size("seq") == 0 and lax.axis_size("dp") == 8
    return (per_device_heads if fits else per_device_split)(hidden_in, *rest)


def solution(mesh):
    in_specs = (
        P("dp", "seq", None, None),
        P(),
        P("dp", None),
        P(("dp", "seq")),
        P(("dp", "seq")),
        P(("dp", "seq")),
        P(("dp", "seq")),
        P(("dp", "seq"), None),
        P(("dp", "seq")),
        P(("dp", "seq"), None),
        P(("dp", "seq")),
        P(("dp", "seq"), None),
        P(("dp", "seq")),
        P(("dp", "seq"), None),
        P(("dp", "seq")),
        P("dp", "seq", None, None),
    )
    out_specs = (
        P("dp", "seq", None, None),
        P("dp", "seq", None, None),
        P(("dp", "seq")),
        P(("dp", "seq")),
        P(("dp", "seq")),
        P(("dp", "seq")),
        P(("dp", "seq"), None),
        P(("dp", "seq")),
        P(("dp", "seq"), None),
        P(("dp", "seq")),
        P(("dp", "seq"), None),
        P(("dp", "seq")),
        P(("dp", "seq"), None),
        P(("dp", "seq")),
    )
    return jax.shard_map(
        per_device, mesh=mesh, in_specs=in_specs, out_specs=out_specs, check_vma=False
    )
```

```python
import functools
import math

import jax
import jax.numpy as jnp
from jax import lax
from jax.experimental import pallas as pl
from jax.experimental.pallas import tpu as pltpu
from jax.sharding import PartitionSpec as P

HD = 64
ROT = 16


eps = 1e-05
masked = -1e30


def layer_norm(rows, gain, shift):
    mean = jnp.mean(rows, axis=-1, keepdims=True)
    centred = rows - mean
    spread = jnp.mean(centred * centred, axis=-1, keepdims=True)
    return centred * lax.rsqrt(spread + eps) * gain + shift


def frequencies():
    return jnp.power(10000.0, -2.0 * jnp.arange(ROT // 2, dtype=jnp.float32) / ROT)


def rotate(heads, cosine, sine):
    half_rot = ROT // 2
    first = heads[..., :half_rot]
    second = heads[..., half_rot:ROT]
    return jnp.concatenate(
        [first * cosine - second * sine, second * cosine + first * sine, heads[..., ROT:]], axis=-1
    )


def doc_ids(positions, ends):
    return jnp.sum((positions[None, :, None] >= ends[:, None, :]).astype(jnp.int32), axis=-1)


def times_transposed(left, right):
    return lax.dot_general(
        left, right, (((1,), (1,)), ((), ())), preferred_element_type=jnp.float32
    )


def inner_rows(left, right):
    return lax.dot_general(
        left, right, (((0,), (0,)), ((), ())), preferred_element_type=jnp.float32
    )


def per_device_split(
    hidden_in,
    stretch_order,
    doc_lengths,
    attn_gain,
    attn_shift,
    feed_gain,
    feed_shift,
    qkv_weight,
    qkv_bias,
    out_weight,
    out_bias,
    up_weight,
    up_bias,
    down_weight,
    down_bias,
    grad_out,
):
    whole = (
        lax.all_gather(attn_gain, ("dp", "seq"), axis=0, tiled=True),
        lax.all_gather(attn_shift, ("dp", "seq"), axis=0, tiled=True),
        lax.all_gather(feed_gain, ("dp", "seq"), axis=0, tiled=True),
        lax.all_gather(feed_shift, ("dp", "seq"), axis=0, tiled=True),
        lax.all_gather(qkv_weight, ("dp", "seq"), axis=0, tiled=True),
        lax.all_gather(qkv_bias, ("dp", "seq"), axis=0, tiled=True),
        lax.all_gather(out_weight, ("dp", "seq"), axis=0, tiled=True),
        lax.all_gather(out_bias, ("dp", "seq"), axis=0, tiled=True),
        lax.all_gather(up_weight, ("dp", "seq"), axis=0, tiled=True),
        lax.all_gather(up_bias, ("dp", "seq"), axis=0, tiled=True),
        lax.all_gather(down_weight, ("dp", "seq"), axis=0, tiled=True),
        lax.all_gather(down_bias, ("dp", "seq"), axis=0, tiled=True),
    )
    seqs, blocks_own, half, width = hidden_in.shape
    heads = width // HD
    hidden_units = whole[8].shape[1]
    ratio = hidden_units // width
    queries = blocks_own * half
    count = seqs * queries
    scale_qk = 1.0 / math.sqrt(HD)
    lane = lax.axis_index("seq")
    offsets = jnp.arange(half, dtype=jnp.int32)
    own_blocks = lax.dynamic_slice_in_dim(stretch_order, lane * blocks_own, blocks_own)
    own_pos = (own_blocks[:, None] * half + offsets[None, :]).reshape(queries)
    ends = jnp.cumsum(doc_lengths, axis=1)[:, :-1]
    own_doc = doc_ids(own_pos, ends)
    angle = own_pos.astype(jnp.float32)[:, None] * frequencies()[None, :]
    cosine = jnp.cos(angle)[None, :, None, :]
    sine = jnp.sin(angle)[None, :, None, :]

    def allowed_of(key_pos, key_doc):
        causal = key_pos[None, None, None, :] <= own_pos[None, None, :, None]
        same = key_doc[:, None, None, :] == own_doc[:, None, :, None]
        return causal & same

    rows = hidden_in.astype(jnp.float32).reshape(count, width)
    normed_first, pull_first = jax.vjp(
        layer_norm, rows, whole[0].astype(jnp.float32), whole[1].astype(jnp.float32)
    )
    normed_second, pull_second = jax.vjp(
        layer_norm, rows, whole[2].astype(jnp.float32), whole[3].astype(jnp.float32)
    )
    first_low = normed_first.astype(jnp.bfloat16)
    second_low = normed_second.astype(jnp.bfloat16)
    mixed = jnp.dot(first_low, whole[4], preferred_element_type=jnp.float32) + whole[5].astype(
        jnp.float32
    )
    mixed = mixed.reshape(seqs, queries, 3, heads, HD)
    query = rotate(mixed[:, :, 0], cosine, sine).astype(jnp.bfloat16)
    key_own = (
        rotate(mixed[:, :, 1], cosine, sine)
        .astype(jnp.bfloat16)
        .reshape(seqs, blocks_own, half, width)
    )
    value_own = mixed[:, :, 2].astype(jnp.bfloat16).reshape(seqs, blocks_own, half, width)
    top = jnp.full((seqs, heads, queries), masked, jnp.float32)
    key_piece = lax.all_gather(key_own, "seq", axis=1, tiled=True)
    value_piece = lax.all_gather(value_own, "seq", axis=1, tiled=True)
    blocks = key_piece.shape[1]
    key_pos = (stretch_order[:, None] * half + offsets[None, :]).reshape(blocks * half)
    allowed = allowed_of(key_pos, doc_ids(key_pos, ends))
    keys = key_piece.reshape(seqs, blocks * half, heads, HD)
    values = value_piece.reshape(seqs, blocks * half, heads, HD)
    scores = (
        jnp.einsum("sqhd,skhd->shqk", query, keys, preferred_element_type=jnp.float32) * scale_qk
    )
    scores = jnp.where(allowed, scores, masked)
    new_top = jnp.maximum(top, jnp.max(scores, axis=-1))
    weights = jnp.where(allowed, jnp.exp(scores - new_top[..., None]), 0.0)
    total = jnp.sum(weights, axis=-1)
    accum = jnp.einsum(
        "shqk,skhd->shqd", weights.astype(jnp.bfloat16), values, preferred_element_type=jnp.float32
    )
    top, total, accum = (new_top, total, accum)
    logsum = top + jnp.log(total)
    heads_rows = jnp.transpose(accum / total[..., None], (0, 2, 1, 3))
    heads_low = heads_rows.reshape(count, width).astype(jnp.bfloat16)
    attended = jnp.dot(heads_low, whole[6], preferred_element_type=jnp.float32) + whole[7].astype(
        jnp.float32
    )
    inner = jnp.dot(second_low, whole[8], preferred_element_type=jnp.float32) + whole[9].astype(
        jnp.float32
    )
    active, pull_gelu = jax.vjp(lambda v: jax.nn.gelu(v, approximate=False), inner)
    active_low = active.astype(jnp.bfloat16)
    fed = jnp.dot(active_low, whole[10], preferred_element_type=jnp.float32) + whole[11].astype(
        jnp.float32
    )
    hidden_out = (rows + attended + fed).astype(jnp.bfloat16).reshape(hidden_in.shape)
    params_back = (
        lax.all_gather(attn_gain, ("dp", "seq"), axis=0, tiled=True),
        lax.all_gather(attn_shift, ("dp", "seq"), axis=0, tiled=True),
        lax.all_gather(feed_gain, ("dp", "seq"), axis=0, tiled=True),
        lax.all_gather(feed_shift, ("dp", "seq"), axis=0, tiled=True),
        lax.all_gather(qkv_weight, ("dp", "seq"), axis=0, tiled=True),
        lax.all_gather(qkv_bias, ("dp", "seq"), axis=0, tiled=True),
        lax.all_gather(out_weight, ("dp", "seq"), axis=0, tiled=True),
        lax.all_gather(out_bias, ("dp", "seq"), axis=0, tiled=True),
        lax.all_gather(up_weight, ("dp", "seq"), axis=0, tiled=True),
        lax.all_gather(up_bias, ("dp", "seq"), axis=0, tiled=True),
        lax.all_gather(down_weight, ("dp", "seq"), axis=0, tiled=True),
        lax.all_gather(down_bias, ("dp", "seq"), axis=0, tiled=True),
    )
    upstream_low = grad_out.reshape(count, width)
    upstream = upstream_low.astype(jnp.float32)
    grad_bias_out = jnp.sum(upstream, axis=0)
    grad_active = times_transposed(upstream_low, params_back[10])
    (grad_inner,) = pull_gelu(grad_active)
    inner_low = grad_inner.astype(jnp.bfloat16)
    grad_up_bias = jnp.sum(grad_inner, axis=0)
    grad_second = times_transposed(inner_low, params_back[8])
    grad_heads = times_transposed(upstream_low, params_back[6])
    heads_grad_low = grad_heads.astype(jnp.bfloat16).reshape(seqs, queries, heads, HD)
    delta = jnp.transpose(
        jnp.sum(heads_grad_low.astype(jnp.float32) * heads_rows, axis=-1), (0, 2, 1)
    )
    key_all, value_all = (
        lax.all_gather(key_own, "seq", axis=1, tiled=True),
        lax.all_gather(value_own, "seq", axis=1, tiled=True),
    )
    blocks_all = key_all.shape[1]

    def backstep(grad_query, block):
        keys = lax.dynamic_slice_in_dim(key_all, block, 1, axis=1).reshape(seqs, half, heads, HD)
        values = lax.dynamic_slice_in_dim(value_all, block, 1, axis=1).reshape(
            seqs, half, heads, HD
        )
        key_pos = lax.dynamic_slice_in_dim(stretch_order, block, 1) * half + offsets
        allowed = allowed_of(key_pos, doc_ids(key_pos, ends))
        scores = (
            jnp.einsum("sqhd,skhd->shqk", query, keys, preferred_element_type=jnp.float32)
            * scale_qk
        )
        probs = jnp.where(allowed, jnp.exp(scores - logsum[..., None]), 0.0)
        grad_probs = jnp.einsum(
            "sqhd,skhd->shqk", heads_grad_low, values, preferred_element_type=jnp.float32
        )
        grad_scores = (probs * (grad_probs - delta[..., None]) * scale_qk).astype(jnp.bfloat16)
        grad_query = grad_query + jnp.einsum(
            "shqk,skhd->sqhd", grad_scores, keys, preferred_element_type=jnp.float32
        )
        key_term = jnp.einsum(
            "shqk,sqhd->skhd", grad_scores, query, preferred_element_type=jnp.float32
        )
        value_term = jnp.einsum(
            "shqk,sqhd->skhd",
            probs.astype(jnp.bfloat16),
            heads_grad_low,
            preferred_element_type=jnp.float32,
        )
        return (
            grad_query,
            (key_term.reshape(seqs, half, width), value_term.reshape(seqs, half, width)),
        )

    grad_query, (grad_keys, grad_values) = lax.scan(
        backstep,
        jnp.zeros((seqs, queries, heads, HD), jnp.float32),
        jnp.arange(blocks_all, dtype=jnp.int32),
    )
    key_part, value_part = (
        lax.psum_scatter(
            grad_keys.astype(jnp.bfloat16), "seq", scatter_dimension=0, tiled=True
        ).astype(jnp.float32),
        lax.psum_scatter(
            grad_values.astype(jnp.bfloat16), "seq", scatter_dimension=0, tiled=True
        ).astype(jnp.float32),
    )
    key_sum = jnp.transpose(key_part, (1, 0, 2, 3))
    value_sum = jnp.transpose(value_part, (1, 0, 2, 3))
    query_back = rotate(grad_query, cosine, -sine).reshape(count, width)
    key_back = rotate(key_sum.reshape(seqs, queries, heads, HD), cosine, -sine).reshape(
        count, width
    )
    grad_mixed = jnp.concatenate([query_back, key_back, value_sum.reshape(count, width)], axis=1)
    mixed_low = grad_mixed.astype(jnp.bfloat16)
    grad_qkv_bias = jnp.sum(grad_mixed, axis=0)
    grad_first = times_transposed(mixed_low, params_back[4])
    rows_first, gain_first, shift_first = pull_first(grad_first)
    rows_second, gain_second, shift_second = pull_second(grad_second)
    grad_in = (upstream + rows_first + rows_second).astype(jnp.bfloat16).reshape(hidden_in.shape)
    factor = 1.0 / math.sqrt(count * lax.axis_size("dp") * lax.axis_size("seq"))
    small_columns = jnp.stack(
        [gain_first, shift_first, gain_second, shift_second, grad_bias_out], axis=1
    )
    qkv_bias_rows = grad_qkv_bias.reshape(width, 3)
    up_bias_rows = grad_up_bias.reshape(width, ratio)
    part_qkv = inner_rows(first_low, mixed_low)
    part_out = inner_rows(heads_low, upstream_low)
    part_up = inner_rows(second_low, inner_low)
    part_down = inner_rows(active_low, upstream_low).reshape(
        lax.axis_size(("dp", "seq")) * qkv_weight.shape[0], ratio * width
    )
    owned = lax.psum_scatter(
        jnp.concatenate(
            [part_qkv, part_out, part_up, part_down, small_columns, qkv_bias_rows, up_bias_rows],
            axis=1,
        )
        * factor,
        ("dp", "seq"),
        scatter_dimension=0,
        tiled=True,
    )
    own_rows = owned.shape[0]
    edge_out = 3 * width
    edge_up = edge_out + width
    edge_down = edge_up + hidden_units
    edge_small = edge_down + hidden_units
    edge_qkvb = edge_small + 5
    edge_upb = edge_qkvb + 3
    grad_qkv_own = owned[:, :edge_out]
    grad_out_own = owned[:, edge_out:edge_up]
    grad_up_own = owned[:, edge_up:edge_down]
    grad_down_own = owned[:, edge_down:edge_small].reshape(own_rows * ratio, width)
    grad_bias_own = owned[:, edge_small + 4]
    grad_qkvb_own = owned[:, edge_qkvb:edge_upb].reshape(own_rows * 3)
    grad_upb_own = owned[:, edge_upb : edge_upb + ratio].reshape(own_rows * ratio)
    return (
        hidden_out,
        grad_in,
        owned[:, edge_small],
        owned[:, edge_small + 1],
        owned[:, edge_small + 2],
        owned[:, edge_small + 3],
        grad_qkv_own,
        grad_qkvb_own,
        grad_out_own,
        grad_bias_own,
        grad_up_own,
        grad_upb_own,
        grad_down_own,
        grad_bias_own,
    )


f32 = jnp.float32
bf16 = jnp.bfloat16


def whole_block(shape):
    return pl.BlockSpec(shape, lambda *_: (0,) * len(shape))


def normalise(rows):
    centred = rows - jnp.mean(rows, axis=-1, keepdims=True)
    spread = jnp.mean(centred * centred, axis=-1, keepdims=True)
    return centred * lax.rsqrt(spread + eps)


def turn(upright, cosine, sine):
    half_rot = ROT // 2
    first = upright[:half_rot]
    second = upright[half_rot:ROT]
    return [first * cosine - second * sine, second * cosine + first * sine, upright[ROT:]]


def product(left, right, left_dim=1, right_dim=0):
    return lax.dot_general(
        left, right, (((left_dim,), (right_dim,)), ((), ())), preferred_element_type=f32
    )


def places(owners, per, base, index):
    lanes = lax.broadcasted_iota(jnp.int32, (LANES, index.shape[1]), 0)
    rows = lax.broadcasted_iota(jnp.int32, (owners, index.shape[1]), 0)
    return rows == index // per, (lanes == base + index % per).astype(bf16)


def vector_maps(rank, share, ranks, cols, hidden, ratio):
    line = lambda n: lax.broadcasted_iota(jnp.int32, (1, n), 1)
    width = ranks * cols
    part = line(3 * cols)
    maps = [(share, j * share, line(width)) for j in range(6)]
    maps.append((3 * share, 6 * share, part // cols * width + rank * cols + part % cols))
    held = ratio * share
    unit = line(hidden)
    maps.append((held, 9 * share, (unit // held * ranks + rank) * held + unit % held))
    return maps


def pack_kernel(rank_ref, up_ref, qkv_ref, out_ref, *refs, vectors, held):
    outs = refs[vectors:]
    ranks = len(outs) - 1
    rank = rank_ref[0]
    up, qkv = up_ref[...], qkv_ref[...]
    width = qkv.shape[1] // 3
    cols = width // ranks
    share = up.shape[0]
    line = jnp.concatenate([ref[...][None].astype(f32) for ref in refs[:vectors]], axis=1)
    line = jnp.pad(line, ((0, 0), (0, LANES - line.shape[1])))
    lines = [line[:, j : j + 128] for j in range(0, LANES, 128)]
    small = jnp.concatenate(lines + [jnp.zeros((share - len(lines), 128), f32)]).astype(bf16)
    for t in range(ranks):
        block = jnp.concatenate(
            [up[:, at : at + held] for at in range(t * held, up.shape[1], ranks * held)]
            + [qkv[:, j * width + t * cols : j * width + (t + 1) * cols] for j in range(3)]
            + [small],
            axis=1,
        )
        for r in range(ranks):

            @pl.when((rank + r) % ranks == t)
            def _():
                outs[r][...] = block

    out = out_ref[...].astype(f32)
    flat = jnp.concatenate([out[:, j * cols : (j + 1) * cols] for j in range(ranks)], axis=0)
    outs[-1][...] = flat.astype(bf16)


def land_kernel(rank_ref, *refs, hidden):
    ranks = len(refs) - 3
    rank = rank_ref[0]
    blocks = [ref[...].astype(f32) for ref in refs[:ranks]]
    ordered = []
    for t in range(ranks):
        picked = blocks[0]
        for r in range(1, ranks):
            picked = jnp.where((rank - r + ranks) % ranks == t, blocks[r], picked)
        ordered.append(picked)
    landed = jnp.concatenate(ordered, axis=0).astype(bf16)
    tail = landed.shape[1] - 128
    refs[-1][...] = jnp.concatenate(
        [landed[:, :hidden], refs[ranks][...], landed[:, hidden:tail], refs[ranks + 1][...],
         landed[:, tail:]], axis=1,
    )


def join(refs):
    return jnp.concatenate([ref[...] for ref in refs], axis=0)


def store_blocks(refs, spot_ref, step, tile, parts):
    half = tile.shape[0] // parts
    for k in range(parts):
        block = tile[k * half : (k + 1) * half]
        where = spot_ref[2 + step * parts + k]
        for r, ref in enumerate(refs):
            for slot in range(parts):

                @pl.when(where == r * parts + slot)
                def _():
                    ref[slot * half : (slot + 1) * half, :] = block


def front_kernel(rank_ref, *refs, ranks, ratio, parts):
    x_refs, (small_ref, cos_ref, sin_ref, up_ref, down_ref, attn_ref) = refs[:parts], refs[parts:-11]
    hat_ref, n1_ref, n2_ref, act_ref, slope_ref, fed_ref, upright_ref, rows_ref = refs[-11:-3]
    vec_ref, own_out_ref, bias_ref = refs[-3:]
    width, part3 = n1_ref.shape[1], upright_ref.shape[0]
    cols, hidden = part3 // 3, act_ref.shape[1]
    owners = ranks * 8
    share = width // owners

    @pl.when(pl.program_id(0) == 0)
    def _():
        table = small_ref[...].astype(f32).reshape(owners, share, 128)
        table = jnp.concatenate([table[:, j, :] for j in range(LANES // 128)], axis=1).astype(bf16)
        vectors = []
        for per, base, index in vector_maps(rank_ref[0], share, ranks, cols, hidden, ratio):
            rows, lanes = places(owners, per, base, index)
            spread = jnp.where(rows, product(table, lanes), 0.0)
            vectors.append(jnp.sum(spread, axis=0, keepdims=True))
        bias_ref[...] = vectors[6]
        vec_ref[...] = jnp.concatenate(
            vectors[:4] + [vectors[7], vectors[4] + vectors[5], jnp.zeros((2, width), f32)], axis=0
        )
        flat = attn_ref[:, part3:].astype(f32)
        rebuilt = []
        for d in range(8):
            start = d * share * ranks
            rebuilt.append(
                jnp.concatenate(
                    [flat[start + j * share : start + (j + 1) * share] for j in range(ranks)], axis=1
                )
            )
        own_out_ref[...] = jnp.concatenate(rebuilt, axis=0).astype(bf16)

    hat = normalise(join(x_refs).astype(f32))
    hat_ref[...] = hat.astype(bf16)
    vec = vec_ref[...]
    n1 = (hat * vec[0:1] + vec[1:2]).astype(bf16)
    n2 = (hat * vec[2:3] + vec[3:4]).astype(bf16)
    n1_ref[...] = n1
    n2_ref[...] = n2
    width = upright_ref.shape[0]
    mixed = product(n1, attn_ref[:, :width]) + bias_ref[...]
    upright = mixed.T
    cosine, sine = cos_ref[...], sin_ref[...]
    part = width // 3
    pieces = []
    for start in range(0, part, HD):
        pieces += [v * HD**-0.5 for v in turn(upright[start : start + HD], cosine, sine)]
    for start in range(part, 2 * part, HD):
        pieces += turn(upright[start : start + HD], cosine, sine)
    upright = jnp.concatenate(pieces + [upright[2 * part :]], axis=0)
    upright_ref[...] = upright.astype(bf16)
    mixed = upright.T.astype(bf16)
    for j in range(width // HD):
        rows_ref[j] = mixed[:, j * HD : (j + 1) * HD]
    inner = product(n2, up_ref[...]) + vec[4:5]
    phi = 0.5 + 0.5 * lax.erf(inner * math.sqrt(0.5))
    active = (inner * phi).astype(bf16)
    act_ref[...] = active
    bell = jnp.exp(inner * inner * -0.5) * (1.0 / math.sqrt(2.0 * math.pi))
    slope_ref[...] = (phi + inner * bell).astype(bf16)
    fed_ref[...] = product(active, down_ref[...])


def attend_kernel(spot_ref, *refs, ranks, parts):
    start_ref, key_ref, query_ref, value_ref, fed_ref, out_ref, soft_ref, inv_ref, heads_ref = refs[:9]
    step, own = pl.program_id(0), query_ref.shape[1]

    def tile(at):
        held = own * (at + 1)
        place = lax.broadcasted_iota(jnp.int32, (held, own), 0)
        asks = lax.broadcasted_iota(jnp.int32, (held, own), 1) + at * own
        bias = jnp.where((place <= asks) & (place >= start_ref[0:1]), 0.0, masked)
        for head in range(key_ref.shape[0]):
            spot = slice(head * HD, (head + 1) * HD)
            scores = product(key_ref[head, :held], query_ref[spot, :]) + bias
            weights = jnp.exp(scores - jnp.max(scores, axis=0, keepdims=True))
            inverse = 1.0 / jnp.sum(weights, axis=0, keepdims=True)
            soft = weights.astype(bf16)
            soft_ref[head, :held] = soft
            inv_ref[head : head + 1] = inverse
            heads_ref[spot, :] = (product(value_ref[spot, :held], soft) * inverse).astype(bf16)

    for at in range(ranks):
        pl.when(step == at)(functools.partial(tile, at))
    part = (fed_ref[...] + product(heads_ref[...], out_ref[...], 0, 0)).astype(bf16)
    store_blocks(refs[9:], spot_ref, step, part, parts)


def feed_back_kernel(spot_ref, *refs, ranks, parts):
    dy_refs, hat_ref, refs = refs[:parts], refs[parts], refs[parts + 1 :]
    own_ref, act_ref, slope_ref, n2_ref, vec_ref, up_ref, down_ref, heads_ref = refs[:8]
    scaled_ref, grads_ref, sums_ref, acc_up, acc_down, acc_out = refs[8:]
    step = pl.program_id(0)

    @pl.when(step == 0)
    def _():
        acc_up[...] = jnp.zeros_like(acc_up)
        acc_down[...] = jnp.zeros_like(acc_down)
        acc_out[...] = jnp.zeros_like(acc_out)
        sums_ref[...] = jnp.zeros_like(sums_ref)
        sums_ref[3:4] = jnp.sum(own_ref[...].astype(f32), axis=0, keepdims=True)

    dy = join(dy_refs)
    grad_inner = product(dy, down_ref[...], 1, 1) * slope_ref[...].astype(f32)
    low = grad_inner.astype(bf16)
    grad = product(low, up_ref[...], 1, 1)
    hat = hat_ref[...].astype(f32)
    scaled_ref[...] = (grad * vec_ref[2:3]).astype(bf16)
    sums_ref[0:1] += jnp.sum(grad * hat, axis=0, keepdims=True)
    sums_ref[1:2] += jnp.sum(grad, axis=0, keepdims=True)
    sums_ref[2:3] += jnp.sum(grad_inner, axis=0, keepdims=True)
    acc_up[...] += product(n2_ref[...], low, 0, 0)
    acc_down[...] += product(act_ref[...], dy, 0, 0)
    acc_out[...] += product(heads_ref[...], dy)

    @pl.when(step == pl.num_programs(0) - 1)
    def _():
        cols = acc_out.shape[0]
        share = cols // 8
        flat = []
        for d in range(8):
            rows = acc_out[d * share : (d + 1) * share]
            flat += [rows[:, j * cols : (j + 1) * cols] for j in range(ranks)]
        flat = jnp.concatenate(flat, axis=0)
        edge = acc_up.shape[1]
        grads_ref[:, :edge] = acc_up[...].astype(bf16)
        grads_ref[:, edge : edge + acc_down.shape[1]] = acc_down[...].astype(bf16)
        grads_ref[:, edge + acc_down.shape[1] :] = flat.astype(bf16)


def attend_back_kernel(spot_ref, *refs, ranks, parts):
    dy_refs, refs = refs[:parts], refs[parts:]
    out_ref, heads_ref, inv_ref, soft_ref, value_ref, key_ref, query_ref, cos_ref, sin_ref = refs[:9]
    gquery_ref, gkey_ref, gvalue_ref = refs[9:]
    step, own = pl.program_id(0), cos_ref.shape[1]

    @pl.when(step == 0)
    def _():
        gkey_ref[...] = jnp.zeros_like(gkey_ref)
        gvalue_ref[...] = jnp.zeros_like(gvalue_ref)

    lifted_all = product(out_ref[...], join(dy_refs), 1, 1).astype(bf16).astype(f32)

    def tile(at):
        held = own * (at + 1)
        for head in range(gkey_ref.shape[0]):
            spot = slice(head * HD, (head + 1) * HD)
            lifted = lifted_all[spot] * inv_ref[head : head + 1]
            delta = jnp.sum(lifted * heads_ref[spot, :].astype(f32), axis=0, keepdims=True)
            lifted_rows = lifted.T.astype(bf16)
            soft = soft_ref[head, :held]
            grad_soft = product(value_ref[head, :held], lifted.astype(bf16))
            grad_scores = (soft.astype(f32) * (grad_soft - delta)).astype(bf16)
            gvalue_ref[head, :held] += product(soft, lifted_rows)
            gkey_ref[head, :held] += product(grad_scores, query_ref[head])
            back = product(key_ref[spot, :held], grad_scores) * HD**-0.5
            gquery_ref[spot, :] = jnp.concatenate(turn(back, cos_ref[...], -sin_ref[...]), axis=0)

    for at in range(ranks):
        pl.when(step == at)(functools.partial(tile, at))


def rear_kernel(spot_ref, *refs, ranks, parts):
    hat_ref, refs = refs[0], refs[1:]
    gquery_ref, gkey_ref, gvalue_ref, cos_ref, sin_ref, scaled_ref, vec_ref, attn_ref = refs[:8]
    mixed_ref, sums_ref, gbias_ref = refs[8:11]
    step = pl.program_id(0)

    @pl.when(step == 0)
    def _():
        sums_ref[...] = jnp.zeros_like(sums_ref)
        gbias_ref[...] = jnp.zeros_like(gbias_ref)

    cosine, sine = cos_ref[...], sin_ref[...]
    pieces = [gquery_ref[...]]
    for j in range(gkey_ref.shape[0]):
        pieces += turn(gkey_ref[j].T, cosine, -sine)
    pieces += [gvalue_ref[j].T for j in range(gvalue_ref.shape[0])]
    mixed = jnp.concatenate(pieces, axis=0).T
    gbias_ref[0:1] += jnp.sum(mixed, axis=0, keepdims=True)
    low = mixed.astype(bf16)
    mixed_ref[...] = low
    grad = product(low, attn_ref[:, : low.shape[1]], 1, 1)
    hat = hat_ref[...].astype(f32)
    total = (grad * vec_ref[0:1] + scaled_ref[...].astype(f32)).astype(bf16)
    store_blocks(refs[11:], spot_ref, step, total, parts)
    sums_ref[0:1] += jnp.sum(grad * hat, axis=0, keepdims=True)
    sums_ref[1:2] += jnp.sum(grad, axis=0, keepdims=True)


def weigh_kernel(
    spot_ref, n1_ref, mixed_ref, sums_ref, gbias_ref, feed_ref, grads_ref, small_ref, *, ranks, ratio
):
    acc = product(n1_ref[...], mixed_ref[...], 0, 0)
    width, part3 = acc.shape
    cols, owners = part3 // 3, small_ref.shape[0]
    share = width // owners
    feed = feed_ref[...]
    vectors = [sums_ref[0:1], sums_ref[1:2], feed[0:1], feed[1:2], feed[3:4], None]
    vectors += [gbias_ref[0:1], feed[2:3]]
    maps = vector_maps(spot_ref[0], share, ranks, cols, feed.shape[1], ratio)
    table = jnp.zeros((owners, LANES), f32)
    for vector, (per, base, index) in zip(vectors, maps):
        if vector is not None:
            rows, lanes = places(owners, per, base, index)
            table += product(jnp.where(rows, vector, 0.0).astype(bf16), lanes, 1, 1)
    small_ref[...] = jnp.zeros_like(small_ref)
    for j in range(LANES // 128):
        small_ref[:, j, :] = table[:, j * 128 : (j + 1) * 128]
    small = small_ref[...].reshape(width, 128)
    grads_ref[...] = jnp.concatenate([acc, small], axis=1).astype(bf16)


def finish_kernel(
    rank_ref, *refs, factor, hidden,
):
    qkv_ref, up_ref, proj_ref, down_ref, *small_refs = refs[-12:]
    down_in, proj_in, refs = refs[-14], refs[-13], refs[:-14]
    ranks, rank = len(refs), rank_ref[0]
    blocks = [ref[...].astype(f32) * factor for ref in refs]
    share, width = proj_ref.shape
    cols = width // ranks
    small = jnp.zeros((share, 128), f32)
    for t in range(ranks):
        picked = blocks[0]
        for r in range(1, ranks):
            picked = jnp.where((rank - r + ranks) % ranks == t, blocks[r], picked)
        for at in range(0, hidden, down_ref.shape[0]):
            where = at * ranks + t * down_ref.shape[0]
            up_ref[:, where : where + down_ref.shape[0]] = picked[:, at : at + down_ref.shape[0]]
        for j in range(3):
            at = j * width + t * cols
            qkv_ref[:, at : at + cols] = picked[:, hidden + j * cols : hidden + (j + 1) * cols]
        small += picked[:, hidden + 3 * cols :]
    down_ref[...] = down_in[...].astype(f32) * factor
    rows = proj_in[...].astype(f32) * factor
    proj_ref[...] = jnp.concatenate(
        [rows[j * share : (j + 1) * share] for j in range(ranks)], axis=1
    )
    line = jnp.concatenate([small[j : j + 1] for j in range(LANES // 128)], axis=1)
    at = 0
    for j, ref in enumerate(small_refs):
        at -= share if j == 5 else 0
        at += share if j == 6 else 0
        ref[...] = line[0, at : at + ref.shape[0]]
        at += ref.shape[0]


LANES = 384
VMEM = 56 * 1024 * 1024


SMEM = pl.BlockSpec(memory_space=pltpu.SMEM)


def call(kernel, grid, ins, outs, scratch=(), cost=1, first=()):
    arrays, in_specs = zip(*ins)
    shapes, out_specs = zip(*outs)
    return pl.pallas_call(
        kernel,
        grid_spec=pltpu.PrefetchScalarGridSpec(
            num_scalar_prefetch=len(first),
            grid=grid,
            in_specs=list(in_specs),
            out_specs=list(out_specs),
            scratch_shapes=list(scratch),
        ),
        out_shape=list(shapes),
        compiler_params=pltpu.CompilerParams(vmem_limit_bytes=VMEM),
        cost_estimate=pl.CostEstimate(flops=cost * 10**9, bytes_accessed=0, transcendentals=0),
    )(*first, *arrays)


def after(value, *others):
    return lax.optimization_barrier((value,) + others)[0]


def shift(block, amount, ranks):
    return lax.ppermute(block, "seq", [(k, (k + amount) % ranks) for k in range(ranks)])


def around(blocks, sign, ranks):
    order = sorted(range(1, ranks), key=lambda r: abs(ranks - 2 * r))
    got = {r: shift(blocks[r - 1], sign * r, ranks) for r in order if blocks[r - 1] is not None}
    return [got.get(r) for r in range(1, ranks)]


def swap(block, mask):
    return lax.ppermute(block, "dp", [(k, k ^ mask) for k in range(8)])


def gather_dp(piece):
    place = lax.axis_index("dp")
    by_x, by_y, by_both = swap(piece, 2), swap(piece, 4), swap(piece, 6)
    near, beside, across = swap(piece, 1), swap(jnp.stack([by_x, by_y]), 1), swap(by_both, 1)
    whole = jnp.zeros((8,) + piece.shape, piece.dtype)
    for mask, part in (
        (0, piece), (1, near), (2, by_x), (4, by_y), (6, by_both),
        (3, beside[0]), (5, beside[1]), (7, across),
    ):
        whole = lax.dynamic_update_slice(whole, part[None], (place ^ mask, 0, 0))
    return whole.reshape(8 * piece.shape[0], piece.shape[1])


def scatter_dp(parts):
    parts = lax.all_to_all(parts.reshape(8, -1, parts.shape[1]), "dp", 0, 0, tiled=True)
    return jnp.sum(parts.astype(f32), axis=0).astype(bf16)


def per_device_heads(
    hidden_in,
    stretch_order,
    doc_lengths,
    attn_gain,
    attn_shift,
    feed_gain,
    feed_shift,
    qkv_weight,
    qkv_bias,
    out_weight,
    out_bias,
    up_weight,
    up_bias,
    down_weight,
    down_bias,
    grad_out,
):
    ranks, groups = lax.axis_size("seq"), lax.axis_size("dp")
    rank = lax.axis_index("seq")
    blocks_own, half, width = hidden_in.shape[1:]
    own = blocks_own * half
    count = ranks * own
    share = qkv_weight.shape[0]
    piece = share * ranks
    cols = width // ranks
    heads = cols // HD
    hidden = up_weight.shape[1] // ranks
    ratio = up_weight.shape[1] // width
    mixed_cols = 3 * cols
    edge = hidden + width + mixed_cols

    x_own = hidden_in.reshape(own, width)
    dy_own = grad_out.reshape(own, width)

    small = [attn_gain, attn_shift, feed_gain, feed_shift, out_bias, down_bias, qkv_bias, up_bias]
    shape = jax.ShapeDtypeStruct
    blocks = stretch_order.shape[0]
    slots = jnp.arange(blocks, dtype=jnp.int32)
    lies = jnp.sum(jnp.where(stretch_order[None] == slots[:, None], slots[None], 0), axis=1)
    lies = (rank - lies // blocks_own) % ranks * blocks_own + lies % blocks_own
    spot = jnp.concatenate([jnp.stack([rank, lax.axis_index("dp")]), lies])
    sent = (share, hidden + mixed_cols + 128)
    *packed, out_piece = call(
        functools.partial(pack_kernel, vectors=len(small), held=ratio * share),
        (1,),
        [(spot, SMEM)]
        + [(a, whole_block(a.shape)) for a in (up_weight, qkv_weight, out_weight, *small)],
        [(shape(sent, bf16), whole_block(sent))] * ranks
        + [(shape((piece, cols), bf16), whole_block((piece, cols)))],
    )
    spread = ranks * groups
    out_piece = lax.ppermute(
        out_piece, ("dp", "seq"),
        [(k, (k % groups) * ranks + k // groups) for k in range(spread)],
    )
    landed = packed[:1] + around(packed[1:], 1, ranks)
    x_next = shift(x_own, 1, ranks)
    landed[0] = after(landed[0], x_next)
    total_cols = edge + cols + 128
    (weight_piece,) = call(
        functools.partial(land_kernel, hidden=hidden),
        (1,),
        [(spot, SMEM)] + [(a, whole_block(a.shape)) for a in (*landed, down_weight, out_piece)],
        [(shape((piece, total_cols), bf16), whole_block((piece, total_cols)))],
    )
    weights = gather_dp(weight_piece)

    x_go = after(x_own, *landed)
    x_rest = around([None] + [x_go] * (ranks - 2), 1, ranks)[1:]
    x_all = jnp.concatenate([x_own] + [after(block, weights) for block in (x_next, *x_rest)])
    dy_go = after(dy_own, x_all)
    dy_got = around([dy_go] * (ranks - 1), 1, ranks)

    ends = jnp.cumsum(doc_lengths[0])[:-1]
    place = jnp.arange(count, dtype=jnp.int32)
    first_of = jnp.max(jnp.where(place[:, None] >= ends[None], ends[None], 0), axis=1)
    start = jnp.broadcast_to(first_of[None], (8, count))
    angle = frequencies()[:, None] * place.astype(f32)[None]
    cosine, sine = jnp.cos(angle), jnp.sin(angle)

    tile = lambda w: pl.BlockSpec((own, w), lambda t, *_: (t, 0))
    upright_tile = lambda n: pl.BlockSpec((n, own), lambda t, *_: (0, t))
    upright_all = lambda j: pl.BlockSpec((cols, count), lambda *_: (j, 0))
    column = lambda j: pl.BlockSpec((width, width), lambda *_: (0, j))
    angles = [(cosine, upright_tile(ROT // 2)), (sine, upright_tile(ROT // 2))]
    by_place = [
        pl.BlockSpec((half, width), lambda t, spot, k=k: (spot[2 + t * blocks_own + k], 0))
        for k in range(blocks_own)
    ]
    in_order = lambda array: [(array, spec) for spec in by_place]
    each = [(shape((own, width), bf16), whole_block((own, width)))] * ranks

    hat, n1, n2, active, slope, fed, upright, rows, vec, out_own = call(
        functools.partial(front_kernel, ranks=ranks, ratio=ratio, parts=blocks_own),
        (ranks,),
        in_order(x_all)
        + [(weights, pl.BlockSpec((width, 128), lambda *_: (0, (edge + cols) // 128)))] + angles
        + [(weights, column(0)), (weights, column(1)), (weights, column(2))],
        [(shape((count, width), bf16), tile(width))] * 3
        + [(shape((count, hidden), bf16), tile(hidden)), (shape((count, hidden), bf16), tile(hidden)),
         (shape((count, width), f32), tile(width)),
         (shape((mixed_cols, count), bf16), upright_tile(mixed_cols)),
         (shape((3 * heads, count, HD), bf16),
          pl.BlockSpec((3 * heads, own, HD), lambda t, *_: (0, t, 0))),
         (shape((8, width), f32), whole_block((8, width))),
         (shape((cols, width), bf16), whole_block((cols, width)))],
        [pltpu.VMEM((1, mixed_cols), f32)],
        cost=10,
        first=(spot,),
    )

    all_heads = lambda j: pl.BlockSpec((heads, count, HD), lambda *_: (j, 0, 0))
    soft_spec = pl.BlockSpec((heads, count, own), lambda t, *_: (0, 0, t))
    soft, inverse, heads_low, *part_out = call(
        functools.partial(attend_kernel, ranks=ranks, parts=blocks_own),
        (ranks,),
        [(start, upright_tile(8)), (rows, all_heads(1)), (upright, upright_tile(cols)),
         (upright, upright_all(2)), (fed, tile(width)), (out_own, whole_block((cols, width)))],
        [(shape((heads, count, count), bf16), soft_spec), (shape((8, count), f32), upright_tile(8)),
         (shape((cols, count), bf16), upright_tile(cols))] + each,
        cost=10,
        first=(spot,),
    )

    dy_all = jnp.concatenate([dy_own] + [after(block, heads_low) for block in dy_got])
    scaled, grads_feed, feed_sums = call(
        functools.partial(feed_back_kernel, ranks=ranks, parts=blocks_own),
        (ranks,),
        in_order(dy_all)
        + [(hat, tile(width)), (dy_own, whole_block((own, width))), (active, tile(hidden)),
         (slope, tile(hidden)), (n2, tile(width)), (vec, whole_block((8, width))),
         (weights, column(0)), (weights, column(1)), (heads_low, upright_tile(cols))],
        [(shape((count, width), bf16), tile(width)),
         (shape((width, edge - mixed_cols + cols), bf16),
          whole_block((width, edge - mixed_cols + cols))),
         (shape((8, width), f32), whole_block((8, width)))],
        [pltpu.VMEM((width, hidden), f32), pltpu.VMEM((hidden, width), f32),
         pltpu.VMEM((cols, width), f32)],
        cost=12,
        first=(spot,),
    )
    feed_part = scatter_dp(grads_feed)

    far = [r for r in range(1, ranks) if 2 * r == ranks]
    near = [r for r in range(1, ranks) if r not in far]
    out_parts = part_out[:1] + [shift(part_out[r], -r, ranks) for r in near]
    heads_low = after(heads_low, scaled, *out_parts)
    far_parts = [shift(after(part_out[r], scaled), -r, ranks) for r in far]
    head_tile = pl.BlockSpec((heads, own, HD), lambda t, *_: (0, t, 0))
    gquery, gkey, gvalue = call(
        functools.partial(attend_back_kernel, ranks=ranks, parts=blocks_own),
        (ranks,),
        in_order(dy_all)
        + [(out_own, whole_block((cols, width))), (heads_low, upright_tile(cols)),
           (inverse, upright_tile(8)), (soft, soft_spec), (rows, all_heads(2)),
           (upright, upright_all(1)), (rows, head_tile)] + angles,
        [(shape((cols, count), f32), upright_tile(cols)),
         (shape((heads, count, HD), f32), whole_block((heads, count, HD))),
         (shape((heads, count, HD), f32), whole_block((heads, count, HD)))],
        cost=10,
        first=(spot,),
    )
    gquery = after(gquery, *far_parts)
    out_sum = sum(part.astype(f32) for part in out_parts + far_parts)
    hidden_out = (x_own.astype(f32) + vec[5:6] + out_sum).astype(bf16)

    mixed, attn_sums, attn_bias, *total = call(
        functools.partial(rear_kernel, ranks=ranks, parts=blocks_own),
        (ranks,),
        [(hat, tile(width)), (gquery, upright_tile(cols)), (gkey, head_tile), (gvalue, head_tile)]
        + angles
        + [(scaled, tile(width)), (vec, whole_block((8, width))), (weights, column(2))],
        [(shape((count, mixed_cols), bf16), tile(mixed_cols)),
         (shape((8, width), f32), whole_block((8, width))),
         (shape((8, mixed_cols), f32), whole_block((8, mixed_cols)))] + each,
        cost=8,
        first=(spot,),
    )
    (grads_attn,) = call(
        functools.partial(weigh_kernel, ranks=ranks, ratio=ratio),
        (1,),
        [(a, whole_block(a.shape)) for a in (n1, mixed, attn_sums, attn_bias, feed_sums)],
        [(shape((width, mixed_cols + 128), bf16), whole_block((width, mixed_cols + 128)))],
        [pltpu.VMEM((spread, share, 128), f32)],
        cost=5,
        first=(spot,),
    )

    grad_parts = total[:1] + around(total[1:], -1, ranks)
    attn_part = scatter_dp(after(grads_attn, feed_part))
    home = [((k % groups) * ranks + k // groups, k) for k in range(spread)]
    proj_part = lax.ppermute(feed_part[:, hidden + width :], ("dp", "seq"), home)
    parts = jnp.concatenate([feed_part[:, :hidden], attn_part], axis=1)
    parts = parts.reshape(ranks, share, parts.shape[1])
    parts = [lax.dynamic_index_in_dim(parts, (rank + r) % ranks, 0, False) for r in range(ranks)]
    parts = parts[:1] + around([after(p, proj_part, *grad_parts) for p in parts[1:]], 1, ranks)
    dy = dy_own.astype(f32)
    grad = sum(part.astype(f32) for part in grad_parts)
    rows_own = x_own.astype(f32)
    centred = rows_own - jnp.mean(rows_own, axis=-1, keepdims=True)
    rstd = lax.rsqrt(jnp.mean(centred * centred, axis=-1, keepdims=True) + eps)
    hat = centred * rstd
    grad_in = dy + rstd * (
        grad
        - jnp.mean(grad, axis=-1, keepdims=True)
        - hat * jnp.mean(grad * hat, axis=-1, keepdims=True)
    )

    factor = 1.0 / math.sqrt(count * groups)
    down_part = feed_part[:, hidden : hidden + width]
    results = [(share, 3 * width), (share, ranks * hidden), (share, width), (piece, width)]
    results += [(share,)] * 6 + [(3 * share,), (ratio * share,)]
    qkv_own, up_own, proj_own, down_own, *small_own = call(
        functools.partial(finish_kernel, factor=factor, hidden=hidden),
        (1,),
        [(spot, SMEM)] + [(a, whole_block(a.shape)) for a in (*parts, down_part, proj_part)],
        [(shape(size, f32), whole_block(size)) for size in results],
    )
    return (
        hidden_out.reshape(hidden_in.shape),
        grad_in.astype(bf16).reshape(hidden_in.shape),
        *small_own[:4],
        qkv_own,
        small_own[6],
        proj_own,
        small_own[4],
        up_own,
        small_own[7],
        down_own,
        small_own[5],
    )


def per_device(hidden_in, *rest):
    heads = hidden_in.shape[-1] // HD
    fits = heads % lax.axis_size("seq") == 0 and lax.axis_size("dp") == 8
    return (per_device_heads if fits else per_device_split)(hidden_in, *rest)


def solution(mesh):
    in_specs = (
        P("dp", "seq", None, None),
        P(),
        P("dp", None),
        P(("dp", "seq")),
        P(("dp", "seq")),
        P(("dp", "seq")),
        P(("dp", "seq")),
        P(("dp", "seq"), None),
        P(("dp", "seq")),
        P(("dp", "seq"), None),
        P(("dp", "seq")),
        P(("dp", "seq"), None),
        P(("dp", "seq")),
        P(("dp", "seq"), None),
        P(("dp", "seq")),
        P("dp", "seq", None, None),
    )
    out_specs = (
        P("dp", "seq", None, None),
        P("dp", "seq", None, None),
        P(("dp", "seq")),
        P(("dp", "seq")),
        P(("dp", "seq")),
        P(("dp", "seq")),
        P(("dp", "seq"), None),
        P(("dp", "seq")),
        P(("dp", "seq"), None),
        P(("dp", "seq")),
        P(("dp", "seq"), None),
        P(("dp", "seq")),
        P(("dp", "seq"), None),
        P(("dp", "seq")),
    )
    return jax.shard_map(
        per_device, mesh=mesh, in_specs=in_specs, out_specs=out_specs, check_vma=False
    )
```

```python
import functools
import math

import jax
import jax.numpy as jnp
from jax import lax
from jax.experimental import pallas as pl
from jax.experimental.pallas import tpu as pltpu
from jax.sharding import PartitionSpec as P

HD = 64
ROT = 16


eps = 1e-05
masked = -1e30


def layer_norm(rows, gain, shift):
    mean = jnp.mean(rows, axis=-1, keepdims=True)
    centred = rows - mean
    spread = jnp.mean(centred * centred, axis=-1, keepdims=True)
    return centred * lax.rsqrt(spread + eps) * gain + shift


def frequencies():
    return jnp.power(10000.0, -2.0 * jnp.arange(ROT // 2, dtype=jnp.float32) / ROT)


def rotate(heads, cosine, sine):
    half_rot = ROT // 2
    first = heads[..., :half_rot]
    second = heads[..., half_rot:ROT]
    return jnp.concatenate(
        [first * cosine - second * sine, second * cosine + first * sine, heads[..., ROT:]], axis=-1
    )


def doc_ids(positions, ends):
    return jnp.sum((positions[None, :, None] >= ends[:, None, :]).astype(jnp.int32), axis=-1)


def times_transposed(left, right):
    return lax.dot_general(
        left, right, (((1,), (1,)), ((), ())), preferred_element_type=jnp.float32
    )


def inner_rows(left, right):
    return lax.dot_general(
        left, right, (((0,), (0,)), ((), ())), preferred_element_type=jnp.float32
    )


def per_device_split(
    hidden_in,
    stretch_order,
    doc_lengths,
    attn_gain,
    attn_shift,
    feed_gain,
    feed_shift,
    qkv_weight,
    qkv_bias,
    out_weight,
    out_bias,
    up_weight,
    up_bias,
    down_weight,
    down_bias,
    grad_out,
):
    whole = (
        lax.all_gather(attn_gain, ("dp", "seq"), axis=0, tiled=True),
        lax.all_gather(attn_shift, ("dp", "seq"), axis=0, tiled=True),
        lax.all_gather(feed_gain, ("dp", "seq"), axis=0, tiled=True),
        lax.all_gather(feed_shift, ("dp", "seq"), axis=0, tiled=True),
        lax.all_gather(qkv_weight, ("dp", "seq"), axis=0, tiled=True),
        lax.all_gather(qkv_bias, ("dp", "seq"), axis=0, tiled=True),
        lax.all_gather(out_weight, ("dp", "seq"), axis=0, tiled=True),
        lax.all_gather(out_bias, ("dp", "seq"), axis=0, tiled=True),
        lax.all_gather(up_weight, ("dp", "seq"), axis=0, tiled=True),
        lax.all_gather(up_bias, ("dp", "seq"), axis=0, tiled=True),
        lax.all_gather(down_weight, ("dp", "seq"), axis=0, tiled=True),
        lax.all_gather(down_bias, ("dp", "seq"), axis=0, tiled=True),
    )
    seqs, blocks_own, half, width = hidden_in.shape
    heads = width // HD
    hidden_units = whole[8].shape[1]
    ratio = hidden_units // width
    queries = blocks_own * half
    count = seqs * queries
    scale_qk = 1.0 / math.sqrt(HD)
    lane = lax.axis_index("seq")
    offsets = jnp.arange(half, dtype=jnp.int32)
    own_blocks = lax.dynamic_slice_in_dim(stretch_order, lane * blocks_own, blocks_own)
    own_pos = (own_blocks[:, None] * half + offsets[None, :]).reshape(queries)
    ends = jnp.cumsum(doc_lengths, axis=1)[:, :-1]
    own_doc = doc_ids(own_pos, ends)
    angle = own_pos.astype(jnp.float32)[:, None] * frequencies()[None, :]
    cosine = jnp.cos(angle)[None, :, None, :]
    sine = jnp.sin(angle)[None, :, None, :]

    def allowed_of(key_pos, key_doc):
        causal = key_pos[None, None, None, :] <= own_pos[None, None, :, None]
        same = key_doc[:, None, None, :] == own_doc[:, None, :, None]
        return causal & same

    rows = hidden_in.astype(jnp.float32).reshape(count, width)
    normed_first, pull_first = jax.vjp(
        layer_norm, rows, whole[0].astype(jnp.float32), whole[1].astype(jnp.float32)
    )
    normed_second, pull_second = jax.vjp(
        layer_norm, rows, whole[2].astype(jnp.float32), whole[3].astype(jnp.float32)
    )
    first_low = normed_first.astype(jnp.bfloat16)
    second_low = normed_second.astype(jnp.bfloat16)
    mixed = jnp.dot(first_low, whole[4], preferred_element_type=jnp.float32) + whole[5].astype(
        jnp.float32
    )
    mixed = mixed.reshape(seqs, queries, 3, heads, HD)
    query = rotate(mixed[:, :, 0], cosine, sine).astype(jnp.bfloat16)
    key_own = (
        rotate(mixed[:, :, 1], cosine, sine)
        .astype(jnp.bfloat16)
        .reshape(seqs, blocks_own, half, width)
    )
    value_own = mixed[:, :, 2].astype(jnp.bfloat16).reshape(seqs, blocks_own, half, width)
    top = jnp.full((seqs, heads, queries), masked, jnp.float32)
    key_piece = lax.all_gather(key_own, "seq", axis=1, tiled=True)
    value_piece = lax.all_gather(value_own, "seq", axis=1, tiled=True)
    blocks = key_piece.shape[1]
    key_pos = (stretch_order[:, None] * half + offsets[None, :]).reshape(blocks * half)
    allowed = allowed_of(key_pos, doc_ids(key_pos, ends))
    keys = key_piece.reshape(seqs, blocks * half, heads, HD)
    values = value_piece.reshape(seqs, blocks * half, heads, HD)
    scores = (
        jnp.einsum("sqhd,skhd->shqk", query, keys, preferred_element_type=jnp.float32) * scale_qk
    )
    scores = jnp.where(allowed, scores, masked)
    new_top = jnp.maximum(top, jnp.max(scores, axis=-1))
    weights = jnp.where(allowed, jnp.exp(scores - new_top[..., None]), 0.0)
    total = jnp.sum(weights, axis=-1)
    accum = jnp.einsum(
        "shqk,skhd->shqd", weights.astype(jnp.bfloat16), values, preferred_element_type=jnp.float32
    )
    top, total, accum = (new_top, total, accum)
    logsum = top + jnp.log(total)
    heads_rows = jnp.transpose(accum / total[..., None], (0, 2, 1, 3))
    heads_low = heads_rows.reshape(count, width).astype(jnp.bfloat16)
    attended = jnp.dot(heads_low, whole[6], preferred_element_type=jnp.float32) + whole[7].astype(
        jnp.float32
    )
    inner = jnp.dot(second_low, whole[8], preferred_element_type=jnp.float32) + whole[9].astype(
        jnp.float32
    )
    active, pull_gelu = jax.vjp(lambda v: jax.nn.gelu(v, approximate=False), inner)
    active_low = active.astype(jnp.bfloat16)
    fed = jnp.dot(active_low, whole[10], preferred_element_type=jnp.float32) + whole[11].astype(
        jnp.float32
    )
    hidden_out = (rows + attended + fed).astype(jnp.bfloat16).reshape(hidden_in.shape)
    params_back = (
        lax.all_gather(attn_gain, ("dp", "seq"), axis=0, tiled=True),
        lax.all_gather(attn_shift, ("dp", "seq"), axis=0, tiled=True),
        lax.all_gather(feed_gain, ("dp", "seq"), axis=0, tiled=True),
        lax.all_gather(feed_shift, ("dp", "seq"), axis=0, tiled=True),
        lax.all_gather(qkv_weight, ("dp", "seq"), axis=0, tiled=True),
        lax.all_gather(qkv_bias, ("dp", "seq"), axis=0, tiled=True),
        lax.all_gather(out_weight, ("dp", "seq"), axis=0, tiled=True),
        lax.all_gather(out_bias, ("dp", "seq"), axis=0, tiled=True),
        lax.all_gather(up_weight, ("dp", "seq"), axis=0, tiled=True),
        lax.all_gather(up_bias, ("dp", "seq"), axis=0, tiled=True),
        lax.all_gather(down_weight, ("dp", "seq"), axis=0, tiled=True),
        lax.all_gather(down_bias, ("dp", "seq"), axis=0, tiled=True),
    )
    upstream_low = grad_out.reshape(count, width)
    upstream = upstream_low.astype(jnp.float32)
    grad_bias_out = jnp.sum(upstream, axis=0)
    grad_active = times_transposed(upstream_low, params_back[10])
    (grad_inner,) = pull_gelu(grad_active)
    inner_low = grad_inner.astype(jnp.bfloat16)
    grad_up_bias = jnp.sum(grad_inner, axis=0)
    grad_second = times_transposed(inner_low, params_back[8])
    grad_heads = times_transposed(upstream_low, params_back[6])
    heads_grad_low = grad_heads.astype(jnp.bfloat16).reshape(seqs, queries, heads, HD)
    delta = jnp.transpose(
        jnp.sum(heads_grad_low.astype(jnp.float32) * heads_rows, axis=-1), (0, 2, 1)
    )
    key_all, value_all = (
        lax.all_gather(key_own, "seq", axis=1, tiled=True),
        lax.all_gather(value_own, "seq", axis=1, tiled=True),
    )
    blocks_all = key_all.shape[1]

    def backstep(grad_query, block):
        keys = lax.dynamic_slice_in_dim(key_all, block, 1, axis=1).reshape(seqs, half, heads, HD)
        values = lax.dynamic_slice_in_dim(value_all, block, 1, axis=1).reshape(
            seqs, half, heads, HD
        )
        key_pos = lax.dynamic_slice_in_dim(stretch_order, block, 1) * half + offsets
        allowed = allowed_of(key_pos, doc_ids(key_pos, ends))
        scores = (
            jnp.einsum("sqhd,skhd->shqk", query, keys, preferred_element_type=jnp.float32)
            * scale_qk
        )
        probs = jnp.where(allowed, jnp.exp(scores - logsum[..., None]), 0.0)
        grad_probs = jnp.einsum(
            "sqhd,skhd->shqk", heads_grad_low, values, preferred_element_type=jnp.float32
        )
        grad_scores = (probs * (grad_probs - delta[..., None]) * scale_qk).astype(jnp.bfloat16)
        grad_query = grad_query + jnp.einsum(
            "shqk,skhd->sqhd", grad_scores, keys, preferred_element_type=jnp.float32
        )
        key_term = jnp.einsum(
            "shqk,sqhd->skhd", grad_scores, query, preferred_element_type=jnp.float32
        )
        value_term = jnp.einsum(
            "shqk,sqhd->skhd",
            probs.astype(jnp.bfloat16),
            heads_grad_low,
            preferred_element_type=jnp.float32,
        )
        return (
            grad_query,
            (key_term.reshape(seqs, half, width), value_term.reshape(seqs, half, width)),
        )

    grad_query, (grad_keys, grad_values) = lax.scan(
        backstep,
        jnp.zeros((seqs, queries, heads, HD), jnp.float32),
        jnp.arange(blocks_all, dtype=jnp.int32),
    )
    key_part, value_part = (
        lax.psum_scatter(
            grad_keys.astype(jnp.bfloat16), "seq", scatter_dimension=0, tiled=True
        ).astype(jnp.float32),
        lax.psum_scatter(
            grad_values.astype(jnp.bfloat16), "seq", scatter_dimension=0, tiled=True
        ).astype(jnp.float32),
    )
    key_sum = jnp.transpose(key_part, (1, 0, 2, 3))
    value_sum = jnp.transpose(value_part, (1, 0, 2, 3))
    query_back = rotate(grad_query, cosine, -sine).reshape(count, width)
    key_back = rotate(key_sum.reshape(seqs, queries, heads, HD), cosine, -sine).reshape(
        count, width
    )
    grad_mixed = jnp.concatenate([query_back, key_back, value_sum.reshape(count, width)], axis=1)
    mixed_low = grad_mixed.astype(jnp.bfloat16)
    grad_qkv_bias = jnp.sum(grad_mixed, axis=0)
    grad_first = times_transposed(mixed_low, params_back[4])
    rows_first, gain_first, shift_first = pull_first(grad_first)
    rows_second, gain_second, shift_second = pull_second(grad_second)
    grad_in = (upstream + rows_first + rows_second).astype(jnp.bfloat16).reshape(hidden_in.shape)
    factor = 1.0 / math.sqrt(count * lax.axis_size("dp") * lax.axis_size("seq"))
    small_columns = jnp.stack(
        [gain_first, shift_first, gain_second, shift_second, grad_bias_out], axis=1
    )
    qkv_bias_rows = grad_qkv_bias.reshape(width, 3)
    up_bias_rows = grad_up_bias.reshape(width, ratio)
    part_qkv = inner_rows(first_low, mixed_low)
    part_out = inner_rows(heads_low, upstream_low)
    part_up = inner_rows(second_low, inner_low)
    part_down = inner_rows(active_low, upstream_low).reshape(
        lax.axis_size(("dp", "seq")) * qkv_weight.shape[0], ratio * width
    )
    owned = lax.psum_scatter(
        jnp.concatenate(
            [part_qkv, part_out, part_up, part_down, small_columns, qkv_bias_rows, up_bias_rows],
            axis=1,
        )
        * factor,
        ("dp", "seq"),
        scatter_dimension=0,
        tiled=True,
    )
    own_rows = owned.shape[0]
    edge_out = 3 * width
    edge_up = edge_out + width
    edge_down = edge_up + hidden_units
    edge_small = edge_down + hidden_units
    edge_qkvb = edge_small + 5
    edge_upb = edge_qkvb + 3
    grad_qkv_own = owned[:, :edge_out]
    grad_out_own = owned[:, edge_out:edge_up]
    grad_up_own = owned[:, edge_up:edge_down]
    grad_down_own = owned[:, edge_down:edge_small].reshape(own_rows * ratio, width)
    grad_bias_own = owned[:, edge_small + 4]
    grad_qkvb_own = owned[:, edge_qkvb:edge_upb].reshape(own_rows * 3)
    grad_upb_own = owned[:, edge_upb : edge_upb + ratio].reshape(own_rows * ratio)
    return (
        hidden_out,
        grad_in,
        owned[:, edge_small],
        owned[:, edge_small + 1],
        owned[:, edge_small + 2],
        owned[:, edge_small + 3],
        grad_qkv_own,
        grad_qkvb_own,
        grad_out_own,
        grad_bias_own,
        grad_up_own,
        grad_upb_own,
        grad_down_own,
        grad_bias_own,
    )


f32 = jnp.float32
bf16 = jnp.bfloat16


def whole_block(shape):
    return pl.BlockSpec(shape, lambda *_: (0,) * len(shape))


def normalise(rows):
    centred = rows - jnp.mean(rows, axis=-1, keepdims=True)
    spread = jnp.mean(centred * centred, axis=-1, keepdims=True)
    return centred * lax.rsqrt(spread + eps)


def turn(upright, cosine, sine):
    half_rot = ROT // 2
    first = upright[:half_rot]
    second = upright[half_rot:ROT]
    return [first * cosine - second * sine, second * cosine + first * sine, upright[ROT:]]


def product(left, right, left_dim=1, right_dim=0):
    return lax.dot_general(
        left, right, (((left_dim,), (right_dim,)), ((), ())), preferred_element_type=f32
    )


def places(owners, per, base, index):
    lanes = lax.broadcasted_iota(jnp.int32, (LANES, index.shape[1]), 0)
    rows = lax.broadcasted_iota(jnp.int32, (owners, index.shape[1]), 0)
    return rows == index // per, (lanes == base + index % per).astype(bf16)


def vector_maps(rank, share, ranks, cols, hidden, ratio):
    line = lambda n: lax.broadcasted_iota(jnp.int32, (1, n), 1)
    width = ranks * cols
    part = line(3 * cols)
    maps = [(share, j * share, line(width)) for j in range(6)]
    maps.append((3 * share, 6 * share, part // cols * width + rank * cols + part % cols))
    held = ratio * share
    unit = line(hidden)
    maps.append((held, 9 * share, (unit // held * ranks + rank) * held + unit % held))
    return maps


def pack_kernel(rank_ref, up_ref, qkv_ref, out_ref, *refs, vectors, held):
    outs = refs[vectors:]
    ranks = len(outs) - 1
    rank = rank_ref[0]
    up, qkv = up_ref[...], qkv_ref[...]
    width = qkv.shape[1] // 3
    cols = width // ranks
    share = up.shape[0]
    line = jnp.concatenate([ref[...][None].astype(f32) for ref in refs[:vectors]], axis=1)
    line = jnp.pad(line, ((0, 0), (0, LANES - line.shape[1])))
    lines = [line[:, j : j + 128] for j in range(0, LANES, 128)]
    small = jnp.concatenate(lines + [jnp.zeros((share - len(lines), 128), f32)]).astype(bf16)
    for t in range(ranks):
        block = jnp.concatenate(
            [up[:, at : at + held] for at in range(t * held, up.shape[1], ranks * held)]
            + [qkv[:, j * width + t * cols : j * width + (t + 1) * cols] for j in range(3)]
            + [small],
            axis=1,
        )
        for r in range(ranks):

            @pl.when((rank + r) % ranks == t)
            def _():
                outs[r][...] = block

    out = out_ref[...].astype(f32)
    flat = jnp.concatenate([out[:, j * cols : (j + 1) * cols] for j in range(ranks)], axis=0)
    outs[-1][...] = flat.astype(bf16)


def land_kernel(rank_ref, *refs, hidden):
    ranks = len(refs) - 3
    rank = rank_ref[0]
    blocks = [ref[...].astype(f32) for ref in refs[:ranks]]
    ordered = []
    for t in range(ranks):
        picked = blocks[0]
        for r in range(1, ranks):
            picked = jnp.where((rank - r + ranks) % ranks == t, blocks[r], picked)
        ordered.append(picked)
    landed = jnp.concatenate(ordered, axis=0).astype(bf16)
    tail = landed.shape[1] - 128
    refs[-1][...] = jnp.concatenate(
        [landed[:, :hidden], refs[ranks][...], landed[:, hidden:tail], refs[ranks + 1][...],
         landed[:, tail:]], axis=1,
    )


def join(refs):
    return jnp.concatenate([ref[...] for ref in refs], axis=0)


def store_blocks(refs, spot_ref, step, tile, parts):
    half = tile.shape[0] // parts
    for k in range(parts):
        block = tile[k * half : (k + 1) * half]
        where = spot_ref[2 + step * parts + k]
        for r, ref in enumerate(refs):
            for slot in range(parts):

                @pl.when(where == r * parts + slot)
                def _():
                    ref[slot * half : (slot + 1) * half, :] = block


def front_kernel(rank_ref, *refs, ranks, ratio, parts):
    x_refs, (small_ref, cos_ref, sin_ref, up_ref, down_ref, attn_ref) = refs[:parts], refs[parts:-11]
    hat_ref, n1_ref, n2_ref, act_ref, slope_ref, fed_ref, upright_ref, rows_ref = refs[-11:-3]
    vec_ref, own_out_ref, bias_ref = refs[-3:]
    width, part3 = n1_ref.shape[1], upright_ref.shape[0]
    cols, hidden = part3 // 3, act_ref.shape[1]
    owners = ranks * 8
    share = width // owners

    @pl.when(pl.program_id(0) == 0)
    def _():
        table = small_ref[...].astype(f32).reshape(owners, share, 128)
        table = jnp.concatenate([table[:, j, :] for j in range(LANES // 128)], axis=1).astype(bf16)
        vectors = []
        for per, base, index in vector_maps(rank_ref[0], share, ranks, cols, hidden, ratio):
            rows, lanes = places(owners, per, base, index)
            spread = jnp.where(rows, product(table, lanes), 0.0)
            vectors.append(jnp.sum(spread, axis=0, keepdims=True))
        bias_ref[...] = vectors[6]
        vec_ref[...] = jnp.concatenate(
            vectors[:4] + [vectors[7], vectors[4] + vectors[5], jnp.zeros((2, width), f32)], axis=0
        )
        flat = attn_ref[:, part3:].astype(f32)
        rebuilt = []
        for d in range(8):
            start = d * share * ranks
            rebuilt.append(
                jnp.concatenate(
                    [flat[start + j * share : start + (j + 1) * share] for j in range(ranks)], axis=1
                )
            )
        own_out_ref[...] = jnp.concatenate(rebuilt, axis=0).astype(bf16)

    hat = normalise(join(x_refs).astype(f32))
    hat_ref[...] = hat.astype(bf16)
    vec = vec_ref[...]
    n1 = (hat * vec[0:1] + vec[1:2]).astype(bf16)
    n2 = (hat * vec[2:3] + vec[3:4]).astype(bf16)
    n1_ref[...] = n1
    n2_ref[...] = n2
    width = upright_ref.shape[0]
    mixed = product(n1, attn_ref[:, :width]) + bias_ref[...]
    upright = mixed.T
    cosine, sine = cos_ref[...], sin_ref[...]
    part = width // 3
    pieces = []
    for start in range(0, part, HD):
        pieces += [v * HD**-0.5 for v in turn(upright[start : start + HD], cosine, sine)]
    for start in range(part, 2 * part, HD):
        pieces += turn(upright[start : start + HD], cosine, sine)
    upright = jnp.concatenate(pieces + [upright[2 * part :]], axis=0)
    upright_ref[...] = upright.astype(bf16)
    mixed = upright.T.astype(bf16)
    for j in range(width // HD):
        rows_ref[j] = mixed[:, j * HD : (j + 1) * HD]
    inner = product(n2, up_ref[...]) + vec[4:5]
    phi = 0.5 + 0.5 * lax.erf(inner * math.sqrt(0.5))
    active = (inner * phi).astype(bf16)
    act_ref[...] = active
    bell = jnp.exp(inner * inner * -0.5) * (1.0 / math.sqrt(2.0 * math.pi))
    slope_ref[...] = (phi + inner * bell).astype(bf16)
    fed_ref[...] = product(active, down_ref[...])


def attend_kernel(spot_ref, *refs, ranks, parts):
    start_ref, key_ref, query_ref, value_ref, fed_ref, out_ref, soft_ref, inv_ref, heads_ref = refs[:9]
    step, own = pl.program_id(0), query_ref.shape[1]

    def tile(at):
        held = own * (at + 1)
        place = lax.broadcasted_iota(jnp.int32, (held, own), 0)
        asks = lax.broadcasted_iota(jnp.int32, (held, own), 1) + at * own
        bias = jnp.where((place <= asks) & (place >= start_ref[0:1]), 0.0, masked)
        for head in range(key_ref.shape[0]):
            spot = slice(head * HD, (head + 1) * HD)
            scores = product(key_ref[head, :held], query_ref[spot, :]) + bias
            weights = jnp.exp(scores - jnp.max(scores, axis=0, keepdims=True))
            inverse = 1.0 / jnp.sum(weights, axis=0, keepdims=True)
            soft = weights.astype(bf16)
            soft_ref[head, :held] = soft
            inv_ref[head : head + 1] = inverse
            heads_ref[spot, :] = (product(value_ref[spot, :held], soft) * inverse).astype(bf16)

    for at in range(ranks):
        pl.when(step == at)(functools.partial(tile, at))
    part = (fed_ref[...] + product(heads_ref[...], out_ref[...], 0, 0)).astype(bf16)
    store_blocks(refs[9:], spot_ref, step, part, parts)


def feed_back_kernel(spot_ref, *refs, ranks, parts):
    dy_refs, hat_ref, refs = refs[:parts], refs[parts], refs[parts + 1 :]
    own_ref, act_ref, slope_ref, n2_ref, vec_ref, up_ref, down_ref, heads_ref = refs[:8]
    scaled_ref, grads_ref, sums_ref, acc_up, acc_down, acc_out = refs[8:]
    step = pl.program_id(0)

    @pl.when(step == 0)
    def _():
        acc_up[...] = jnp.zeros_like(acc_up)
        acc_down[...] = jnp.zeros_like(acc_down)
        acc_out[...] = jnp.zeros_like(acc_out)
        sums_ref[...] = jnp.zeros_like(sums_ref)
        sums_ref[3:4] = jnp.sum(own_ref[...].astype(f32), axis=0, keepdims=True)

    dy = join(dy_refs)
    grad_inner = product(dy, down_ref[...], 1, 1) * slope_ref[...].astype(f32)
    low = grad_inner.astype(bf16)
    grad = product(low, up_ref[...], 1, 1)
    hat = hat_ref[...].astype(f32)
    scaled_ref[...] = (grad * vec_ref[2:3]).astype(bf16)
    sums_ref[0:1] += jnp.sum(grad * hat, axis=0, keepdims=True)
    sums_ref[1:2] += jnp.sum(grad, axis=0, keepdims=True)
    sums_ref[2:3] += jnp.sum(grad_inner, axis=0, keepdims=True)
    acc_up[...] += product(n2_ref[...], low, 0, 0)
    acc_down[...] += product(act_ref[...], dy, 0, 0)
    acc_out[...] += product(heads_ref[...], dy)

    @pl.when(step == pl.num_programs(0) - 1)
    def _():
        cols = acc_out.shape[0]
        share = cols // 8
        flat = []
        for d in range(8):
            rows = acc_out[d * share : (d + 1) * share]
            flat += [rows[:, j * cols : (j + 1) * cols] for j in range(ranks)]
        flat = jnp.concatenate(flat, axis=0)
        edge = acc_up.shape[1]
        grads_ref[:, :edge] = acc_up[...].astype(bf16)
        grads_ref[:, edge : edge + acc_down.shape[1]] = acc_down[...].astype(bf16)
        grads_ref[:, edge + acc_down.shape[1] :] = flat.astype(bf16)


def attend_back_kernel(spot_ref, *refs, ranks, parts):
    dy_refs, refs = refs[:parts], refs[parts:]
    out_ref, heads_ref, inv_ref, soft_ref, value_ref, key_ref, query_ref, cos_ref, sin_ref = refs[:9]
    gquery_ref, low_key_ref, low_value_ref, gkey_ref, gvalue_ref = refs[9:]
    step, own = pl.program_id(0), cos_ref.shape[1]

    @pl.when(step == 0)
    def _():
        gkey_ref[...] = jnp.zeros_like(gkey_ref)
        gvalue_ref[...] = jnp.zeros_like(gvalue_ref)

    lifted_all = product(out_ref[...], join(dy_refs), 1, 1).astype(bf16).astype(f32)

    def tile(at):
        held = own * (at + 1)
        for head in range(gkey_ref.shape[0]):
            spot = slice(head * HD, (head + 1) * HD)
            lifted = lifted_all[spot] * inv_ref[head : head + 1]
            delta = jnp.sum(lifted * heads_ref[spot, :].astype(f32), axis=0, keepdims=True)
            lifted_rows = lifted.T.astype(bf16)
            soft = soft_ref[head, :held]
            grad_soft = product(value_ref[head, :held], lifted.astype(bf16))
            grad_scores = (soft.astype(f32) * (grad_soft - delta)).astype(bf16)
            gvalue_ref[head, :held] += product(soft, lifted_rows)
            gkey_ref[head, :held] += product(grad_scores, query_ref[head])
            back = product(key_ref[spot, :held], grad_scores) * HD**-0.5
            gquery_ref[spot, :] = jnp.concatenate(turn(back, cos_ref[...], -sin_ref[...]), axis=0)

    for at in range(ranks):
        pl.when(step == at)(functools.partial(tile, at))

    @pl.when(step == ranks - 1)
    def _():
        low_key_ref[...] = gkey_ref[...].astype(bf16)
        low_value_ref[...] = gvalue_ref[...].astype(bf16)


def rear_kernel(spot_ref, *refs, ranks, parts):
    hat_ref, refs = refs[0], refs[1:]
    gquery_ref, gkey_ref, gvalue_ref, cos_ref, sin_ref, scaled_ref, vec_ref, attn_ref = refs[:8]
    mixed_ref, sums_ref, gbias_ref = refs[8:11]
    step = pl.program_id(0)

    @pl.when(step == 0)
    def _():
        sums_ref[...] = jnp.zeros_like(sums_ref)
        gbias_ref[...] = jnp.zeros_like(gbias_ref)

    cosine, sine = cos_ref[...], sin_ref[...]
    pieces = [gquery_ref[...]]
    for j in range(gkey_ref.shape[0]):
        pieces += turn(gkey_ref[j].astype(f32).T, cosine, -sine)
    pieces += [gvalue_ref[j].astype(f32).T for j in range(gvalue_ref.shape[0])]
    mixed = jnp.concatenate(pieces, axis=0).T
    gbias_ref[0:1] += jnp.sum(mixed, axis=0, keepdims=True)
    low = mixed.astype(bf16)
    mixed_ref[...] = low
    grad = product(low, attn_ref[:, : low.shape[1]], 1, 1)
    hat = hat_ref[...].astype(f32)
    total = (grad * vec_ref[0:1] + scaled_ref[...].astype(f32)).astype(bf16)
    store_blocks(refs[11:], spot_ref, step, total, parts)
    sums_ref[0:1] += jnp.sum(grad * hat, axis=0, keepdims=True)
    sums_ref[1:2] += jnp.sum(grad, axis=0, keepdims=True)


def weigh_kernel(
    spot_ref, n1_ref, mixed_ref, sums_ref, gbias_ref, feed_ref, grads_ref, small_ref, *, ranks, ratio
):
    acc = product(n1_ref[...], mixed_ref[...], 0, 0)
    width, part3 = acc.shape
    cols, owners = part3 // 3, small_ref.shape[0]
    share = width // owners
    feed = feed_ref[...]
    vectors = [sums_ref[0:1], sums_ref[1:2], feed[0:1], feed[1:2], feed[3:4], None]
    vectors += [gbias_ref[0:1], feed[2:3]]
    maps = vector_maps(spot_ref[0], share, ranks, cols, feed.shape[1], ratio)
    table = jnp.zeros((owners, LANES), f32)
    for vector, (per, base, index) in zip(vectors, maps):
        if vector is not None:
            rows, lanes = places(owners, per, base, index)
            table += product(jnp.where(rows, vector, 0.0).astype(bf16), lanes, 1, 1)
    small_ref[...] = jnp.zeros_like(small_ref)
    for j in range(LANES // 128):
        small_ref[:, j, :] = table[:, j * 128 : (j + 1) * 128]
    small = small_ref[...].reshape(width, 128)
    grads_ref[...] = jnp.concatenate([acc, small], axis=1).astype(bf16)


def finish_kernel(
    rank_ref, *refs, factor, hidden,
):
    qkv_ref, up_ref, proj_ref, down_ref, *small_refs = refs[-12:]
    down_in, proj_in, refs = refs[-14], refs[-13], refs[:-14]
    ranks, rank = len(refs), rank_ref[0]
    blocks = [ref[...].astype(f32) * factor for ref in refs]
    share, width = proj_ref.shape
    cols = width // ranks
    small = jnp.zeros((share, 128), f32)
    for t in range(ranks):
        picked = blocks[0]
        for r in range(1, ranks):
            picked = jnp.where((rank - r + ranks) % ranks == t, blocks[r], picked)
        for at in range(0, hidden, down_ref.shape[0]):
            where = at * ranks + t * down_ref.shape[0]
            up_ref[:, where : where + down_ref.shape[0]] = picked[:, at : at + down_ref.shape[0]]
        for j in range(3):
            at = j * width + t * cols
            qkv_ref[:, at : at + cols] = picked[:, hidden + j * cols : hidden + (j + 1) * cols]
        small += picked[:, hidden + 3 * cols :]
    down_ref[...] = down_in[...].astype(f32) * factor
    rows = proj_in[...].astype(f32) * factor
    proj_ref[...] = jnp.concatenate(
        [rows[j * share : (j + 1) * share] for j in range(ranks)], axis=1
    )
    line = jnp.concatenate([small[j : j + 1] for j in range(LANES // 128)], axis=1)
    at = 0
    for j, ref in enumerate(small_refs):
        at -= share if j == 5 else 0
        at += share if j == 6 else 0
        ref[...] = line[0, at : at + ref.shape[0]]
        at += ref.shape[0]


LANES = 384
VMEM = 56 * 1024 * 1024


SMEM = pl.BlockSpec(memory_space=pltpu.SMEM)


def call(kernel, grid, ins, outs, scratch=(), cost=1, first=()):
    arrays, in_specs = zip(*ins)
    shapes, out_specs = zip(*outs)
    return pl.pallas_call(
        kernel,
        grid_spec=pltpu.PrefetchScalarGridSpec(
            num_scalar_prefetch=len(first),
            grid=grid,
            in_specs=list(in_specs),
            out_specs=list(out_specs),
            scratch_shapes=list(scratch),
        ),
        out_shape=list(shapes),
        compiler_params=pltpu.CompilerParams(vmem_limit_bytes=VMEM),
        cost_estimate=pl.CostEstimate(flops=cost * 10**9, bytes_accessed=0, transcendentals=0),
    )(*first, *arrays)


def after(value, *others):
    return lax.optimization_barrier((value,) + others)[0]


def shift(block, amount, ranks):
    return lax.ppermute(block, "seq", [(k, (k + amount) % ranks) for k in range(ranks)])


def around(blocks, sign, ranks):
    order = sorted(range(1, ranks), key=lambda r: abs(ranks - 2 * r))
    got = {r: shift(blocks[r - 1], sign * r, ranks) for r in order if blocks[r - 1] is not None}
    return [got.get(r) for r in range(1, ranks)]


def swap(block, mask):
    return lax.ppermute(block, "dp", [(k, k ^ mask) for k in range(8)])


def gather_dp(piece):
    place = lax.axis_index("dp")
    by_x, by_y, by_both = swap(piece, 2), swap(piece, 4), swap(piece, 6)
    near, beside, across = swap(piece, 1), swap(jnp.stack([by_x, by_y]), 1), swap(by_both, 1)
    whole = jnp.zeros((8,) + piece.shape, piece.dtype)
    for mask, part in (
        (0, piece), (1, near), (2, by_x), (4, by_y), (6, by_both),
        (3, beside[0]), (5, beside[1]), (7, across),
    ):
        whole = lax.dynamic_update_slice(whole, part[None], (place ^ mask, 0, 0))
    return whole.reshape(8 * piece.shape[0], piece.shape[1])


def scatter_dp(parts):
    parts = lax.all_to_all(parts.reshape(8, -1, parts.shape[1]), "dp", 0, 0, tiled=True)
    return jnp.sum(parts.astype(f32), axis=0).astype(bf16)


def per_device_heads(
    hidden_in,
    stretch_order,
    doc_lengths,
    attn_gain,
    attn_shift,
    feed_gain,
    feed_shift,
    qkv_weight,
    qkv_bias,
    out_weight,
    out_bias,
    up_weight,
    up_bias,
    down_weight,
    down_bias,
    grad_out,
):
    ranks, groups = lax.axis_size("seq"), lax.axis_size("dp")
    rank = lax.axis_index("seq")
    blocks_own, half, width = hidden_in.shape[1:]
    own = blocks_own * half
    count = ranks * own
    share = qkv_weight.shape[0]
    piece = share * ranks
    cols = width // ranks
    heads = cols // HD
    hidden = up_weight.shape[1] // ranks
    ratio = up_weight.shape[1] // width
    mixed_cols = 3 * cols
    edge = hidden + width + mixed_cols

    x_own = hidden_in.reshape(own, width)
    dy_own = grad_out.reshape(own, width)

    small = [attn_gain, attn_shift, feed_gain, feed_shift, out_bias, down_bias, qkv_bias, up_bias]
    shape = jax.ShapeDtypeStruct
    blocks = stretch_order.shape[0]
    slots = jnp.arange(blocks, dtype=jnp.int32)
    lies = jnp.sum(jnp.where(stretch_order[None] == slots[:, None], slots[None], 0), axis=1)
    lies = (rank - lies // blocks_own) % ranks * blocks_own + lies % blocks_own
    spot = jnp.concatenate([jnp.stack([rank, lax.axis_index("dp")]), lies])
    sent = (share, hidden + mixed_cols + 128)
    *packed, out_piece = call(
        functools.partial(pack_kernel, vectors=len(small), held=ratio * share),
        (1,),
        [(spot, SMEM)]
        + [(a, whole_block(a.shape)) for a in (up_weight, qkv_weight, out_weight, *small)],
        [(shape(sent, bf16), whole_block(sent))] * ranks
        + [(shape((piece, cols), bf16), whole_block((piece, cols)))],
    )
    spread = ranks * groups
    out_piece = lax.ppermute(
        out_piece, ("dp", "seq"),
        [(k, (k % groups) * ranks + k // groups) for k in range(spread)],
    )
    landed = packed[:1] + around(packed[1:], 1, ranks)
    x_next = shift(x_own, 1, ranks)
    landed[0] = after(landed[0], x_next)
    total_cols = edge + cols + 128
    (weight_piece,) = call(
        functools.partial(land_kernel, hidden=hidden),
        (1,),
        [(spot, SMEM)] + [(a, whole_block(a.shape)) for a in (*landed, down_weight, out_piece)],
        [(shape((piece, total_cols), bf16), whole_block((piece, total_cols)))],
    )
    weights = gather_dp(weight_piece)

    x_go = after(x_own, *landed)
    x_rest = around([None] + [x_go] * (ranks - 2), 1, ranks)[1:]
    x_all = jnp.concatenate([x_own] + [after(block, weights) for block in (x_next, *x_rest)])
    dy_go = after(dy_own, x_all)
    dy_got = around([dy_go] * (ranks - 1), 1, ranks)

    ends = jnp.cumsum(doc_lengths[0])[:-1]
    place = jnp.arange(count, dtype=jnp.int32)
    first_of = jnp.max(jnp.where(place[:, None] >= ends[None], ends[None], 0), axis=1)
    start = jnp.broadcast_to(first_of[None], (8, count))
    angle = frequencies()[:, None] * place.astype(f32)[None]
    cosine, sine = jnp.cos(angle), jnp.sin(angle)

    tile = lambda w: pl.BlockSpec((own, w), lambda t, *_: (t, 0))
    upright_tile = lambda n: pl.BlockSpec((n, own), lambda t, *_: (0, t))
    upright_all = lambda j: pl.BlockSpec((cols, count), lambda *_: (j, 0))
    column = lambda j: pl.BlockSpec((width, width), lambda *_: (0, j))
    angles = [(cosine, upright_tile(ROT // 2)), (sine, upright_tile(ROT // 2))]
    by_place = [
        pl.BlockSpec((half, width), lambda t, spot, k=k: (spot[2 + t * blocks_own + k], 0))
        for k in range(blocks_own)
    ]
    in_order = lambda array: [(array, spec) for spec in by_place]
    each = [(shape((own, width), bf16), whole_block((own, width)))] * ranks

    hat, n1, n2, active, slope, fed, upright, rows, vec, out_own = call(
        functools.partial(front_kernel, ranks=ranks, ratio=ratio, parts=blocks_own),
        (ranks,),
        in_order(x_all)
        + [(weights, pl.BlockSpec((width, 128), lambda *_: (0, (edge + cols) // 128)))] + angles
        + [(weights, column(0)), (weights, column(1)), (weights, column(2))],
        [(shape((count, width), bf16), tile(width))] * 3
        + [(shape((count, hidden), bf16), tile(hidden)), (shape((count, hidden), bf16), tile(hidden)),
         (shape((count, width), f32), tile(width)),
         (shape((mixed_cols, count), bf16), upright_tile(mixed_cols)),
         (shape((3 * heads, count, HD), bf16),
          pl.BlockSpec((3 * heads, own, HD), lambda t, *_: (0, t, 0))),
         (shape((8, width), f32), whole_block((8, width))),
         (shape((cols, width), bf16), whole_block((cols, width)))],
        [pltpu.VMEM((1, mixed_cols), f32)],
        cost=10,
        first=(spot,),
    )

    all_heads = lambda j: pl.BlockSpec((heads, count, HD), lambda *_: (j, 0, 0))
    soft_spec = pl.BlockSpec((heads, count, own), lambda t, *_: (0, 0, t))
    soft, inverse, heads_low, *part_out = call(
        functools.partial(attend_kernel, ranks=ranks, parts=blocks_own),
        (ranks,),
        [(start, upright_tile(8)), (rows, all_heads(1)), (upright, upright_tile(cols)),
         (upright, upright_all(2)), (fed, tile(width)), (out_own, whole_block((cols, width)))],
        [(shape((heads, count, count), bf16), soft_spec), (shape((8, count), f32), upright_tile(8)),
         (shape((cols, count), bf16), upright_tile(cols))] + each,
        cost=10,
        first=(spot,),
    )

    dy_all = jnp.concatenate([dy_own] + [after(block, heads_low) for block in dy_got])
    scaled, grads_feed, feed_sums = call(
        functools.partial(feed_back_kernel, ranks=ranks, parts=blocks_own),
        (ranks,),
        in_order(dy_all)
        + [(hat, tile(width)), (dy_own, whole_block((own, width))), (active, tile(hidden)),
         (slope, tile(hidden)), (n2, tile(width)), (vec, whole_block((8, width))),
         (weights, column(0)), (weights, column(1)), (heads_low, upright_tile(cols))],
        [(shape((count, width), bf16), tile(width)),
         (shape((width, edge - mixed_cols + cols), bf16),
          whole_block((width, edge - mixed_cols + cols))),
         (shape((8, width), f32), whole_block((8, width)))],
        [pltpu.VMEM((width, hidden), f32), pltpu.VMEM((hidden, width), f32),
         pltpu.VMEM((cols, width), f32)],
        cost=12,
        first=(spot,),
    )
    feed_part = scatter_dp(grads_feed)

    far = [r for r in range(1, ranks) if 2 * r == ranks]
    near = [r for r in range(1, ranks) if r not in far]
    out_parts = part_out[:1] + [shift(part_out[r], -r, ranks) for r in near]
    heads_low = after(heads_low, scaled, *out_parts)
    far_parts = [shift(after(part_out[r], scaled), -r, ranks) for r in far]
    head_tile = pl.BlockSpec((heads, own, HD), lambda t, *_: (0, t, 0))
    gquery, gkey, gvalue = call(
        functools.partial(attend_back_kernel, ranks=ranks, parts=blocks_own),
        (ranks,),
        in_order(dy_all)
        + [(out_own, whole_block((cols, width))), (heads_low, upright_tile(cols)),
           (inverse, upright_tile(8)), (soft, soft_spec), (rows, all_heads(2)),
           (upright, upright_all(1)), (rows, head_tile)] + angles,
        [(shape((cols, count), f32), upright_tile(cols)),
         (shape((heads, count, HD), bf16), whole_block((heads, count, HD))),
         (shape((heads, count, HD), bf16), whole_block((heads, count, HD)))],
        [pltpu.VMEM((heads, count, HD), f32), pltpu.VMEM((heads, count, HD), f32)],
        cost=10,
        first=(spot,),
    )
    gquery = after(gquery, *far_parts)
    out_sum = sum(part.astype(f32) for part in out_parts + far_parts)
    hidden_out = (x_own.astype(f32) + vec[5:6] + out_sum).astype(bf16)

    mixed, attn_sums, attn_bias, *total = call(
        functools.partial(rear_kernel, ranks=ranks, parts=blocks_own),
        (ranks,),
        [(hat, tile(width)), (gquery, upright_tile(cols)), (gkey, head_tile), (gvalue, head_tile)]
        + angles
        + [(scaled, tile(width)), (vec, whole_block((8, width))), (weights, column(2))],
        [(shape((count, mixed_cols), bf16), tile(mixed_cols)),
         (shape((8, width), f32), whole_block((8, width))),
         (shape((8, mixed_cols), f32), whole_block((8, mixed_cols)))] + each,
        cost=8,
        first=(spot,),
    )
    (grads_attn,) = call(
        functools.partial(weigh_kernel, ranks=ranks, ratio=ratio),
        (1,),
        [(a, whole_block(a.shape)) for a in (n1, mixed, attn_sums, attn_bias, feed_sums)],
        [(shape((width, mixed_cols + 128), bf16), whole_block((width, mixed_cols + 128)))],
        [pltpu.VMEM((spread, share, 128), f32)],
        cost=5,
        first=(spot,),
    )

    grad_parts = total[:1] + around(total[1:], -1, ranks)
    attn_part = scatter_dp(after(grads_attn, feed_part))
    home = [((k % groups) * ranks + k // groups, k) for k in range(spread)]
    proj_part = lax.ppermute(feed_part[:, hidden + width :], ("dp", "seq"), home)
    parts = jnp.concatenate([feed_part[:, :hidden], attn_part], axis=1)
    parts = parts.reshape(ranks, share, parts.shape[1])
    parts = [lax.dynamic_index_in_dim(parts, (rank + r) % ranks, 0, False) for r in range(ranks)]
    parts = parts[:1] + around([after(p, proj_part, *grad_parts) for p in parts[1:]], 1, ranks)
    dy = dy_own.astype(f32)
    grad = sum(part.astype(f32) for part in grad_parts)
    rows_own = x_own.astype(f32)
    centred = rows_own - jnp.mean(rows_own, axis=-1, keepdims=True)
    rstd = lax.rsqrt(jnp.mean(centred * centred, axis=-1, keepdims=True) + eps)
    hat = centred * rstd
    grad_in = dy + rstd * (
        grad
        - jnp.mean(grad, axis=-1, keepdims=True)
        - hat * jnp.mean(grad * hat, axis=-1, keepdims=True)
    )

    factor = 1.0 / math.sqrt(count * groups)
    down_part = feed_part[:, hidden : hidden + width]
    results = [(share, 3 * width), (share, ranks * hidden), (share, width), (piece, width)]
    results += [(share,)] * 6 + [(3 * share,), (ratio * share,)]
    qkv_own, up_own, proj_own, down_own, *small_own = call(
        functools.partial(finish_kernel, factor=factor, hidden=hidden),
        (1,),
        [(spot, SMEM)] + [(a, whole_block(a.shape)) for a in (*parts, down_part, proj_part)],
        [(shape(size, f32), whole_block(size)) for size in results],
    )
    return (
        hidden_out.reshape(hidden_in.shape),
        grad_in.astype(bf16).reshape(hidden_in.shape),
        *small_own[:4],
        qkv_own,
        small_own[6],
        proj_own,
        small_own[4],
        up_own,
        small_own[7],
        down_own,
        small_own[5],
    )


def per_device(hidden_in, *rest):
    heads = hidden_in.shape[-1] // HD
    fits = heads % lax.axis_size("seq") == 0 and lax.axis_size("dp") == 8
    return (per_device_heads if fits else per_device_split)(hidden_in, *rest)


def solution(mesh):
    in_specs = (
        P("dp", "seq", None, None),
        P(),
        P("dp", None),
        P(("dp", "seq")),
        P(("dp", "seq")),
        P(("dp", "seq")),
        P(("dp", "seq")),
        P(("dp", "seq"), None),
        P(("dp", "seq")),
        P(("dp", "seq"), None),
        P(("dp", "seq")),
        P(("dp", "seq"), None),
        P(("dp", "seq")),
        P(("dp", "seq"), None),
        P(("dp", "seq")),
        P("dp", "seq", None, None),
    )
    out_specs = (
        P("dp", "seq", None, None),
        P("dp", "seq", None, None),
        P(("dp", "seq")),
        P(("dp", "seq")),
        P(("dp", "seq")),
        P(("dp", "seq")),
        P(("dp", "seq"), None),
        P(("dp", "seq")),
        P(("dp", "seq"), None),
        P(("dp", "seq")),
        P(("dp", "seq"), None),
        P(("dp", "seq")),
        P(("dp", "seq"), None),
        P(("dp", "seq")),
    )
    return jax.shard_map(
        per_device, mesh=mesh, in_specs=in_specs, out_specs=out_specs, check_vma=False
    )
```
